256 devices in a mesh: loop: 16 (over x_hi, z), column: 4 (over y), dp: 4 (over x_lo, core).
Axes of the slice: x: 4 (x_hi: 2, x_lo: 2; x = x_hi * 2 + x_lo), y: 4, z: 8, core: 2. Of those that a mesh axis runs over, the one named last changes fastest.
Arguments:
- tokens: bfloat16 [4096, 16384], P('dp', 'loop'), may hold values from -8 to 8
- doc_ids: int32 [4096], P('dp'), may hold values from 0 to 11, never falling along the last dimension, each value on 1 to 1536 neighbouring positions
- w_query: bfloat16 [16384, 8192], P('loop', 'column'), may hold values from -1.00581 to 1.00581
- key_weight: bfloat16 [16384, 512], P('loop', 'column'), may hold values from -0.0390625 to 0.0390625
- value_weight: bfloat16 [16384, 512], P('loop', 'column'), may hold values from -0.046875 to 0.046875
- w_out: bfloat16 [8192, 16384], P('column', 'loop'), may hold values from -0.09375 to 0.09375
Outputs:
- result: bfloat16 [4096, 16384], P('dp', ('loop', 'column'))
The draws below stay inside these ranges and needn't reach their ends.
Inputs may be any that keep to these rules, and one draw needn't show every extreme that they name: `doc_ids`: never falling along the tokens; each document spans 1 to 1536 tokens and one spans exactly that many.
All inputs are finite; a program needn't handle non-finite values.
Results may differ from the reference program's by a relative error of at most 0.0078.
Values may be sent and summed in bfloat16 or wider, within the bound.
A program may use at most 64 MiB of HBM per device.

```python
import math
import jax
import jax.numpy as jnp
import numpy as np

MODEL_WIDTH = 16384
QUERY_HEADS = 64
KEY_VALUE_HEADS = 4
HEAD_SIZE = 128
SEQUENCE_TOKENS = 1024
TOKENS = 4096
N_DP = 4


def shared_basis(key):
    return jnp.clip(jax.random.normal(jax.random.fold_in(key, 17), (MODEL_WIDTH, KEY_VALUE_HEADS, HEAD_SIZE), jnp.float32), -5.0, 5.0)


def single_order(group_random_key):
    return jax.random.permutation(group_random_key, QUERY_HEADS // KEY_VALUE_HEADS)


def head_strength(key):
    count_of_groups = QUERY_HEADS // KEY_VALUE_HEADS
    head_permutation = jax.vmap(single_order)(jax.random.split(key, KEY_VALUE_HEADS))
    head_signs = 1.0 - 2.0 * (head_permutation % 2).astype(jnp.float32)
    rank_steps = max(count_of_groups // 2 - 1, 1)
    levels = (head_permutation // 2).astype(jnp.float32) / rank_steps
    return head_signs * 200.0 * jnp.exp(-jnp.log(40.0) * levels)


def draw_key_weight(key, part):
    basis_vectors = shared_basis(key)
    return (basis_vectors * MODEL_WIDTH ** (-0.5)).reshape(MODEL_WIDTH, KEY_VALUE_HEADS * HEAD_SIZE).astype(jnp.bfloat16)


def draw_w_query(key, part):
    basis_vectors = shared_basis(key)
    key = jax.random.fold_in(key, 3)
    first_key, second_random_key = jax.random.split(key)
    count_of_groups = QUERY_HEADS // KEY_VALUE_HEADS
    strength = head_strength(first_key) * HEAD_SIZE ** (-0.5)
    random_noise = jnp.clip(jax.random.normal(second_random_key, (MODEL_WIDTH, KEY_VALUE_HEADS, count_of_groups, HEAD_SIZE), jnp.float32), -5.0, 5.0)
    own_scale = 0.6 * jnp.abs(strength) + 1.0
    weights = (0.8 * strength[None, :, :, None] * basis_vectors[:, :, None, :] + own_scale[None, :, :, None] * random_noise) * MODEL_WIDTH ** (-0.5)
    return weights.reshape(MODEL_WIDTH, QUERY_HEADS * HEAD_SIZE).astype(jnp.bfloat16)


def draw_tokens(key, part):
    key = jax.random.fold_in(key, 7)
    dir_key = jax.random.fold_in(key, 0)
    noise_key = jax.random.fold_in(key, 1)
    amount_key = jax.random.fold_in(key, 3)
    direction = jnp.clip(jax.random.normal(dir_key, (MODEL_WIDTH,), jnp.float32), -4.0, 4.0)
    random_noise = jnp.clip(jax.random.normal(noise_key, (TOKENS, MODEL_WIDTH), jnp.float32), -4.0, 4.0)
    amount = jax.random.uniform(amount_key, (TOKENS, 1), jnp.float32, 1.0, 2.0)
    return jnp.clip(0.6 * random_noise + 0.8 * amount * direction[None, :], -8.0, 8.0).astype(jnp.bfloat16)


def spiked(values, key, source, target, blocks, factor):
    def block_of(position):
        return (jnp.arange(values.shape[position]) // (values.shape[position] // blocks)).reshape((-1,) + (1,) * (values.ndim - 1 - position))

    near = jax.random.permutation(key, blocks)[block_of(target)]
    other_side = (block_of(target) + blocks // 2) % blocks
    return jnp.where((block_of(source) == near) | (block_of(source) == other_side), factor * values, values)


def shard_levels(stream_key, dims, cuts, smallest, high):
    def one(dim, shards_of):
        heights = jax.random.uniform(jax.random.fold_in(jax.random.fold_in(stream_key, 6), dim), (shards_of,), jnp.float32, smallest / len(cuts), high / len(cuts))
        return jnp.repeat(jnp.exp(heights), dims[dim] // shards_of).reshape((-1,) + (1,) * (len(dims) - dim - 1))

    factor_of = one(*cuts[0])
    for cut in cuts[1:]:
        factor_of = factor_of * one(*cut)
    return factor_of


def profile(count, total, bound, skew):
    loads = [(1 << 20) // math.isqrt(rank ** skew) + 1 for rank in range(2, count + 1)]
    surplus, given = total - bound - (count - 1), [1] * (count - 1)
    while surplus > 0:
        free = [i for i in range(count - 1) if given[i] < bound]
        mass, left = sum([loads[i] for i in free]), surplus
        for i in free:
            extra = min(bound - given[i], max(1, left * loads[i] // mass), surplus)
            given[i] = given[i] + extra
            surplus = surplus - extra
    return np.array([bound] + given)


def ragged_sizes(rng, count, total, bound, slope):
    if count == 2:
        one = jax.random.randint(rng, (), max(1, total - bound), min(bound, total - 1) + 1)
        return jnp.stack([one, total - one])
    sizes = jnp.asarray(profile(count, total, bound, slope), jnp.int32)
    twos = (count - 1) // 2
    donor, taker = sizes[1:1 + 2 * twos:2], sizes[2:2 + 2 * twos:2]
    margin = jnp.minimum(donor - 1, bound - taker)
    passed = jax.random.randint(jax.random.fold_in(rng, 1), (twos,), 0, 1 << 20) % (margin + 1)
    sizes = sizes.at[1:1 + 2 * twos:2].set(donor - passed).at[2:2 + 2 * twos:2].set(taker + passed)
    return sizes[jax.random.permutation(jax.random.fold_in(rng, 2), count)]


def centred(stream_key, extent, scale, reach, cuts=(), held_as=jnp.bfloat16):
    loudness = shard_levels(stream_key, extent, cuts, -0.22, 0.18) if cuts else 1.0
    result = jax.random.normal(stream_key, extent, jnp.float32) * scale * loudness
    return jnp.minimum(jnp.maximum(result, -reach), reach).astype(held_as)


def bell_draw_with(own_key, shape, width, limit, shards, heavy, kind=jnp.bfloat16):
    result = width * jax.random.normal(own_key, shape, jnp.float32)
    if shards:
        result = result * shard_levels(own_key, shape, shards, -0.22, 0.18)
    return jnp.clip(spiked(result, jax.random.fold_in(own_key, 3), *heavy), -limit, limit).astype(kind)


def setup_inputs(seed: int = 0) -> dict:
    key_of = jax.random.split(jax.random.key(seed), 7)
    tokens = draw_tokens(jax.random.fold_in(key_of[6], 71), 0)
    doc_ids = jnp.searchsorted(jnp.cumsum(ragged_sizes(key_of[1], 3 * N_DP, TOKENS, 3 * SEQUENCE_TOKENS // 2, 1)), jnp.arange(TOKENS), side="right").astype(jnp.int32)
    w_query = draw_w_query(jax.random.fold_in(key_of[6], 71), 0)
    key_weight = draw_key_weight(jax.random.fold_in(key_of[6], 71), 0)
    value_weight = centred(key_of[4], (MODEL_WIDTH, KEY_VALUE_HEADS * HEAD_SIZE), MODEL_WIDTH ** -0.5, 0.046875, ((0, 16), (1, 4)))
    w_out = bell_draw_with(key_of[5], (QUERY_HEADS * HEAD_SIZE, MODEL_WIDTH), (QUERY_HEADS * HEAD_SIZE) ** -0.5, 0.09375, ((0, 4), (1, 16)), (0, 1, 16, 2.0))
    return {"tokens": tokens, "doc_ids": doc_ids, "w_query": w_query, "key_weight": key_weight, "value_weight": value_weight, "w_out": w_out}


def rotate(vectors, positions):
    half_width = vectors.shape[-1] // 2
    frequency = jnp.exp(-jnp.log(500000.0) * jnp.arange(half_width, dtype=jnp.float32) * 2.0 / vectors.shape[-1])
    angles = positions.astype(jnp.float32)[:, None, None] * frequency
    cosine = jnp.cos(angles)
    sine_table = jnp.sin(angles)
    leading = vectors[..., :half_width]
    trailing = vectors[..., half_width:]
    return jnp.concatenate([leading * cosine - trailing * sine_table, trailing * cosine + leading * sine_table], -1)


def reference(tokens, doc_ids, w_query, key_weight, value_weight, w_out):
    every_row = tokens.shape[0]
    positions = jnp.arange(every_row, dtype=jnp.int32) % SEQUENCE_TOKENS
    raw_query = jnp.dot(tokens, w_query, preferred_element_type=jnp.float32).reshape(every_row, QUERY_HEADS, HEAD_SIZE)
    unprojected_key = jnp.dot(tokens, key_weight, preferred_element_type=jnp.float32).reshape(every_row, KEY_VALUE_HEADS, HEAD_SIZE)
    unprojected_value = jnp.dot(tokens, value_weight, preferred_element_type=jnp.float32).reshape(every_row, KEY_VALUE_HEADS, HEAD_SIZE)
    query_matrix = rotate(raw_query, positions).astype(jnp.bfloat16)
    key = rotate(unprojected_key, positions).astype(jnp.bfloat16)
    value = unprojected_value.astype(jnp.bfloat16)
    queries_per_group = QUERY_HEADS // KEY_VALUE_HEADS
    scale = 1.0 / (HEAD_SIZE ** 0.5)
    pieces = []
    for sequence in range(every_row // SEQUENCE_TOKENS):
        causal_window = slice(sequence * SEQUENCE_TOKENS, (sequence + 1) * SEQUENCE_TOKENS)
        query_sequence = query_matrix[causal_window].reshape(SEQUENCE_TOKENS, KEY_VALUE_HEADS, queries_per_group, HEAD_SIZE).astype(jnp.float32)
        key_seq = key[causal_window].astype(jnp.float32)
        value_seq = value[causal_window].astype(jnp.float32)
        documents = doc_ids[causal_window]
        order = jnp.arange(SEQUENCE_TOKENS, dtype=jnp.int32)
        allowed = (documents[:, None] == documents[None, :]) & (order[None, :] <= order[:, None])
        scores = jnp.einsum('qkgd,pkd->kgqp', query_sequence, key_seq) * scale
        masked = jnp.where(allowed, scores, -1e30)
        largest = jnp.max(masked, axis=-1, keepdims=True)
        weights = jnp.where(allowed, jnp.exp(masked - largest), 0.0)
        denominator = jnp.sum(weights, axis=-1)
        summed = jnp.einsum('kgqp,pkd->kgqd', weights, value_seq) / denominator[..., None]
        attended = jnp.transpose(summed, (2, 0, 1, 3)).reshape(SEQUENCE_TOKENS, QUERY_HEADS * HEAD_SIZE).astype(jnp.bfloat16)
        pieces.append(attended)
    attended_all = jnp.concatenate(pieces, 0)
    return jnp.dot(attended_all, w_out, preferred_element_type=jnp.float32).astype(jnp.bfloat16)
```

```python
import functools
import math

import jax
import jax.numpy as jnp
import numpy as np
from jax import lax
from jax.experimental import pallas as pl
from jax.experimental.pallas import tpu as pltpu
from jax.sharding import PartitionSpec as P

HEAD = 128
SEQ = 1024
MODEL = 1024
QCOLS = 2048
OCOLS = 1024
NZ = 8
NY = 4
CHUNKS = 2
ROWS = SEQ // CHUNKS
R = ROWS // (2 * NZ)
XFIRST = ((0, 640), (640, 640))
ZFIRST = ((1280, 384), (1664, 384))
BF = jnp.bfloat16
F32 = jnp.float32
SCALE = math.log2(math.e) / math.sqrt(HEAD)
ORDER = (
    0, 13, 21, 9, 5, 18, 1, 148, 45, 152, 4, 82, 79, 14, 75, 10, 3, 19, 22, 60, 46, 149, 76, 81, 2, 53, 59, 153,
    80, 11, 78, 64, 6, 157, 41, 7, 160, 77, 63, 61, 23, 15, 65, 83, 12, 150, 54, 50, 42, 24, 86, 16, 62, 158, 161,
    91, 66, 67, 55, 8, 47, 20, 43, 182, 17, 87, 189, 151, 71, 183, 68, 187, 56, 27, 30, 159, 162, 25, 51, 154, 167,
    188, 184, 166, 84, 44, 31, 26, 69, 88, 28, 72, 186, 185, 193, 32, 85, 169, 34, 170, 163, 173, 171, 70, 38, 155,
    168, 48, 190, 73, 33, 29, 172, 52, 177, 194, 89, 174, 35, 39, 74, 191, 94, 178, 57, 175, 195, 36, 90, 114, 95,
    127, 110, 49, 124, 92, 198, 179, 58, 196, 192, 40, 37, 164, 93, 111, 115, 125, 128, 134, 180, 100, 117, 96,
    121, 165, 106, 176, 156, 200, 103, 116, 131, 197, 202, 199, 122, 231, 234, 129, 112, 181, 201, 97, 220, 101,
    135, 217, 232, 104, 107, 210, 126, 113, 118, 132, 140, 203, 238, 235, 221, 123, 245, 218, 241, 207, 102, 227,
    119, 233, 224, 213, 142, 108, 222, 130, 136, 236, 138, 246, 208, 105, 228, 98, 133, 219, 214, 239, 247, 242,
    240, 204, 211, 223, 225, 137, 109, 99, 144, 141, 237, 120, 215, 209, 205, 243, 226, 212, 143, 229, 249, 146,
    230, 248, 216, 206, 244, 251, 253, 250, 147, 145, 252, 139, 254,
)


def narrow(value):
    return value.astype(BF)


def widen(value):
    return value.astype(F32)


def narrow_pair(value):
    key = value[..., 0:HEAD]
    high = key.astype(BF)
    low = (key - high.astype(F32)).astype(BF)
    return jnp.concatenate([high, low, value[..., HEAD : 2 * HEAD].astype(BF)], -1)


def widen_pair(value):
    value = value.astype(F32)
    key = value[..., 0:HEAD] + value[..., HEAD : 2 * HEAD]
    return jnp.concatenate([key, value[..., 2 * HEAD : 3 * HEAD]], -1)


class Node:
    def __init__(self, name, rank, cost, after, waits, sends, emit):
        self.name, self.rank, self.cost = name, rank, cost
        self.after, self.waits, self.sends, self.emit = after, waits, sends, emit


def rotary_table():
    frequency = np.exp(-np.log(500000.0) * np.arange(HEAD // 2, dtype=np.float64) * 2.0 / HEAD)
    angles = np.arange(SEQ, dtype=np.float64)[:, None] * frequency
    cosine, sine = np.cos(angles), np.sin(angles)
    table = np.concatenate([cosine, cosine, -sine, sine], 1).astype(np.float32)
    return table.reshape(CHUNKS, 2 * NZ, R, 2 * HEAD)


def split(parity):
    return (4, 3) if parity == 0 else (3, 4)


def build(k):
    nodes = []

    def add(name, rank, cost, after, waits, sends, emit):
        nodes.append(Node(name, rank, cost, after, waits, sends, emit))

    def zlink(sign):
        return ["z+"] if sign > 0 else ["z-"]

    def emit_kv():
        k.load("wkv")
        for t in range(CHUNKS):
            k.load("tok%d" % t)
            res = jnp.dot(k.tok[pl.ds(t * ROWS, ROWS)], k.wkv[...], preferred_element_type=F32)
            k.pkv[t] = res.reshape(NZ, 2, R, 2 * HEAD)
        k.ready()

    add("kvmm", 0, 3.0, [], [], [], emit_kv)

    def emit_q(t, c0, width):
        k.load("tok%d" % t)
        for c in range(c0 // 512, (c0 + width - 1) // 512 + 1):
            k.load("wq%d" % c)
        res = jnp.dot(k.tok[pl.ds(t * ROWS, ROWS)], k.wq[:, c0 : c0 + width], preferred_element_type=F32)
        k.pq[t, :, :, :, c0 : c0 + width] = res.reshape(NZ, 2, R, width)

    for t in range(CHUNKS):
        for c0, width in ZFIRST + XFIRST:
            add(
                "q%d_%d" % (t, c0),
                1 + t * 40 + (0.1 if c0 < ZFIRST[0][0] else 0),
                width / 600.0,
                ["kvmm"],
                [],
                [],
                functools.partial(emit_q, t, c0, width),
            )

    def ring(tag, rank, stride, cost, size, counts, own, start_after, step_waits, down=narrow, up=widen):
        for sign, n in ((1, counts[0]), (-1, counts[1])):
            base = 0 if sign > 0 else counts[0]
            for s in range(n):
                name = (tag, sign, s)

                def emit(sign=sign, n=n, s=s, base=base, name=name):
                    d = k.zi(sign * (n - s))
                    value = own(sign, s, d)
                    if s > 0:
                        value = value + up(k.buf[tag, "r"][base + s - 1])
                    k.buf[tag, "s"][base + s] = down(value)
                    k.send(name, k.buf[tag, "s"].at[base + s], k.buf[tag, "r"].at[base + s], k.dev_z(sign))

                waits = list(step_waits(sign, s))
                after = list(start_after)
                if s > 0:
                    waits.append((tag, sign, s - 1))
                    after.append((tag, sign, s - 1))
                add(name, rank + stride * s, cost, after, waits, [(name, zlink(sign), size)], emit)
        return [(tag, 1, counts[0] - 1), (tag, -1, counts[1] - 1)]

    def ring_sum(tag, counts, pick, up=widen):
        bufs = k.buf[tag, "r"]
        return up(pick(bufs, counts[0] - 1)) + up(pick(bufs, NZ - 2))

    for t in range(CHUNKS):
        tag, counts, base = "kv%d" % t, split(t), 20 * t
        last = ring(
            tag,
            base + 2,
            4,
            0.15,
            2 * R * 768,
            counts,
            lambda sign, s, d, t=t: k.pkv[t, d],
            ["kvmm"],
            lambda sign, s: [],
            narrow_pair,
            widen_pair,
        )

        def emit_kv_fin(t=t, tag=tag, counts=counts):
            o = 1 - k.xh
            value = k.pkv[t, k.z, o] + ring_sum(tag, counts, lambda b, i: b[i, o], widen_pair)
            k.buf[tag + "x", "s"][...] = narrow_pair(value)
            k.send(tag + "x", k.buf[tag + "x", "s"], k.buf[tag + "x", "r"], k.dev_x())

        add(tag + "fin", base + 2, 0.12, last, last, [(tag + "x", ["x"], R * 768)], emit_kv_fin)

        def emit_kv_own(t=t, tag=tag, counts=counts):
            k.load("tab")
            value = k.pkv[t, k.z, k.xh] + ring_sum(tag, counts, lambda b, i: b[i, k.xh], widen_pair)
            value = value + widen_pair(k.buf[tag + "x", "r"][...])
            k.kvf[t, k.z, k.xh, :, 0:HEAD] = k.rotate(value[:, 0:HEAD], t).astype(BF)
            k.kvf[t, k.z, k.xh, :, HEAD : 2 * HEAD] = value[:, HEAD : 2 * HEAD].astype(BF)
            here = k.kvf.at[t, k.z, k.xh]
            k.send("kgx%d" % t, here, here, k.dev_x())

        add(tag + "own", base + 2, 0.2, [tag + "fin"], [tag + "x"], [("kgx%d" % t, ["x"], R * 512)], emit_kv_own)

    def gather(tag, rank, stride, size, counts, block, start_after, start_waits):
        for sign, n in ((1, counts[0]), (-1, counts[1])):
            for s in range(n):
                name = (tag, sign, s)

                def emit(sign=sign, s=s, name=name):
                    here = block(k.zi(-sign * s))
                    k.send(name, here, here, k.dev_z(sign))

                after = list(start_after) if s == 0 else [(tag, sign, s - 1)]
                waits = list(start_waits) if s == 0 else [(tag, sign, s - 1)]
                add(name, rank + stride * s, 0.05, after, waits, [(name, zlink(sign), size)], emit)
        return [(tag, 1, counts[0] - 1), (tag, -1, counts[1] - 1)]

    kg_last = [
        gather(
            "kg%d" % t,
            20 * t + 2,
            1,
            2 * R * 512,
            split(1 - t),
            lambda d, t=t: k.kvf.at[t, d],
            ["kv%down" % t],
            ["kgx%d" % t],
        )
        for t in range(CHUNKS)
    ]

    for t in range(CHUNKS):
        base = 40 * t
        own_nodes = {}
        for j, (c0, width) in enumerate(ZFIRST):
            tag, counts = "zf%d_%d" % (t, c0), split(j)
            last = ring(
                tag,
                base + 3 + 0.2 * j,
                8,
                0.15,
                2 * R * width * 2,
                counts,
                lambda sign, s, d, c0=c0, width=width, t=t: k.pq[t, d, :, :, c0 : c0 + width],
                ["q%d_%d" % (t, c0)],
                lambda sign, s: [],
            )

            def emit_fin(t=t, tag=tag, c0=c0, width=width, counts=counts):
                o = 1 - k.xh
                value = k.pq[t, k.z, o, :, c0 : c0 + width] + ring_sum(tag, counts, lambda b, i: b[i, o])
                k.buf[tag + "x", "s"][...] = value.astype(BF)
                k.send(tag + "x", k.buf[tag + "x", "s"], k.buf[tag + "x", "r"], k.dev_x())

            add(tag + "fin", base + 36, 0.1, last, last, [(tag + "x", ["x"], R * width * 2)], emit_fin)

            def emit_own(t=t, tag=tag, c0=c0, width=width, counts=counts):
                k.load("tab")
                value = k.pq[t, k.z, k.xh, :, c0 : c0 + width] + ring_sum(tag, counts, lambda b, i: b[i, k.xh])
                k.store_query(t, c0, value + k.buf[tag + "x", "r"][...].astype(F32))

            add(tag + "own", base + 37, 0.15, [tag + "fin"], [tag + "x"], [], emit_own)
            own_nodes[c0] = tag + "own"

        for j, (c0, width) in enumerate(XFIRST):
            tag, counts = "xf%d_%d" % (t, c0), split(j + t)
            slots = [(1, s) for s in range(counts[0])] + [(-1, s) for s in range(counts[1])] + [(0, 0)]
            queue = sorted(range(NZ), key=lambda i, slots=slots: (slots[i][1] if slots[i][0] else 9, i))

            def where(i, counts=counts, slots=slots):
                sign, s = slots[i]
                n = counts[0] if sign > 0 else counts[1]
                return k.zi(sign * (n - s)) if sign else k.z

            for place, i in enumerate(queue):

                def emit_x(t=t, tag=tag, i=i, c0=c0, width=width, where=where):
                    k.buf[tag + "x", "s"][i] = k.pq[t, where(i), 1 - k.xh, :, c0 : c0 + width].astype(BF)
                    k.send((tag, "x", i), k.buf[tag + "x", "s"].at[i], k.buf[tag + "x", "r"].at[i], k.dev_x())

                add(
                    (tag, "x", i),
                    base + 4 + 0.1 * place - (8 if t else 0),
                    0.06,
                    ["q%d_%d" % (t, c0)],
                    [],
                    [((tag, "x", i), ["x"], R * width * 2)],
                    emit_x,
                )

            def own_xf(sign, s, d, t=t, tag=tag, c0=c0, width=width, counts=counts):
                i = s if sign > 0 else counts[0] + s
                return k.pq[t, d, k.xh, :, c0 : c0 + width] + k.buf[tag + "x", "r"][i].astype(F32)

            last = ring(
                tag,
                base + 9,
                8,
                0.15,
                R * width * 2,
                counts,
                own_xf,
                [(tag, "x", i) for i in range(NZ)],
                lambda sign, s, tag=tag, counts=counts: [(tag, "x", s if sign > 0 else counts[0] + s)],
            )

            def emit_xf_own(t=t, tag=tag, c0=c0, width=width, counts=counts):
                k.load("tab")
                value = k.pq[t, k.z, k.xh, :, c0 : c0 + width] + k.buf[tag + "x", "r"][NZ - 1].astype(F32)
                k.store_query(t, c0, value + ring_sum(tag, counts, lambda b, i: b[i]))

            add(tag + "own", base + 37.5, 0.15, last, last + [(tag, "x", NZ - 1)], [], emit_xf_own)
            own_nodes[c0] = tag + "own"

        add("mask%d" % t, base + 20, 0.3, ["kvmm"], [], [], functools.partial(lambda t: k.mask(t), t))
        keys_in = [m for u in range(t + 1) for m in ["kgx%d" % u] + kg_last[u]]
        keys_after = [m for u in range(t + 1) for m in ["kv%down" % u] + kg_last[u]]
        for place, (c0, width) in enumerate(ZFIRST + XFIRST):
            gtag = "g%d_%d" % (t, c0)

            def emit_att(t=t, gtag=gtag, c0=c0, width=width):
                k.attend(t, c0 // HEAD, width // HEAD)
                here = k.att.at[t, k.z, k.xh, :, c0 : c0 + width]
                k.send((gtag, "x", 0), here, here, k.dev_x())

            add(
                gtag + "att",
                base + 40 + place,
                width / 1000.0 + 0.05,
                [own_nodes[c0], "mask%d" % t] + keys_after,
                keys_in,
                [((gtag, "x", 0), ["x"], R * width * 2)],
                emit_att,
            )
        last_step = []
        for j, (c0, width) in enumerate(ZFIRST):
            gtag = "g%d_%d" % (t, c0)
            gather(
                gtag,
                base + 44 + 0.1 * j,
                4,
                2 * R * width * 2,
                split(j),
                lambda d, t=t, c0=c0, width=width: k.att.at[t, d, :, :, c0 : c0 + width],
                [gtag + "att"],
                [(gtag, "x", 0)],
            )
            last_step.append((gtag, False, split(j)))
        for j, (c0, width) in enumerate(XFIRST):
            gtag, counts = "g%d_%d" % (t, c0), split(j + t)
            gather(
                gtag,
                base + 43,
                4,
                R * width * 2,
                counts,
                lambda d, t=t, c0=c0, width=width: k.att.at[t, d, k.xh, :, c0 : c0 + width],
                [gtag + "att"],
                [],
            )
            last_step.append((gtag, True, counts))
            for sign, n in ((1, counts[0]), (-1, counts[1])):
                for s in range(n):
                    name = (gtag, "x", sign, s)

                    def emit_pass(t=t, sign=sign, s=s, name=name, c0=c0, width=width):
                        here = k.att.at[t, k.zi(-sign * (s + 1)), k.xh, :, c0 : c0 + width]
                        k.send(name, here, here, k.dev_x())

                    after = [(gtag, sign, s + 1)] if s + 1 < n else [(gtag, sign, s)]
                    add(
                        name,
                        base + 43.5 + 4 * s,
                        0.05,
                        after,
                        [(gtag, sign, s)],
                        [(name, ["x"], R * width * 2)],
                        emit_pass,
                    )
        for r in range(5):
            shifts = [0] if r == 0 else [4] if r == 4 else [-r, r]
            first = 0 if r == 0 else 2 * r - 1
            waits, after = [], []
            for gtag, passes, counts in last_step:
                if r == 0:
                    waits.append((gtag, "x", 0))
                    after.append(gtag + "att")
                for sign, n in ((1, counts[0]), (-1, counts[1])):
                    if 0 < r <= n:
                        waits.append((gtag, sign, r - 1))
                        after.append((gtag, sign, r - 1))
                        if passes:
                            waits.append((gtag, "x", sign, r - 1))
                            after.append((gtag, "x", sign, r - 1))

            def emit_out(t=t, r=r, shifts=shifts, first=first):
                k.load("wout")
                count = len(shifts)
                rows = [k.att[t, k.zi(s)].reshape(2 * R, QCOLS) for s in shifts]
                lhs = rows[0] if count == 1 else jnp.concatenate(rows, 0)
                for delta in (2, 1, 3, 0):
                    c0 = pl.multiple_of(lax.rem(k.y + delta, NY) * 256, 256)
                    res = jnp.dot(lhs, k.wout[:, pl.ds(c0, 256)], preferred_element_type=F32)
                    res = res.reshape(count, 2 * R, 256)
                    if delta == 0:
                        k.oown[t, first : first + count] = res
                    else:
                        k.ys[t, delta - 1, first : first + count] = res.astype(BF)
                        k.send(
                            ("y", t, r, delta),
                            k.ys.at[t, delta - 1, first : first + count],
                            k.yr.at[t, delta - 1, first : first + count],
                            k.dev_y(delta),
                        )

            size = len(shifts) * 2 * R * 512
            add(
                ("out", t, r),
                base + 45 + 4 * r,
                1.4,
                after,
                waits,
                [(("y", t, r, 2), ["y+", "y-"], size), (("y", t, r, 1), ["y+"], size), (("y", t, r, 3), ["y-"], size)],
                emit_out,
            )

            def emit_fin(t=t, shifts=shifts, first=first):
                for i, shift in enumerate(shifts):
                    total = k.oown[t, first + i]
                    for delta in range(NY - 1):
                        total = total + k.yr[t, delta, first + i].astype(F32)
                    row = pl.multiple_of(t * ROWS + k.zi(shift) * 2 * R, 2 * R)
                    k.out[pl.ds(row, 2 * R), :] = total.astype(BF)

            add(
                ("fin", t, r),
                base + 50 + 4 * r,
                0.15,
                [("out", t, r)],
                [("y", t, r, delta) for delta in (1, 2, 3)],
                [],
                emit_fin,
            )
    return nodes


def buffers():
    shapes = {}
    for t in range(CHUNKS):
        shapes["kv%d" % t] = (7, 2, R, 384)
        shapes["kv%dx" % t] = (R, 384)
        for c0, width in ZFIRST:
            shapes["zf%d_%d" % (t, c0)] = (7, 2, R, width)
            shapes["zf%d_%dx" % (t, c0)] = (R, width)
        for c0, width in XFIRST:
            shapes["xf%d_%d" % (t, c0)] = (7, R, width)
            shapes["xf%d_%dx" % (t, c0)] = (8, R, width)
    return shapes


class Kernel:
    pass


def kernel(order_names, messages, *refs):
    shapes = buffers()
    names = ["docs", "h_tok", "h_wq", "h_wk", "h_wv", "h_wout", "h_tab", "out"]
    names += ["tok", "wq", "wkv", "wout", "tab", "bias", "pq", "pkv", "kvf", "qs", "att", "oown", "ys", "yr"]
    k = Kernel()
    for name, ref in zip(names, refs):
        setattr(k, name, ref)
    rest = refs[len(names) :]
    k.buf = {}
    for i, name in enumerate(shapes):
        k.buf[name, "s"], k.buf[name, "r"] = rest[2 * i], rest[2 * i + 1]
    send_sem, recv_sem, load_sem = rest[2 * len(shapes) :]

    loop, k.y = lax.axis_index("loop"), lax.axis_index("column")
    k.xh, k.z = loop // NZ, lax.rem(loop, NZ)
    k.zi = lambda delta: lax.rem(k.z + (delta + NZ), NZ) if delta else k.z
    k.dev_z = lambda sign: {"loop": k.xh * NZ + k.zi(sign)}
    k.dev_x = lambda: {"loop": (1 - k.xh) * NZ + k.z}
    k.dev_y = lambda delta: {"column": lax.rem(k.y + delta, NY)}
    mesh_id = pl.DeviceIdType.MESH

    barrier = pltpu.get_barrier_semaphore()
    peers = [k.dev_z(1), k.dev_z(-1), k.dev_x()] + [k.dev_y(delta) for delta in (1, 2, 3)]
    for peer in peers:
        pl.semaphore_signal(barrier, inc=1, device_id=peer, device_id_type=mesh_id)

    loads = {}

    def start_load(name, src, dst):
        loads[name] = [pltpu.make_async_copy(src, dst, load_sem.at[len(started)])]
        started.append(name)
        loads[name][0].start()

    started = []
    start_load("wk", k.h_wk, k.wkv.at[:, 0:HEAD])
    start_load("wv", k.h_wv, k.wkv.at[:, HEAD : 2 * HEAD])
    for t in range(CHUNKS):
        start_load("tok%d" % t, k.h_tok.at[pl.ds(t * ROWS, ROWS)], k.tok.at[pl.ds(t * ROWS, ROWS)])
    for c in (2, 3, 0, 1):
        cols = slice(c * 512, (c + 1) * 512)
        start_load("wq%d" % c, k.h_wq.at[:, cols], k.wq.at[:, cols])
    start_load("tab", k.h_tab.at[:, k.z * 2 + k.xh], k.tab)
    start_load("wout", k.h_wout, k.wout)

    def load(name):
        if name == "wkv":
            load("wk")
            load("wv")
        elif name in loads:
            loads.pop(name)[0].wait()

    k.load = load
    k.ready = lambda: pl.semaphore_wait(barrier, len(peers))
    sent, waited = {}, set()

    def send(name, src, dst, device):
        i = messages.index(name)
        sent[name] = pltpu.make_async_remote_copy(
            src_ref=src,
            dst_ref=dst,
            send_sem=send_sem.at[i],
            recv_sem=recv_sem.at[i],
            device_id=device,
            device_id_type=mesh_id,
        )
        sent[name].start()

    k.send = send

    def rotate(value, t):
        return value * k.tab[t, :, 0:HEAD] + pltpu.roll(value, HEAD // 2, 1) * k.tab[t, :, HEAD : 2 * HEAD]

    k.rotate = rotate

    def store_query(t, c0, value):
        for i in range(value.shape[1] // HEAD):
            k.qs[t, c0 // HEAD + i] = rotate(value[:, i * HEAD : (i + 1) * HEAD], t).astype(BF)

    k.store_query = store_query

    def mask(t):
        keys = (t + 1) * ROWS
        row = t * ROWS + (k.z * 2 + k.xh) * R + lax.broadcasted_iota(jnp.int32, (R, keys), 0)
        col = lax.broadcasted_iota(jnp.int32, (R, keys), 1)
        docs = jnp.broadcast_to(k.docs[0:1, 0:keys].astype(F32), (R, keys))
        mine = jnp.sum(jnp.where(row == col, docs, 0.0), axis=1, keepdims=True)
        allowed = (docs == mine) & (col <= row)
        k.bias[t, :, 0:keys] = jnp.where(allowed, 0.0, -1e30)

    k.mask = mask

    def attend(t, first, count):
        keys = (t + 1) * ROWS
        query = k.qs[t, first : first + count].reshape(count * R, HEAD)
        key = k.kvf[0 : t + 1, :, :, :, 0:HEAD].reshape(keys, HEAD)
        value = k.kvf[0 : t + 1, :, :, :, HEAD : 2 * HEAD].reshape(keys, HEAD)
        scores = lax.dot_general(query, key, (((1,), (1,)), ((), ())), preferred_element_type=F32)
        scores = (scores * SCALE).reshape(count, R, keys) + k.bias[t, :, 0:keys][None]
        top = jnp.max(scores, axis=-1, keepdims=True)
        weights = jnp.exp2(scores - top)
        total = jnp.sum(weights, axis=-1, keepdims=True)
        mixed = jnp.dot(weights.reshape(count * R, keys).astype(BF), value, preferred_element_type=F32)
        mixed = (mixed.reshape(count, R, HEAD) / total).astype(BF)
        for i in range(count):
            c0 = (first + i) * HEAD
            k.att[t, k.z, k.xh, :, c0 : c0 + HEAD] = mixed[i]

    k.attend = attend

    nodes = {node.name: node for node in build(k)}
    for name in order_names:
        node = nodes[name]
        for message in node.waits:
            if message not in waited:
                waited.add(message)
                sent[message].wait_recv()
        node.emit()
    for name in messages:
        if name not in waited:
            sent[name].wait_recv()
        sent[name].wait_send()
    for name in list(loads):
        load(name)


def shards(tokens, doc_ids, w_query, key_weight, value_weight, w_out):
    nodes = build(None)
    order = [nodes[i] for i in ORDER]
    messages = [send[0] for node in order for send in node.sends]
    scratch = [
        pltpu.VMEM((SEQ, MODEL), BF),
        pltpu.VMEM((MODEL, QCOLS), BF),
        pltpu.VMEM((MODEL, 2 * HEAD), BF),
        pltpu.VMEM((QCOLS, OCOLS), BF),
        pltpu.VMEM((CHUNKS, R, 2 * HEAD), F32),
        pltpu.VMEM((CHUNKS, R, SEQ), F32),
        pltpu.VMEM((CHUNKS, NZ, 2, R, QCOLS), F32),
        pltpu.VMEM((CHUNKS, NZ, 2, R, 2 * HEAD), F32),
        pltpu.VMEM((CHUNKS, NZ, 2, R, 2 * HEAD), BF),
        pltpu.VMEM((CHUNKS, QCOLS // HEAD, R, HEAD), BF),
        pltpu.VMEM((CHUNKS, NZ, 2, R, QCOLS), BF),
        pltpu.VMEM((CHUNKS, NZ, 2 * R, 256), F32),
        pltpu.VMEM((CHUNKS, NY - 1, NZ, 2 * R, 256), BF),
        pltpu.VMEM((CHUNKS, NY - 1, NZ, 2 * R, 256), BF),
    ]
    for shape in buffers().values():
        scratch += [pltpu.VMEM(shape, BF), pltpu.VMEM(shape, BF)]
    scratch += [
        pltpu.SemaphoreType.DMA((len(messages),)),
        pltpu.SemaphoreType.DMA((len(messages),)),
        pltpu.SemaphoreType.DMA((16,)),
    ]
    anywhere = pl.BlockSpec(memory_space=pl.ANY)
    vmem = pl.BlockSpec(memory_space=pltpu.VMEM)
    return pl.pallas_call(
        functools.partial(kernel, [node.name for node in order], messages),
        out_shape=jax.ShapeDtypeStruct((SEQ, 256), BF),
        in_specs=[vmem] + [anywhere] * 6,
        out_specs=vmem,
        scratch_shapes=scratch,
        compiler_params=pltpu.CompilerParams(
            collective_id=0, has_side_effects=True, vmem_limit_bytes=56 * 1024 * 1024
        ),
        name="sublayer",
    )(doc_ids.reshape(1, SEQ), tokens, w_query, key_weight, value_weight, w_out, jnp.asarray(rotary_table()))


def solution(mesh):
    placed = (
        P("dp", "loop"),
        P("dp"),
        P("loop", "column"),
        P("loop", "column"),
        P("loop", "column"),
        P("column", "loop"),
    )
    return jax.shard_map(
        shards, mesh=mesh, in_specs=placed, out_specs=P("dp", ("loop", "column")), check_vma=False
    )
```

```python
import functools
import math

import jax
import jax.numpy as jnp
import numpy as np
from jax import lax
from jax.experimental import pallas as pl
from jax.experimental.pallas import tpu as pltpu
from jax.sharding import PartitionSpec as P

HEAD = 128
SEQ = 1024
MODEL = 1024
QCOLS = 2048
OCOLS = 1024
NZ = 8
NY = 4
CHUNKS = 2
ROWS = SEQ // CHUNKS
R = ROWS // (2 * NZ)
XFIRST = ((0, 768), (768, 640))
ZFIRST = ((1408, 640),)
QUERY_PARTS = (2, 3, 0, 1)
XWIDTH = sum(width for _, width in XFIRST)
OUTS = (((0,), (1,), (2,), (3,), (4,)), ((0,), (1,), (2,), (3,), (4,)))
BF = jnp.bfloat16
F32 = jnp.float32
SCALE = math.log2(math.e) / math.sqrt(HEAD)
ORDER = (
    0, 11, 7, 3, 64, 16, 70, 19, 1, 39, 67, 43, 12, 8, 69, 68, 66, 65, 17, 2, 53, 4, 20, 40, 133, 54, 9, 71, 21,
    49, 48, 13, 129, 51, 80, 44, 10, 72, 18, 75, 41, 22, 5, 14, 50, 170, 139, 52, 55, 60, 56, 134, 6, 155, 45, 23,
    42, 130, 15, 144, 28, 158, 138, 61, 154, 25, 57, 73, 143, 76, 29, 62, 46, 157, 141, 156, 161, 24, 160, 159, 26,
    58, 165, 32, 36, 131, 140, 74, 142, 145, 30, 77, 135, 37, 59, 27, 149, 47, 33, 146, 166, 31, 132, 78, 63, 162,
    34, 150, 82, 95, 91, 79, 167, 163, 136, 151, 147, 83, 38, 81, 35, 164, 168, 96, 102, 152, 108, 148, 105, 92,
    137, 98, 171, 169, 173, 198, 84, 153, 172, 184, 106, 181, 109, 112, 97, 115, 195, 103, 119, 199, 93, 185, 174,
    191, 107, 88, 110, 104, 182, 99, 178, 209, 113, 200, 205, 186, 120, 188, 196, 85, 89, 175, 202, 111, 94, 117,
    116, 179, 114, 206, 100, 192, 201, 183, 187, 197, 203, 121, 86, 90, 176, 189, 207, 211, 180, 193, 204, 190,
    123, 194, 101, 208, 118, 87, 125, 177, 213, 215, 217, 127, 212, 126, 122, 214, 210, 218, 124, 216, 128,
)


def narrow(value):
    return value.astype(BF)


def widen(value):
    return value.astype(F32)


def narrow_pair(value):
    key = value[..., 0:HEAD]
    high = key.astype(BF)
    low = (key - high.astype(F32)).astype(BF)
    return jnp.concatenate([high, low, value[..., HEAD : 2 * HEAD].astype(BF)], -1)


def widen_pair(value):
    value = value.astype(F32)
    key = value[..., 0:HEAD] + value[..., HEAD : 2 * HEAD]
    return jnp.concatenate([key, value[..., 2 * HEAD : 3 * HEAD]], -1)


class Node:
    def __init__(self, name, rank, cost, after, waits, sends, emit):
        self.name, self.rank, self.cost = name, rank, cost
        self.after, self.waits, self.sends, self.emit = after, waits, sends, emit


def rotary_table():
    frequency = np.exp(-np.log(500000.0) * np.arange(HEAD // 2, dtype=np.float64) * 2.0 / HEAD)
    angles = np.arange(SEQ, dtype=np.float64)[:, None] * frequency
    cosine, sine = np.cos(angles), np.sin(angles)
    table = np.concatenate([cosine, cosine, -sine, sine], 1).astype(np.float32)
    return table.reshape(CHUNKS, NZ, 2, R, 2 * HEAD)


def split(parity):
    return (4, 3) if parity == 0 else (3, 4)


def build(k):
    nodes = []

    def add(name, rank, cost, after, waits, sends, emit):
        nodes.append(Node(name, rank, cost, after, waits, sends, emit))

    def zlink(sign):
        return ["z+"] if sign > 0 else ["z-"]

    def emit_kv():
        k.load("wkv")
        for t in range(CHUNKS):
            k.load("tok%d" % t)
            res = jnp.dot(k.tok[pl.ds(t * ROWS, ROWS)], k.wkv[...], preferred_element_type=F32)
            k.pkv[t] = res.reshape(NZ, 2, R, 2 * HEAD)
        k.query_loads()
        k.ready()

    add("kvmm", 0, 4.0, [], [], [], emit_kv)

    def emit_q(t, c0, width):
        for c in range(c0 // 512, (c0 + width - 1) // 512 + 1):
            k.load("wq%d" % c)
        res = jnp.dot(k.tok[pl.ds(t * ROWS, ROWS)], k.wq[:, c0 : c0 + width], preferred_element_type=F32)
        k.pq[t, :, :, :, c0 : c0 + width] = res.reshape(NZ, 2, R, width)
        if k.last_loads:
            k.last_loads()
            k.last_loads = None

    for t in range(CHUNKS):
        for c0, width in ZFIRST + XFIRST:
            add(
                "q%d_%d" % (t, c0),
                1 + t * 40 + (0.1 if c0 < ZFIRST[0][0] else 0),
                width / 620.0,
                ["kvmm"],
                [],
                [],
                functools.partial(emit_q, t, c0, width),
            )

    def ring(tag, rank, stride, cost, size, counts, own, start_after, step_waits, down=narrow, up=widen):
        for sign, n in ((1, counts[0]), (-1, counts[1])):
            base = 0 if sign > 0 else counts[0]
            for s in range(n):
                name = (tag, sign, s)

                def emit(sign=sign, n=n, s=s, base=base, name=name):
                    d = k.zi(sign * (n - s))
                    value = own(sign, s, d)
                    if s > 0:
                        value = value + up(k.buf[tag, "r"][base + s - 1])
                    k.buf[tag, "s"][base + s] = down(value)
                    k.send(name, k.buf[tag, "s"].at[base + s], k.buf[tag, "r"].at[base + s], k.dev_z(sign), tag, k.buf[tag, "s"])

                waits = list(step_waits(sign, s))
                after = list(start_after)
                if s > 0:
                    waits.append((tag, sign, s - 1))
                    after.append((tag, sign, s - 1))
                add(name, rank + stride * s, cost, after, waits, [(name, zlink(sign), size)], emit)
        return [(tag, 1, counts[0] - 1), (tag, -1, counts[1] - 1)]

    def ring_sum(tag, counts, pick, up=widen):
        bufs = k.buf[tag, "r"]
        return up(pick(bufs, counts[0] - 1)) + up(pick(bufs, NZ - 2))

    for t in range(CHUNKS):
        tag, counts, base = "kv%d" % t, split(t), 20 * t
        last = ring(
            tag,
            base + 2,
            4,
            0.2,
            2 * R * 768,
            counts,
            lambda sign, s, d, t=t: k.pkv[t, d],
            ["kvmm"],
            lambda sign, s: [],
            narrow_pair,
            widen_pair,
        )

        def kv_pair(t, tag, counts):
            return k.pkv[t, k.z] + ring_sum(tag, counts, lambda b, i: b[i], widen_pair)

        def emit_kv_fin(t=t, tag=tag, counts=counts):
            k.buf[tag + "x", "s"][...] = narrow_pair(kv_pair(t, tag, counts))
            k.send(tag + "x", k.buf[tag + "x", "s"], k.buf[tag + "x", "r"], k.dev_x())

        add(tag + "fin", base + 2, 0.2, last, last, [(tag + "x", ["x"], 2 * R * 768)], emit_kv_fin)

        def emit_kv_own(t=t, tag=tag, counts=counts):
            k.load("tab")
            value = kv_pair(t, tag, counts) + widen_pair(k.buf[tag + "x", "r"][...])
            for i in range(2):
                k.kvf[t, k.z, i, :, 0:HEAD] = k.rotate(value[i, :, 0:HEAD], t, i).astype(BF)
            k.kvf[t, k.z, :, :, HEAD : 2 * HEAD] = value[:, :, HEAD : 2 * HEAD].astype(BF)

        add(tag + "own", base + 2, 0.3, [tag + "fin"], [tag + "x"], [], emit_kv_own)

    def gather(tag, rank, stride, size, counts, block, start_after, start_waits, seven):
        for sign, n in ((1, counts[0]), (-1, counts[1])):
            for s in range(n):
                name = (tag, sign, s)

                def emit(sign=sign, s=s, name=name):
                    here = block(k.zi(-sign * s))
                    k.send(name, here, here, k.dev_z(sign), tag, seven())

                after = list(start_after) if s == 0 else [(tag, sign, s - 1)]
                waits = list(start_waits) if s == 0 else [(tag, sign, s - 1)]
                add(name, rank + stride * s, 0.1, after, waits, [(name, zlink(sign), size)], emit)
        return [(tag, 1, counts[0] - 1), (tag, -1, counts[1] - 1)]

    kg_last = [
        gather(
            "kg%d" % t,
            20 * t + 2,
            1,
            2 * R * 512,
            split(1 - t),
            lambda d, t=t: k.kvf.at[t, d],
            ["kv%down" % t],
            [],
            lambda t=t: k.kvf.at[t, 0 : NZ - 1],
        )
        for t in range(CHUNKS)
    ]

    for t in range(CHUNKS):
        base = 40 * t
        own_nodes = {}
        for j, (c0, width) in enumerate(ZFIRST):
            tag, counts = "zf%d_%d" % (t, c0), split(j)
            last = ring(
                tag,
                base + 3 + 0.2 * j,
                8,
                0.2,
                2 * R * width * 2,
                counts,
                lambda sign, s, d, c0=c0, width=width, t=t: k.pq[t, d, :, :, c0 : c0 + width],
                ["q%d_%d" % (t, c0)],
                lambda sign, s: [],
            )

            def emit_fin(t=t, tag=tag, c0=c0, width=width, counts=counts):
                o = 1 - k.xh
                value = k.pq[t, k.z, o, :, c0 : c0 + width] + ring_sum(tag, counts, lambda b, i: b[i, o])
                k.buf[tag + "x", "s"][...] = value.astype(BF)
                k.send(tag + "x", k.buf[tag + "x", "s"], k.buf[tag + "x", "r"], k.dev_x())

            add(tag + "fin", base + 36, 0.2, last, last, [(tag + "x", ["x"], R * width * 2)], emit_fin)

            def emit_own(t=t, tag=tag, c0=c0, width=width, counts=counts):
                k.load("tab")
                value = k.pq[t, k.z, k.xh, :, c0 : c0 + width] + ring_sum(tag, counts, lambda b, i: b[i, k.xh])
                k.store_query(t, c0, value + k.buf[tag + "x", "r"][...].astype(F32))

            add(tag + "own", base + 37, 0.25, [tag + "fin"], [tag + "x"], [], emit_own)
            own_nodes[c0] = tag + "own"

        for j, (c0, width) in enumerate(XFIRST):
            tag, counts = "xf%d_%d" % (t, c0), split(j + t)
            slots = [(1, s) for s in range(counts[0])] + [(-1, s) for s in range(counts[1])] + [(0, 0)]
            queue = sorted(range(NZ), key=lambda i, slots=slots: (slots[i][1] if slots[i][0] else 9, i))

            def where(i, counts=counts, slots=slots):
                sign, s = slots[i]
                n = counts[0] if sign > 0 else counts[1]
                return k.zi(sign * (n - s)) if sign else k.z

            for place, i in enumerate(queue):

                def emit_x(t=t, tag=tag, i=i, c0=c0, width=width, where=where):
                    k.buf[tag + "x", "s"][i] = k.pq[t, where(i), 1 - k.xh, :, c0 : c0 + width].astype(BF)
                    k.send(
                        (tag, "x", i),
                        k.buf[tag + "x", "s"].at[i],
                        k.buf[tag + "x", "r"].at[i],
                        k.dev_x(),
                        tag + "x",
                        k.buf[tag + "x", "s"],
                    )

                add(
                    (tag, "x", i),
                    base + 4 + 0.1 * place - (8 if t else 0),
                    0.1,
                    ["q%d_%d" % (t, c0)],
                    [],
                    [((tag, "x", i), ["x"], R * width * 2)],
                    emit_x,
                )

            def own_xf(sign, s, d, t=t, tag=tag, c0=c0, width=width, counts=counts):
                i = s if sign > 0 else counts[0] + s
                return k.pq[t, d, k.xh, :, c0 : c0 + width] + k.buf[tag + "x", "r"][i].astype(F32)

            last = ring(
                tag,
                base + 9,
                8,
                0.2,
                R * width * 2,
                counts,
                own_xf,
                [(tag, "x", i) for i in range(NZ)],
                lambda sign, s, tag=tag, counts=counts: [(tag, "x", s if sign > 0 else counts[0] + s)],
            )

            def emit_xf_own(t=t, tag=tag, c0=c0, width=width, counts=counts):
                k.load("tab")
                value = k.pq[t, k.z, k.xh, :, c0 : c0 + width] + k.buf[tag + "x", "r"][NZ - 1].astype(F32)
                k.store_query(t, c0, value + ring_sum(tag, counts, lambda b, i: b[i]))

            add(tag + "own", base + 37.5, 0.25, last, last + [(tag, "x", NZ - 1)], [], emit_xf_own)
            own_nodes[c0] = tag + "own"

        add("mask%d" % t, base + 20, 0.3, ["kvmm"], [], [], functools.partial(lambda t: k.mask(t), t))
        keys_in = [m for u in range(t + 1) for m in kg_last[u]]
        keys_after = [m for u in range(t + 1) for m in ["kv%down" % u] + kg_last[u]]
        for place, (c0, width) in enumerate(ZFIRST + XFIRST):
            gtag = "g%d_%d" % (t, c0)

            def emit_att(t=t, gtag=gtag, c0=c0, width=width):
                k.attend(t, c0 // HEAD, width // HEAD)
                here = k.att.at[t, k.z, k.xh, :, c0 : c0 + width]
                count = NZ if (c0, width) in XFIRST else 1
                k.send(
                    (gtag, "x", 0), here, here, k.dev_x(), gtag + "x", k.att.at[t, 0:count, 0, :, c0 : c0 + width]
                )

            add(
                gtag + "att",
                base + 40 + place,
                width / 1700.0 + 0.15,
                [own_nodes[c0], "mask%d" % t] + keys_after,
                keys_in,
                [((gtag, "x", 0), ["x"], R * width * 2)],
                emit_att,
            )
        last_step = []
        for j, (c0, width) in enumerate(ZFIRST):
            gtag = "g%d_%d" % (t, c0)
            gather(
                gtag,
                base + 44 + 0.1 * j,
                4,
                2 * R * width * 2,
                split(j),
                lambda d, t=t, c0=c0, width=width: k.att.at[t, d, :, :, c0 : c0 + width],
                [gtag + "att"],
                [(gtag, "x", 0)],
                lambda t=t, c0=c0, width=width: k.att.at[t, 0 : NZ - 1, :, :, c0 : c0 + width],
            )
            last_step.append((gtag, False, split(j)))
        for j, (c0, width) in enumerate(XFIRST):
            gtag, counts = "g%d_%d" % (t, c0), split(j + t)
            gather(
                gtag,
                base + 43,
                4,
                R * width * 2,
                counts,
                lambda d, t=t, c0=c0, width=width: k.att.at[t, d, k.xh, :, c0 : c0 + width],
                [gtag + "att"],
                [],
                lambda t=t, c0=c0, width=width: k.att.at[t, 0 : NZ - 1, 0, :, c0 : c0 + width],
            )
            last_step.append((gtag, True, counts))
            for sign, n in ((1, counts[0]), (-1, counts[1])):
                for s in range(n):
                    name = (gtag, "x", sign, s)

                    def emit_pass(t=t, gtag=gtag, sign=sign, s=s, name=name, c0=c0, width=width):
                        here = k.att.at[t, k.zi(-sign * (s + 1)), k.xh, :, c0 : c0 + width]
                        blocks = 1 if s == 3 else 2
                        k.send(
                            name,
                            here,
                            here,
                            k.dev_x(),
                            gtag + "x",
                            k.att.at[t, 0:NZ, 0, :, c0 : c0 + width],
                            ("pass", t, s),
                            k.att.at[t, 0:blocks, 0, :, 0:XWIDTH],
                        )

                    after = [(gtag, sign, s + 1)] if s + 1 < n else [(gtag, sign, s)]
                    add(
                        name,
                        base + 43.5 + 4 * s,
                        0.1,
                        after,
                        [(gtag, sign, s)],
                        [(name, ["x"], R * width * 2)],
                        emit_pass,
                    )
        for rounds in OUTS[t]:
            r = rounds[-1]
            shifts, first = [], (2 * rounds[0] - 1 if rounds[0] else 0)
            waits, after = [], []
            for q in rounds:
                shifts += [0] if q == 0 else [4] if q == 4 else [-q, q]
                for gtag, passes, counts in last_step:
                    if q == 0:
                        waits.append((gtag, "x", 0))
                        after.append(gtag + "att")
                    for sign, n in ((1, counts[0]), (-1, counts[1])):
                        if 0 < q <= n:
                            waits.append((gtag, sign, q - 1))
                            after.append((gtag, sign, q - 1))
                            if passes:
                                waits.append((gtag, "x", sign, q - 1))
                                after.append((gtag, "x", sign, q - 1))

            def emit_out(t=t, r=r, shifts=shifts, first=first):
                k.load("wout")
                count = len(shifts)
                rows = [k.att[t, k.zi(s)].reshape(2 * R, QCOLS) for s in shifts]
                lhs = rows[0] if count == 1 else jnp.concatenate(rows, 0)
                for delta in (2, 1, 3, 0):
                    c0 = pl.multiple_of(lax.rem(k.y + delta, NY) * 256, 256)
                    res = jnp.dot(lhs, k.wout[:, pl.ds(c0, 256)], preferred_element_type=F32)
                    res = res.reshape(count, 2 * R, 256)
                    if delta == 0:
                        k.oown[t, first : first + count] = res
                    else:
                        k.ys[t, delta - 1, first : first + count] = res.astype(BF)
                        k.send(
                            ("y", t, r, delta),
                            k.ys.at[t, delta - 1, first : first + count],
                            k.yr.at[t, delta - 1, first : first + count],
                            k.dev_y(delta),
                            "y",
                            k.ys,
                            ("y", t, r),
                            k.yr.at[t, :, first : first + count],
                        )

            size = len(shifts) * 2 * R * 512
            add(
                ("out", t, r),
                base + 45 + 4 * r,
                0.55 + 0.15 + 0.0024 * 2 * R * len(shifts),
                after,
                waits,
                [(("y", t, r, 2), ["y+", "y-"], size), (("y", t, r, 1), ["y+"], size), (("y", t, r, 3), ["y-"], size)],
                emit_out,
            )

            def emit_fin(t=t, shifts=shifts, first=first):
                for i, shift in enumerate(shifts):
                    total = k.oown[t, first + i]
                    for delta in range(NY - 1):
                        total = total + k.yr[t, delta, first + i].astype(F32)
                    row = pl.multiple_of(t * ROWS + k.zi(shift) * 2 * R, 2 * R)
                    k.out[pl.ds(row, 2 * R), :] = total

            add(
                ("fin", t, r),
                base + 50 + 4 * r,
                0.15 + 0.05 * len(shifts),
                [("out", t, r)],
                [("y", t, r, delta) for delta in (1, 2, 3)],
                [],
                emit_fin,
            )
    return nodes


def buffers():
    shapes = {}
    for t in range(CHUNKS):
        shapes["kv%d" % t] = (7, 2, R, 384)
        shapes["kv%dx" % t] = (2, R, 384)
        for c0, width in ZFIRST:
            shapes["zf%d_%d" % (t, c0)] = (7, 2, R, width)
            shapes["zf%d_%dx" % (t, c0)] = (R, width)
        for c0, width in XFIRST:
            shapes["xf%d_%d" % (t, c0)] = (7, R, width)
            shapes["xf%d_%dx" % (t, c0)] = (8, R, width)
    return shapes


class Kernel:
    pass


def kernel(order_names, messages, *refs):
    shapes = buffers()
    names = ["docs", "h_tok", "h_wq", "h_wk", "h_wv", "h_wout", "h_tab", "out"]
    names += ["tok", "wq", "wkv", "wout", "tab", "bias", "pq", "pkv", "kvf", "qs", "att", "oown", "ys", "yr"]
    k = Kernel()
    for name, ref in zip(names, refs):
        setattr(k, name, ref)
    rest = refs[len(names) :]
    k.buf = {}
    for i, name in enumerate(shapes):
        k.buf[name, "s"], k.buf[name, "r"] = rest[2 * i], rest[2 * i + 1]
    send_sem, recv_sem, load_sem = rest[2 * len(shapes) :]

    loop, k.y = lax.axis_index("loop"), lax.axis_index("column")
    k.xh, k.z = loop // NZ, lax.rem(loop, NZ)
    k.zi = lambda delta: lax.rem(k.z + (delta + NZ), NZ) if delta else k.z
    k.dev_z = lambda sign: {"loop": k.xh * NZ + k.zi(sign)}
    k.dev_x = lambda: {"loop": (1 - k.xh) * NZ + k.z}
    k.dev_y = lambda delta: {"column": lax.rem(k.y + delta, NY)}
    mesh_id = pl.DeviceIdType.MESH

    barrier = pltpu.get_barrier_semaphore()
    peers = [k.dev_z(1), k.dev_z(-1), k.dev_x()] + [k.dev_y(delta) for delta in (1, 2, 3)]
    for peer in peers:
        pl.semaphore_signal(barrier, inc=1, device_id=peer, device_id_type=mesh_id)

    loads, started = {}, []

    def start_load(name, src, dst):
        loads[name] = pltpu.make_async_copy(src, dst, load_sem.at[len(started)])
        started.append(name)
        loads[name].start()

    def first_loads():
        start_load("wk", k.h_wk, k.wkv.at[:, 0:HEAD])
        start_load("wv", k.h_wv, k.wkv.at[:, HEAD : 2 * HEAD])
        for t in range(CHUNKS):
            start_load("tok%d" % t, k.h_tok.at[pl.ds(t * ROWS, ROWS)], k.tok.at[pl.ds(t * ROWS, ROWS)])

    def query_loads():
        for c in QUERY_PARTS:
            cols = slice(c * 512, (c + 1) * 512)
            start_load("wq%d" % c, k.h_wq.at[:, cols], k.wq.at[:, cols])

    def last_loads():
        start_load("tab", k.h_tab.at[:, k.z], k.tab)
        start_load("wout", k.h_wout, k.wout)

    first_loads()
    k.query_loads, k.last_loads = query_loads, last_loads

    def load(name):
        if name in ("tab", "wout") and k.last_loads:
            k.last_loads()
            k.last_loads = None
        if name == "wkv":
            load("wk")
            load("wv")
        elif name in loads:
            loads.pop(name).wait()

    k.load = load
    k.ready = lambda: pl.semaphore_wait(barrier, len(peers))
    sent, waited, send_groups, recv_groups, recv_wholes = {}, set(), {}, {}, {}

    def send(name, src, dst, device, group=None, whole=None, recv=None, recv_whole=None):
        group, recv = group or name, recv or name
        i = list(send_groups).index(group) if group in send_groups else len(send_groups)
        j = recv_ids.setdefault(recv, len(recv_ids))
        sent[name] = pltpu.make_async_remote_copy(
            src_ref=src,
            dst_ref=dst,
            send_sem=send_sem.at[i],
            recv_sem=recv_sem.at[j],
            device_id=device,
            device_id_type=mesh_id,
        )
        sent[name].start()
        recv_groups[name] = recv
        if group not in send_groups:
            ref = src if whole is None else whole
            send_groups[group] = pltpu.make_async_remote_copy(ref, ref, send_sem.at[i], recv_sem.at[j], device, mesh_id)
        if recv not in recv_wholes:
            ref = dst if recv_whole is None else recv_whole
            recv_wholes[recv] = pltpu.make_async_remote_copy(ref, ref, send_sem.at[i], recv_sem.at[j], device, mesh_id)

    def receive(name):
        recv = recv_groups[name]
        if recv not in waited:
            waited.add(recv)
            recv_wholes[recv].wait_recv()

    recv_ids = {}
    k.send = send

    def rotate(value, t, half):
        table = k.tab[t, half]
        return value * table[:, 0:HEAD] + pltpu.roll(value, HEAD // 2, 1) * table[:, HEAD : 2 * HEAD]

    k.rotate = rotate

    def store_query(t, c0, value):
        for i in range(value.shape[1] // HEAD):
            k.qs[t, c0 // HEAD + i] = rotate(value[:, i * HEAD : (i + 1) * HEAD], t, k.xh).astype(BF)

    k.store_query = store_query

    def mask(t):
        keys = (t + 1) * ROWS
        row = t * ROWS + (k.z * 2 + k.xh) * R + lax.broadcasted_iota(jnp.int32, (R, keys), 0)
        col = lax.broadcasted_iota(jnp.int32, (R, keys), 1)
        docs = jnp.broadcast_to(k.docs[0:1, 0:keys].astype(F32), (R, keys))
        mine = jnp.sum(jnp.where(row == col, docs, 0.0), axis=1, keepdims=True)
        allowed = (docs == mine) & (col <= row)
        k.bias[t, :, 0:keys] = jnp.where(allowed, 0.0, -1e30)

    k.mask = mask

    def attend(t, first, count):
        keys = (t + 1) * ROWS
        query = k.qs[t, first : first + count].reshape(count * R, HEAD)
        key = k.kvf[0 : t + 1, :, :, :, 0:HEAD].reshape(keys, HEAD)
        value = k.kvf[0 : t + 1, :, :, :, HEAD : 2 * HEAD].reshape(keys, HEAD)
        scores = lax.dot_general(query, key, (((1,), (1,)), ((), ())), preferred_element_type=F32)
        scores = (scores * SCALE).reshape(count, R, keys) + k.bias[t, :, 0:keys][None]
        top = jnp.max(scores, axis=-1, keepdims=True)
        weights = jnp.exp2(scores - top)
        total = jnp.sum(weights, axis=-1, keepdims=True)
        mixed = jnp.dot(weights.reshape(count * R, keys).astype(BF), value, preferred_element_type=F32)
        mixed = (mixed.reshape(count, R, HEAD) / total).astype(BF)
        for i in range(count):
            c0 = (first + i) * HEAD
            k.att[t, k.z, k.xh, :, c0 : c0 + HEAD] = mixed[i]

    k.attend = attend

    nodes = {node.name: node for node in build(k)}
    for name in order_names:
        node = nodes[name]
        for message in node.waits:
            receive(message)
        node.emit()
    for name in messages:
        receive(name)
    for copy in send_groups.values():
        copy.wait_send()
    for name in list(loads):
        load(name)


def semaphores(messages):
    sends, receives = set(), set()
    for name in messages:
        group, receive = name, name
        if isinstance(name, tuple):
            tag = name[0]
            if tag == "y":
                group, receive = "y", name[:3]
            elif name[1] == "x":
                group = tag + "x"
                if len(name) == 4:
                    receive = ("pass", tag[:2], name[3])
            else:
                group = tag
        sends.add(group)
        receives.add(receive)
    return len(sends), len(receives)


def shards(tokens, doc_ids, w_query, key_weight, value_weight, w_out):
    nodes = build(None)
    order = [nodes[i] for i in ORDER]
    messages = [send[0] for node in order for send in node.sends]
    sends, receives = semaphores(messages)
    scratch = [
        pltpu.VMEM((SEQ, MODEL), BF),
        pltpu.VMEM((MODEL, QCOLS), BF),
        pltpu.VMEM((MODEL, 2 * HEAD), BF),
        pltpu.VMEM((QCOLS, OCOLS), BF),
        pltpu.VMEM((CHUNKS, 2, R, 2 * HEAD), F32),
        pltpu.VMEM((CHUNKS, R, SEQ), F32),
        pltpu.VMEM((CHUNKS, NZ, 2, R, QCOLS), F32),
        pltpu.VMEM((CHUNKS, NZ, 2, R, 2 * HEAD), F32),
        pltpu.VMEM((CHUNKS, NZ, 2, R, 2 * HEAD), BF),
        pltpu.VMEM((CHUNKS, QCOLS // HEAD, R, HEAD), BF),
        pltpu.VMEM((CHUNKS, NZ, 2, R, QCOLS), BF),
        pltpu.VMEM((CHUNKS, NZ, 2 * R, 256), F32),
        pltpu.VMEM((CHUNKS, NY - 1, NZ, 2 * R, 256), BF),
        pltpu.VMEM((CHUNKS, NY - 1, NZ, 2 * R, 256), BF),
    ]
    for shape in buffers().values():
        scratch += [pltpu.VMEM(shape, BF), pltpu.VMEM(shape, BF)]
    scratch += [
        pltpu.SemaphoreType.DMA((sends,)),
        pltpu.SemaphoreType.DMA((receives,)),
        pltpu.SemaphoreType.DMA((16,)),
    ]
    anywhere = pl.BlockSpec(memory_space=pl.ANY)
    vmem = pl.BlockSpec(memory_space=pltpu.VMEM)
    return pl.pallas_call(
        functools.partial(kernel, [node.name for node in order], messages),
        out_shape=jax.ShapeDtypeStruct((SEQ, 256), F32),
        in_specs=[vmem] + [anywhere] * 6,
        out_specs=vmem,
        scratch_shapes=scratch,
        compiler_params=pltpu.CompilerParams(
            collective_id=0, has_side_effects=True, vmem_limit_bytes=56 * 1024 * 1024
        ),
        name="sublayer",
    )(doc_ids.reshape(1, SEQ), tokens, w_query, key_weight, value_weight, w_out, jnp.asarray(rotary_table())).astype(BF)


def solution(mesh):
    placed = (
        P("dp", "loop"),
        P("dp"),
        P("loop", "column"),
        P("loop", "column"),
        P("loop", "column"),
        P("column", "loop"),
    )
    return jax.shard_map(
        shards, mesh=mesh, in_specs=placed, out_specs=P("dp", ("loop", "column")), check_vma=False
    )
```

```python
import functools
import math

import jax
import jax.numpy as jnp
import numpy as np
from jax import lax
from jax.experimental import pallas as pl
from jax.experimental.pallas import tpu as pltpu
from jax.sharding import PartitionSpec as P

HEAD = 128
SEQ = 1024
MODEL = 1024
QCOLS = 2048
OCOLS = 1024
NZ = 8
NY = 4
CHUNKS = 2
ROWS = SEQ // CHUNKS
R = ROWS // (2 * NZ)
XFIRST = ((0, 1024),)
ZFIRST = ((1024, 512), (1536, 512))
QUERY_PARTS = (2, 3, 0, 1)
QUARTER = QCOLS // 4
PIECES = 4
PIECE = QUARTER // PIECES
OUTS = (((0,), (1,), (2,), (3,), (4,)), ((0,), (1,), (2,), (3,), (4,)))
BF = jnp.bfloat16
F32 = jnp.float32
SCALE = math.log2(math.e) / math.sqrt(HEAD)
ORDER = (
    0, 8, 206, 7, 4, 9, 15, 14, 2, 203, 1, 117, 11, 10, 29, 3, 48, 18, 17, 16, 47, 5, 125, 6, 138, 38, 12, 113, 30,
    51, 41, 197, 49, 122, 118, 33, 42, 13, 126, 31, 63, 133, 23, 50, 132, 54, 39, 19, 134, 52, 53, 114, 131, 123,
    43, 200, 136, 59, 115, 32, 55, 21, 135, 137, 24, 34, 60, 20, 25, 142, 22, 56, 35, 147, 44, 127, 143, 139, 40,
    128, 36, 119, 27, 116, 124, 57, 45, 140, 144, 201, 120, 61, 129, 58, 28, 26, 141, 37, 145, 64, 71, 46, 65, 77,
    67, 74, 207, 198, 121, 62, 66, 202, 130, 84, 81, 149, 161, 158, 148, 154, 204, 146, 150, 88, 168, 165, 172,
    151, 208, 68, 82, 72, 78, 93, 199, 205, 85, 159, 155, 169, 75, 162, 173, 166, 177, 79, 152, 90, 174, 95, 69,
    86, 76, 83, 179, 100, 163, 156, 153, 167, 184, 91, 170, 182, 70, 175, 80, 73, 180, 160, 87, 98, 164, 89, 96,
    157, 171, 185, 101, 105, 178, 110, 189, 94, 194, 192, 187, 103, 111, 106, 108, 190, 195, 183, 99, 193, 186, 92,
    112, 188, 104, 107, 97, 176, 181, 102, 109, 191, 196,
)


def narrow(value):
    return value.astype(BF)


def widen(value):
    return value.astype(F32)


def narrow_pair(value):
    key = value[..., 0:HEAD]
    high = key.astype(BF)
    low = (key - high.astype(F32)).astype(BF)
    return jnp.concatenate([high, low, value[..., HEAD : 2 * HEAD].astype(BF)], -1)


def widen_pair(value):
    value = value.astype(F32)
    key = value[..., 0:HEAD] + value[..., HEAD : 2 * HEAD]
    return jnp.concatenate([key, value[..., 2 * HEAD : 3 * HEAD]], -1)


class Node:
    def __init__(self, name, rank, cost, after, waits, sends, emit):
        self.name, self.rank, self.cost = name, rank, cost
        self.after, self.waits, self.sends, self.emit = after, waits, sends, emit


def rotary_table():
    frequency = np.exp(-np.log(500000.0) * np.arange(HEAD // 2, dtype=np.float64) * 2.0 / HEAD)
    angles = np.arange(SEQ, dtype=np.float64)[:, None] * frequency
    cosine, sine = np.cos(angles), np.sin(angles)
    table = np.concatenate([cosine, cosine, -sine, sine], 1).astype(np.float32)
    return table.reshape(CHUNKS, NZ, 2, R, 2 * HEAD)


def split(parity):
    return (4, 3) if parity == 0 else (3, 4)


def build(k):
    nodes = []

    def add(name, rank, cost, after, waits, sends, emit):
        nodes.append(Node(name, rank, cost, after, waits, sends, emit))

    def zlink(sign):
        return ["z+"] if sign > 0 else ["z-"]

    def emit_kv():
        k.load("wkv")
        for t in range(CHUNKS):
            k.load("tok%d" % t)
            res = jnp.dot(k.tok[pl.ds(t * ROWS, ROWS)], k.wkv[...], preferred_element_type=F32)
            k.pkv[t] = res.reshape(NZ, 2, R, 2 * HEAD)
        k.query_loads()
        k.ready()

    add("kvmm", 0, 4.0, [], [], [], emit_kv)

    def emit_q(t, c0, width):
        for c in range(c0 // 512, (c0 + width - 1) // 512 + 1):
            k.load("wq%d" % c)
        res = jnp.dot(k.tok[pl.ds(t * ROWS, ROWS)], k.wq[:, c0 : c0 + width], preferred_element_type=F32)
        k.pq[t, :, :, :, c0 : c0 + width] = res.reshape(NZ, 2, R, width)
        if k.last_loads:
            k.last_loads()
            k.last_loads = None

    for t in range(CHUNKS):
        for c0, width in ZFIRST + XFIRST:
            add(
                "q%d_%d" % (t, c0),
                1 + t * 40 + (0.1 if c0 < ZFIRST[0][0] else 0),
                width / 620.0,
                ["kvmm"],
                [],
                [],
                functools.partial(emit_q, t, c0, width),
            )

    def ring(tag, rank, stride, cost, size, counts, own, start_after, step_waits, down=narrow, up=widen):
        for sign, n in ((1, counts[0]), (-1, counts[1])):
            base = 0 if sign > 0 else counts[0]
            for s in range(n):
                name = (tag, sign, s)

                def emit(sign=sign, n=n, s=s, base=base, name=name):
                    d = k.zi(sign * (n - s))
                    value = own(sign, s, d)
                    if s > 0:
                        value = value + up(k.buf[tag, "r"][base + s - 1])
                    k.buf[tag, "s"][base + s] = down(value)
                    k.send(name, k.buf[tag, "s"].at[base + s], k.buf[tag, "r"].at[base + s], k.dev_z(sign), tag, k.buf[tag, "s"])

                waits = list(step_waits(sign, s))
                after = list(start_after)
                if s > 0:
                    waits.append((tag, sign, s - 1))
                    after.append((tag, sign, s - 1))
                add(name, rank + stride * s, cost, after, waits, [(name, zlink(sign), size)], emit)
        return [(tag, 1, counts[0] - 1), (tag, -1, counts[1] - 1)]

    def ring_sum(tag, counts, pick, up=widen):
        bufs = k.buf[tag, "r"]
        return up(pick(bufs, counts[0] - 1)) + up(pick(bufs, NZ - 2))

    for t in range(CHUNKS):
        tag, base = "kv%d" % t, 20 * t
        unit = 2 * R * 512

        def emit_far(sign, t=t, tag=tag):
            half, slot = (0, 0) if sign > 0 else (1, 1)
            buf, quarter_buf = k.buf[tag, "s"], k.buf[tag + "q", "s"]
            buf[slot] = k.pkv[t, k.zi(3 * sign)].astype(BF)
            k.send((tag, "m", slot), buf.at[slot], k.buf[tag, "r"].at[slot], k.dev_z(sign), tag, buf)
            cols = slice(half * HEAD, (half + 1) * HEAD)
            quarter_buf[half] = k.pkv[t, k.zi(4), :, :, cols].astype(BF)
            k.send(
                (tag, "q", half),
                quarter_buf.at[half],
                k.buf[tag + "q", "r"].at[half],
                k.dev_z(2 * sign),
                tag + "q",
                quarter_buf,
            )

        def emit_near(t=t, tag=tag):
            for sign in (1, -1):
                slot = 2 if sign > 0 else 3
                k.buf[tag, "s"][slot] = k.pkv[t, k.zi(sign)].astype(BF)
                k.send(
                    (tag, "m", slot),
                    k.buf[tag, "s"].at[slot],
                    k.buf[tag, "r"].at[slot],
                    k.dev_z(sign),
                    tag,
                    k.buf[tag, "s"],
                )

        def emit_on(sign, t=t, tag=tag):
            half, slot = (0, 4) if sign > 0 else (1, 5)
            value = k.pkv[t, k.zi(2 * sign)] + k.buf[tag, "r"][slot - 4].astype(F32)
            extra = k.buf[tag + "q", "r"][half].astype(F32)
            parts = [value[..., 0:HEAD], value[..., HEAD : 2 * HEAD]]
            parts[half] = parts[half] + extra
            k.buf[tag, "s"][slot] = jnp.concatenate(parts, -1).astype(BF)
            k.send(
                (tag, "m", slot),
                k.buf[tag, "s"].at[slot],
                k.buf[tag, "r"].at[slot],
                k.dev_z(2 * sign),
                tag,
                k.buf[tag, "s"],
            )

        for sign in (1, -1):
            half = 0 if sign > 0 else 1
            add(
                (tag, "A", sign),
                base + 2,
                0.3,
                ["kvmm"],
                [],
                [((tag, "m", half), zlink(sign), unit), ((tag, "q", half), zlink(sign), unit)],
                functools.partial(emit_far, sign),
            )
        add(
            (tag, "C", 0),
            base + 3,
            0.3,
            [(tag, "A", 1), (tag, "A", -1)],
            [],
            [((tag, "m", 2), ["z+"], unit), ((tag, "m", 3), ["z-"], unit)],
            emit_near,
        )
        for sign in (1, -1):
            half = 0 if sign > 0 else 1
            add(
                (tag, "B", sign),
                base + 2,
                0.2,
                [(tag, "A", 1), (tag, "A", -1)],
                [(tag, "m", half), (tag, "q", half)],
                [((tag, "m", 4 + half), zlink(sign), 2 * unit)],
                functools.partial(emit_on, sign),
            )
        last = [(tag, "B", 1), (tag, "B", -1), (tag, "C", 0)]

        def kv_pair(t, tag):
            total = k.pkv[t, k.z]
            for slot in range(2, 6):
                total = total + k.buf[tag, "r"][slot].astype(F32)
            return total

        def emit_kv_fin(t=t, tag=tag):
            k.buf[tag + "x", "s"][...] = narrow_pair(kv_pair(t, tag))
            k.send(tag + "x", k.buf[tag + "x", "s"], k.buf[tag + "x", "r"], k.dev_x())

        add(
            tag + "fin",
            base + 2,
            0.2,
            last,
            [(tag, "m", slot) for slot in range(2, 6)],
            [(tag + "x", ["x"], 2 * R * 768)],
            emit_kv_fin,
        )

        def emit_kv_own(t=t, tag=tag):
            k.load("tab")
            value = kv_pair(t, tag) + widen_pair(k.buf[tag + "x", "r"][...])
            for i in range(2):
                k.kvf[t, k.z, i, :, 0:HEAD] = k.rotate(value[i, :, 0:HEAD], t, i).astype(BF)
            k.kvf[t, k.z, :, :, HEAD : 2 * HEAD] = value[:, :, HEAD : 2 * HEAD].astype(BF)

        add(tag + "own", base + 2, 0.3, [tag + "fin"], [tag + "x"], [], emit_kv_own)

    def gather(tag, rank, stride, size, counts, block, start_after, start_waits, seven):
        for sign, n in ((1, counts[0]), (-1, counts[1])):
            for s in range(n):
                name = (tag, sign, s)

                def emit(sign=sign, s=s, name=name):
                    here = block(k.zi(-sign * s))
                    k.send(name, here, here, k.dev_z(sign), tag, seven())

                after = list(start_after) if s == 0 else [(tag, sign, s - 1)]
                waits = list(start_waits) if s == 0 else [(tag, sign, s - 1)]
                add(name, rank + stride * s, 0.1, after, waits, [(name, zlink(sign), size)], emit)
        return [(tag, 1, counts[0] - 1), (tag, -1, counts[1] - 1)]

    kg_waits, kg_nodes = [], []
    for t in range(CHUNKS):
        tag, unit = "kg%d" % t, 2 * R * 512

        def emit_own_block(sign, t=t, tag=tag):
            here = k.kvf.at[t, k.z]
            k.send((tag, "n", sign), here, here, k.dev_z(sign))
            k.send((tag, "f", sign), here, here, k.dev_z(2 * sign))

        def emit_on_block(sign, t=t, tag=tag):
            here = k.kvf.at[t, k.zi(-2 * sign)]
            k.send((tag, "t", sign), here, here, k.dev_z(sign))
            first = 0 if sign > 0 else HEAD
            here = k.kvf.at[t, k.zi(-2 * sign), :, :, first : first + HEAD]
            k.send((tag, "h", sign), here, here, k.dev_z(2 * sign))

        for sign in (1, -1):
            add(
                (tag, "A", sign),
                20 * t + 2,
                0.2,
                ["kv%down" % t],
                [],
                [((tag, "f", sign), zlink(sign), 2 * unit), ((tag, "n", sign), zlink(sign), unit)],
                functools.partial(emit_own_block, sign),
            )
            add(
                (tag, "B", sign),
                20 * t + 2,
                0.2,
                [(tag, "A", sign)],
                [(tag, "f", sign)],
                [((tag, "t", sign), zlink(sign), unit), ((tag, "h", sign), zlink(sign), unit)],
                functools.partial(emit_on_block, sign),
            )
        kg_waits.append([(tag, part, sign) for part in "nth" for sign in (1, -1)])
        kg_nodes.append([(tag, "B", 1), (tag, "B", -1)])

    for t in range(CHUNKS):
        base = 40 * t
        own_nodes = {}
        for j, (c0, width) in enumerate(ZFIRST):
            tag, counts = "zf%d_%d" % (t, c0), split(j)
            last = ring(
                tag,
                base + 3 + 0.2 * j,
                8,
                0.2,
                2 * R * width * 2,
                counts,
                lambda sign, s, d, c0=c0, width=width, t=t: k.pq[t, d, :, :, c0 : c0 + width],
                ["q%d_%d" % (t, c0)],
                lambda sign, s: [],
            )

            def emit_fin(t=t, tag=tag, c0=c0, width=width, counts=counts):
                o = 1 - k.xh
                value = k.pq[t, k.z, o, :, c0 : c0 + width] + ring_sum(tag, counts, lambda b, i: b[i, o])
                k.buf[tag + "x", "s"][...] = value.astype(BF)
                k.send(tag + "x", k.buf[tag + "x", "s"], k.buf[tag + "x", "r"], k.dev_x())

            add(tag + "fin", base + 36, 0.2, last, last, [(tag + "x", ["x"], R * width * 2)], emit_fin)

            def emit_own(t=t, tag=tag, c0=c0, width=width, counts=counts):
                k.load("tab")
                value = k.pq[t, k.z, k.xh, :, c0 : c0 + width] + ring_sum(tag, counts, lambda b, i: b[i, k.xh])
                k.store_query(t, c0, value + k.buf[tag + "x", "r"][...].astype(F32))

            add(tag + "own", base + 37, 0.25, [tag + "fin"], [tag + "x"], [], emit_own)
            own_nodes[c0] = tag + "own"

        for j, (c0, width) in enumerate(XFIRST):
            tag, counts = "xf%d_%d" % (t, c0), split(j + t)
            slots = [(1, s) for s in range(counts[0])] + [(-1, s) for s in range(counts[1])] + [(0, 0)]
            queue = sorted(range(NZ), key=lambda i, slots=slots: (slots[i][1] if slots[i][0] else 9, i))

            def where(i, counts=counts, slots=slots):
                sign, s = slots[i]
                n = counts[0] if sign > 0 else counts[1]
                return k.zi(sign * (n - s)) if sign else k.z

            for place, i in enumerate(queue):

                def emit_x(t=t, tag=tag, i=i, c0=c0, width=width, where=where):
                    k.buf[tag + "x", "s"][i] = k.pq[t, where(i), 1 - k.xh, :, c0 : c0 + width].astype(BF)
                    k.send(
                        (tag, "x", i),
                        k.buf[tag + "x", "s"].at[i],
                        k.buf[tag + "x", "r"].at[i],
                        k.dev_x(),
                        tag + "x",
                        k.buf[tag + "x", "s"],
                    )

                add(
                    (tag, "x", i),
                    base + 4 + 0.1 * place - (8 if t else 0),
                    0.1,
                    ["q%d_%d" % (t, c0)],
                    [],
                    [((tag, "x", i), ["x"], R * width * 2)],
                    emit_x,
                )

            def own_xf(sign, s, d, t=t, tag=tag, c0=c0, width=width, counts=counts):
                i = s if sign > 0 else counts[0] + s
                return k.pq[t, d, k.xh, :, c0 : c0 + width] + k.buf[tag + "x", "r"][i].astype(F32)

            last = ring(
                tag,
                base + 9,
                8,
                0.2,
                R * width * 2,
                counts,
                own_xf,
                [(tag, "x", i) for i in range(NZ)],
                lambda sign, s, tag=tag, counts=counts: [(tag, "x", s if sign > 0 else counts[0] + s)],
            )

            def emit_xf_own(t=t, tag=tag, c0=c0, width=width, counts=counts):
                k.load("tab")
                value = k.pq[t, k.z, k.xh, :, c0 : c0 + width] + k.buf[tag + "x", "r"][NZ - 1].astype(F32)
                k.store_query(t, c0, value + ring_sum(tag, counts, lambda b, i: b[i]))

            add(tag + "own", base + 37.5, 0.25, last, last + [(tag, "x", NZ - 1)], [], emit_xf_own)
            own_nodes[c0] = tag + "own"

        add("mask%d" % t, base + 20, 0.3, ["kvmm"], [], [], functools.partial(lambda t: k.mask(t), t))
        keys_in = [m for u in range(t + 1) for m in kg_waits[u]]
        keys_after = [m for u in range(t + 1) for m in ["kv%down" % u] + kg_nodes[u]]
        for place, (c0, width) in enumerate(ZFIRST + XFIRST):
            gtag = "g%d_%d" % (t, c0)

            add(
                gtag + "att",
                base + 40 + place,
                width / 1700.0 + 0.15,
                [own_nodes[c0], "mask%d" % t] + keys_after,
                keys_in,
                [],
                functools.partial(lambda t, first, count: k.attend(t, first, count), t, c0 // HEAD, width // HEAD),
            )
        last_step = []
        for j, (c0, width) in enumerate(ZFIRST + XFIRST):
            gtag = "g%d_%d" % (t, c0)
            gather(
                gtag,
                base + 44 + 0.1 * j,
                4,
                R * width * 2,
                split(j + t),
                lambda d, t=t, c0=c0, width=width: k.att.at[t, d, :, c0 : c0 + width],
                [gtag + "att"],
                [],
                lambda t=t, c0=c0, width=width: k.att.at[t, 0 : NZ - 1, :, c0 : c0 + width],
            )
            last_step.append((gtag, split(j + t)))
        for rounds in OUTS[t]:
            r = rounds[-1]
            shifts, first = [], (2 * rounds[0] - 1 if rounds[0] else 0)
            waits, after = [], []
            for q in rounds:
                shifts += [0] if q == 0 else [4] if q == 4 else [-q, q]
                for gtag, counts in last_step:
                    if q == 0:
                        after.append(gtag + "att")
                    for sign, n in ((1, counts[0]), (-1, counts[1])):
                        if 0 < q <= n:
                            waits.append((gtag, sign, q - 1))
                            after.append((gtag, sign, q - 1))
            for half in range(2):
                if half:
                    after = after + [("wo", "d", p) for p in range(PIECES)]
                    waits = waits + [("wo", leg, p) for leg in ("d", "e") for p in range(PIECES)]

                def emit_out(t=t, r=r, half=half, shifts=shifts, first=first):
                    k.load("wout")
                    count = len(shifts)
                    rows = [k.att[t, k.zi(s)] for s in shifts]
                    lhs = rows[0] if count == 1 else jnp.concatenate(rows, 0)
                    weights = k.wother if half else k.wout
                    for delta in (2, 1, 3, 0):
                        c0 = pl.multiple_of(lax.rem(k.y + delta, NY) * 256, 256)
                        res = jnp.dot(lhs, weights[:, pl.ds(c0, 256)], preferred_element_type=F32)
                        res = res.reshape(count, R, 256)
                        if delta == 0:
                            k.oown[half, t, first : first + count] = res
                        else:
                            k.ys[half, t, delta - 1, first : first + count] = res.astype(BF)
                            k.send(
                                ("y", t, r, half, delta),
                                k.ys.at[half, t, delta - 1, first : first + count],
                                k.yr.at[half, t, delta - 1, first : first + count],
                                k.dev_y(delta),
                                "y",
                                k.ys,
                                ("y", t, r, half),
                                k.yr.at[half, t, :, first : first + count],
                            )

                size = len(shifts) * R * 512
                add(
                    ("out", t, r, half),
                    base + 45 + 4 * r,
                    0.75 + 0.0012 * R * len(shifts),
                    after,
                    waits,
                    [
                        (("y", t, r, half, 2), ["y+", "y-"], size),
                        (("y", t, r, half, 1), ["y+"], size),
                        (("y", t, r, half, 3), ["y-"], size),
                    ],
                    emit_out,
                )

                def put(t, shift, half, value):
                    row = pl.multiple_of(t * ROWS + (k.zi(shift) * 2 + half) * R, R)
                    k.out[pl.ds(row, R), :] = value

                def emit_fin(t=t, r=r, half=half, shifts=shifts, first=first):
                    for i, shift in enumerate(shifts):
                        total = k.oown[half, t, first + i]
                        for delta in range(NY - 1):
                            total = total + k.yr[half, t, delta, first + i].astype(F32)
                        if half:
                            k.xs[t, first + i] = total.astype(BF)
                        else:
                            put(t, shift, k.xh, total.astype(BF))
                    if half:
                        slots = slice(first, first + len(shifts))
                        k.send(("xo", t, r), k.xs.at[t, slots], k.xr.at[t, slots], k.dev_x(), "xo", k.xs)

                add(
                    ("fin", t, r, half),
                    base + 50 + 4 * r,
                    0.15 + 0.03 * len(shifts),
                    [("out", t, r, half)],
                    [("y", t, r, half, delta) for delta in (1, 2, 3)],
                    [(("xo", t, r), ["x"], len(shifts) * R * 512)] if half else [],
                    emit_fin,
                )

            def emit_in(t=t, shifts=shifts, first=first):
                for i, shift in enumerate(shifts):
                    put(t, shift, 1 - k.xh, k.xr[t, first + i])

            add(
                ("in", t, r), base + 54 + 4 * r, 0.1 + 0.02 * len(shifts), [("fin", t, r, 1)], [("xo", t, r)], [], emit_in
            )

    def quarter(owner, p):
        return pl.ds(pl.multiple_of(owner * QUARTER + p * PIECE, PIECE), PIECE)

    size = PIECE * OCOLS * 2
    for p in range(PIECES):

        def emit_cross(p=p):
            k.load("wout")
            k.send(
                ("wo", "c", p),
                k.wout.at[quarter(k.dp, p)],
                k.wother.at[quarter(k.dp, p)],
                k.dev_cross(),
                "woc",
                k.wother.at[0:QUARTER],
            )

        add(("wo", "c", p), 12 + p, 0.12, ["kvmm"], [], [(("wo", "c", p), ["x"], size // 2)], emit_cross)

        def emit_inner(p=p):
            here = k.wother.at[quarter(k.dp_cross, p)]
            k.send(("wo", "i", p), here, here, k.dev_inner(), "woi", k.wother.at[0:QUARTER])
            k.send(("wo", "d", p), here, here, k.dev_core(), "wod", k.wother.at[0:QUARTER])

        add(
            ("wo", "i", p),
            18 + p,
            0.2,
            [("wo", "c", p)],
            [("wo", "c", p)],
            [(("wo", "i", p), ["x"], size // 2), (("wo", "d", p), ["c"], size // 7)],
            emit_inner,
        )

        def emit_core(p=p):
            here = k.wother.at[quarter(k.dp_core, p)]
            k.send(("wo", "e", p), here, here, k.dev_core(), "woe", k.wother.at[0:QUARTER])

        add(
            ("wo", "d", p),
            24 + p,
            0.12,
            [("wo", "i", p)],
            [("wo", "i", p)],
            [(("wo", "e", p), ["c"], size // 7)],
            emit_core,
        )
    return nodes


def buffers():
    shapes = {}
    for t in range(CHUNKS):
        shapes["kv%d" % t] = (6, 2, R, 256)
        shapes["kv%dq" % t] = (2, 2, R, 128)
        shapes["kv%dx" % t] = (2, R, 384)
        for c0, width in ZFIRST:
            shapes["zf%d_%d" % (t, c0)] = (7, 2, R, width)
            shapes["zf%d_%dx" % (t, c0)] = (R, width)
        for c0, width in XFIRST:
            shapes["xf%d_%d" % (t, c0)] = (7, R, width)
            shapes["xf%d_%dx" % (t, c0)] = (8, R, width)
    return shapes


class Kernel:
    pass


def kernel(order_names, messages, *refs):
    shapes = buffers()
    names = ["docs", "h_tok", "h_wq", "h_wk", "h_wv", "h_wout", "h_tab", "out"]
    names += ["tok", "wq", "wkv", "wout", "wother", "tab", "bias", "pq", "pkv", "kvf", "qs", "att"]
    names += ["oown", "ys", "yr", "xs", "xr"]
    k = Kernel()
    for name, ref in zip(names, refs):
        setattr(k, name, ref)
    rest = refs[len(names) :]
    k.buf = {}
    for i, name in enumerate(shapes):
        k.buf[name, "s"], k.buf[name, "r"] = rest[2 * i], rest[2 * i + 1]
    send_sem, recv_sem, load_sem = rest[2 * len(shapes) :]

    loop, k.y = lax.axis_index("loop"), lax.axis_index("column")
    k.xh, k.z = loop // NZ, lax.rem(loop, NZ)
    k.zi = lambda delta: lax.rem(k.z + (delta + NZ), NZ) if delta else k.z
    k.dev_z = lambda sign: {"loop": k.xh * NZ + k.zi(sign)}
    k.dev_x = lambda: {"loop": (1 - k.xh) * NZ + k.z}
    k.dev_y = lambda delta: {"column": lax.rem(k.y + delta, NY)}
    k.dp = lax.axis_index("dp")
    other_chip = lax.rem(k.dp + 2, 4)
    other_core = k.dp + 1 - 2 * lax.rem(k.dp, 2)
    k.dp_cross, k.dp_core = other_chip, k.dp
    k.dev_cross = lambda: {"loop": (1 - k.xh) * NZ + k.z, "dp": other_chip}
    k.dev_inner = lambda: {"dp": other_chip}
    k.dev_core = lambda: {"dp": other_core}
    mesh_id = pl.DeviceIdType.MESH

    barrier = pltpu.get_barrier_semaphore()
    peers = [k.dev_z(1), k.dev_z(-1), k.dev_z(2), k.dev_z(-2), k.dev_x(), k.dev_cross(), k.dev_inner(), k.dev_core()]
    peers += [k.dev_y(delta) for delta in (1, 2, 3)]
    for peer in peers:
        pl.semaphore_signal(barrier, inc=1, device_id=peer, device_id_type=mesh_id)

    loads, started = {}, []

    def start_load(name, src, dst):
        loads[name] = pltpu.make_async_copy(src, dst, load_sem.at[len(started)])
        started.append(name)
        loads[name].start()

    def first_loads():
        start_load("wk", k.h_wk, k.wkv.at[:, 0:HEAD])
        start_load("wv", k.h_wv, k.wkv.at[:, HEAD : 2 * HEAD])
        for t in range(CHUNKS):
            start_load("tok%d" % t, k.h_tok.at[pl.ds(t * ROWS, ROWS)], k.tok.at[pl.ds(t * ROWS, ROWS)])

    def query_loads():
        for c in QUERY_PARTS:
            cols = slice(c * 512, (c + 1) * 512)
            start_load("wq%d" % c, k.h_wq.at[:, cols], k.wq.at[:, cols])

    def last_loads():
        start_load("tab", k.h_tab.at[:, k.z], k.tab)
        start_load("wout", k.h_wout, k.wout)

    first_loads()
    k.query_loads, k.last_loads = query_loads, last_loads

    def load(name):
        if name in ("tab", "wout") and k.last_loads:
            k.last_loads()
            k.last_loads = None
        if name == "wkv":
            load("wk")
            load("wv")
        elif name in loads:
            loads.pop(name).wait()

    k.load = load
    k.ready = lambda: pl.semaphore_wait(barrier, len(peers))
    sent, waited, send_groups, recv_groups, recv_wholes = {}, set(), {}, {}, {}

    def send(name, src, dst, device, group=None, whole=None, recv=None, recv_whole=None):
        group, recv = group or name, recv or name
        i = list(send_groups).index(group) if group in send_groups else len(send_groups)
        j = recv_ids.setdefault(recv, len(recv_ids))
        sent[name] = pltpu.make_async_remote_copy(
            src_ref=src,
            dst_ref=dst,
            send_sem=send_sem.at[i],
            recv_sem=recv_sem.at[j],
            device_id=device,
            device_id_type=mesh_id,
        )
        sent[name].start()
        recv_groups[name] = recv
        if group not in send_groups:
            ref = src if whole is None else whole
            send_groups[group] = pltpu.make_async_remote_copy(ref, ref, send_sem.at[i], recv_sem.at[j], device, mesh_id)
        if recv not in recv_wholes:
            ref = dst if recv_whole is None else recv_whole
            recv_wholes[recv] = pltpu.make_async_remote_copy(ref, ref, send_sem.at[i], recv_sem.at[j], device, mesh_id)

    def receive(name):
        recv = recv_groups[name]
        if recv not in waited:
            waited.add(recv)
            recv_wholes[recv].wait_recv()

    recv_ids = {}
    k.send = send

    def rotate(value, t, half):
        table = k.tab[t, half]
        return value * table[:, 0:HEAD] + pltpu.roll(value, HEAD // 2, 1) * table[:, HEAD : 2 * HEAD]

    k.rotate = rotate

    def store_query(t, c0, value):
        for i in range(value.shape[1] // HEAD):
            k.qs[t, c0 // HEAD + i] = rotate(value[:, i * HEAD : (i + 1) * HEAD], t, k.xh).astype(BF)

    k.store_query = store_query

    def mask(t):
        keys = (t + 1) * ROWS
        row = t * ROWS + (k.z * 2 + k.xh) * R + lax.broadcasted_iota(jnp.int32, (R, keys), 0)
        col = lax.broadcasted_iota(jnp.int32, (R, keys), 1)
        docs = jnp.broadcast_to(k.docs[0:1, 0:keys].astype(F32), (R, keys))
        mine = jnp.sum(jnp.where(row == col, docs, 0.0), axis=1, keepdims=True)
        allowed = (docs == mine) & (col <= row)
        k.bias[t, :, 0:keys] = jnp.where(allowed, 0.0, -1e30)

    k.mask = mask

    def attend(t, first, count):
        keys = (t + 1) * ROWS
        query = k.qs[t, first : first + count].reshape(count * R, HEAD)
        key = k.kvf[0 : t + 1, :, :, :, 0:HEAD].reshape(keys, HEAD)
        value = k.kvf[0 : t + 1, :, :, :, HEAD : 2 * HEAD].reshape(keys, HEAD)
        scores = lax.dot_general(query, key, (((1,), (1,)), ((), ())), preferred_element_type=F32)
        scores = (scores * SCALE).reshape(count, R, keys) + k.bias[t, :, 0:keys][None]
        top = jnp.max(scores, axis=-1, keepdims=True)
        weights = jnp.exp2(scores - top)
        total = jnp.sum(weights, axis=-1, keepdims=True)
        mixed = jnp.dot(weights.reshape(count * R, keys).astype(BF), value, preferred_element_type=F32)
        mixed = (mixed.reshape(count, R, HEAD) / total).astype(BF)
        for i in range(count):
            c0 = (first + i) * HEAD
            k.att[t, k.z, :, c0 : c0 + HEAD] = mixed[i]

    k.attend = attend

    nodes = {node.name: node for node in build(k)}
    for name in order_names:
        node = nodes[name]
        for message in node.waits:
            receive(message)
        node.emit()
    for name in messages:
        receive(name)
    for copy in send_groups.values():
        copy.wait_send()
    for name in list(loads):
        load(name)


def semaphores(messages):
    sends, receives = set(), set()
    for name in messages:
        group, receive = name, name
        if isinstance(name, tuple):
            tag = name[0]
            if tag == "y":
                group, receive = "y", name[:4]
            elif tag == "wo":
                group = tag + name[1]
            elif tag[:2] == "kv" and name[1] == "q":
                group = tag + "q"
            elif tag[:2] == "kg":
                group = name
            elif tag == "xo":
                group = tag
            elif name[1] == "x":
                group = tag + "x"
            else:
                group = tag
        sends.add(group)
        receives.add(receive)
    return len(sends), len(receives)


def shards(tokens, doc_ids, w_query, key_weight, value_weight, w_out):
    nodes = build(None)
    order = [nodes[i] for i in ORDER]
    messages = [send[0] for node in order for send in node.sends]
    sends, receives = semaphores(messages)
    scratch = [
        pltpu.VMEM((SEQ, MODEL), BF),
        pltpu.VMEM((MODEL, QCOLS), BF),
        pltpu.VMEM((MODEL, 2 * HEAD), BF),
        pltpu.VMEM((QCOLS, OCOLS), BF),
        pltpu.VMEM((QCOLS, OCOLS), BF),
        pltpu.VMEM((CHUNKS, 2, R, 2 * HEAD), F32),
        pltpu.VMEM((CHUNKS, R, SEQ), F32),
        pltpu.VMEM((CHUNKS, NZ, 2, R, QCOLS), F32),
        pltpu.VMEM((CHUNKS, NZ, 2, R, 2 * HEAD), F32),
        pltpu.VMEM((CHUNKS, NZ, 2, R, 2 * HEAD), BF),
        pltpu.VMEM((CHUNKS, QCOLS // HEAD, R, HEAD), BF),
        pltpu.VMEM((CHUNKS, NZ, R, QCOLS), BF),
        pltpu.VMEM((2, CHUNKS, NZ, R, 256), F32),
        pltpu.VMEM((2, CHUNKS, NY - 1, NZ, R, 256), BF),
        pltpu.VMEM((2, CHUNKS, NY - 1, NZ, R, 256), BF),
        pltpu.VMEM((CHUNKS, NZ, R, 256), BF),
        pltpu.VMEM((CHUNKS, NZ, R, 256), BF),
    ]
    for shape in buffers().values():
        scratch += [pltpu.VMEM(shape, BF), pltpu.VMEM(shape, BF)]
    scratch += [
        pltpu.SemaphoreType.DMA((sends,)),
        pltpu.SemaphoreType.DMA((receives,)),
        pltpu.SemaphoreType.DMA((16,)),
    ]
    anywhere = pl.BlockSpec(memory_space=pl.ANY)
    vmem = pl.BlockSpec(memory_space=pltpu.VMEM)
    return pl.pallas_call(
        functools.partial(kernel, [node.name for node in order], messages),
        out_shape=jax.ShapeDtypeStruct((SEQ, 256), BF),
        in_specs=[vmem] + [anywhere] * 6,
        out_specs=vmem,
        scratch_shapes=scratch,
        compiler_params=pltpu.CompilerParams(
            collective_id=0, has_side_effects=True, vmem_limit_bytes=56 * 1024 * 1024
        ),
        name="sublayer",
    )(doc_ids.reshape(1, SEQ), tokens, w_query, key_weight, value_weight, w_out, jnp.asarray(rotary_table()))


def solution(mesh):
    placed = (
        P("dp", "loop"),
        P("dp"),
        P("loop", "column"),
        P("loop", "column"),
        P("loop", "column"),
        P("column", "loop"),
    )
    return jax.shard_map(
        shards, mesh=mesh, in_specs=placed, out_specs=P("dp", ("loop", "column")), check_vma=False
    )
```

```python
import functools
import math

import jax
import jax.numpy as jnp
import numpy as np
from jax import lax
from jax.experimental import pallas as pl
from jax.experimental.pallas import tpu as pltpu
from jax.sharding import PartitionSpec as P

HEAD = 128
SEQ = 1024
MODEL = 1024
QCOLS = 2048
OCOLS = 1024
NZ = 8
NY = 4
CHUNKS = 2
ROWS = SEQ // CHUNKS
R = ROWS // (2 * NZ)
XFIRST = (((0, 768), (768, 640)), ((0, 768), (768, 640)))
ZFIRST = (((1408, 640),), ((1408, 640),))
QUERY_PARTS = (1, 2, 3, 0)
XWIDTH = tuple(sum(width for _, width in streams) for streams in XFIRST)
OUTS = (((0,), (1,), (2,), (3,), (4,)), ((0,), (1,), (2,), (3,), (4,)))
BF = jnp.bfloat16
F32 = jnp.float32
SCALE = math.log2(math.e) / math.sqrt(HEAD)
ORDER = (
    0, 1, 12, 8, 4, 65, 17, 71, 20, 2, 40, 68, 44, 13, 9, 70, 69, 67, 66, 18, 3, 54, 5, 21, 41, 134, 55, 10, 72,
    22, 50, 49, 14, 130, 52, 81, 45, 11, 73, 19, 76, 42, 23, 6, 15, 51, 171, 140, 53, 56, 61, 57, 135, 7, 156, 46,
    24, 43, 131, 16, 145, 29, 159, 139, 62, 155, 26, 58, 74, 144, 77, 30, 63, 47, 158, 142, 157, 162, 25, 161, 160,
    27, 59, 166, 33, 37, 132, 141, 75, 143, 146, 31, 78, 136, 38, 60, 28, 150, 48, 34, 147, 167, 32, 133, 79, 64,
    163, 35, 151, 83, 96, 92, 80, 168, 164, 137, 152, 148, 84, 39, 82, 36, 165, 169, 97, 103, 153, 109, 149, 106,
    93, 138, 99, 172, 170, 174, 199, 85, 154, 173, 185, 107, 182, 110, 113, 98, 116, 196, 104, 120, 200, 94, 186,
    175, 192, 108, 89, 111, 105, 183, 100, 179, 210, 114, 201, 206, 187, 121, 189, 197, 86, 90, 176, 203, 112, 95,
    118, 117, 180, 115, 207, 101, 193, 202, 184, 188, 198, 204, 122, 87, 91, 177, 190, 208, 212, 181, 194, 205,
    191, 124, 195, 102, 209, 119, 88, 126, 178, 214, 216, 218, 128, 213, 127, 123, 215, 211, 219, 125, 217, 129,
)


def narrow(value):
    return value.astype(BF)


def widen(value):
    return value.astype(F32)


def narrow_pair(value):
    key = value[..., 0:HEAD]
    high = key.astype(BF)
    low = (key - high.astype(F32)).astype(BF)
    return jnp.concatenate([high, low, value[..., HEAD : 2 * HEAD].astype(BF)], -1)


def widen_pair(value):
    value = value.astype(F32)
    key = value[..., 0:HEAD] + value[..., HEAD : 2 * HEAD]
    return jnp.concatenate([key, value[..., 2 * HEAD : 3 * HEAD]], -1)


class Node:
    def __init__(self, name, rank, cost, after, waits, sends, emit):
        self.name, self.rank, self.cost = name, rank, cost
        self.after, self.waits, self.sends, self.emit = after, waits, sends, emit


def rotary_table():
    frequency = np.exp(-np.log(500000.0) * np.arange(HEAD // 2, dtype=np.float64) * 2.0 / HEAD)
    angles = np.arange(SEQ, dtype=np.float64)[:, None] * frequency
    cosine, sine = np.cos(angles), np.sin(angles)
    table = np.concatenate([cosine, cosine, -sine, sine], 1).astype(np.float32)
    return table.reshape(CHUNKS, NZ, 2, R, 2 * HEAD)


def split(parity):
    return (4, 3) if parity == 0 else (3, 4)


def build(k):
    nodes = []

    def add(name, rank, cost, after, waits, sends, emit):
        nodes.append(Node(name, rank, cost, after, waits, sends, emit))

    def zlink(sign):
        return ["z+"] if sign > 0 else ["z-"]

    def emit_kv(t):
        k.load("wkv")
        k.load("tok%d" % t)
        if t == 0:
            k.query_loads()
        res = jnp.dot(k.tok[pl.ds(t * ROWS, ROWS)], k.wkv[...], preferred_element_type=F32)
        k.pkv[t] = res.reshape(NZ, 2, R, 2 * HEAD)
        if t == 0:
            k.ready()

    for t in range(CHUNKS):
        add("kvmm%d" % t, t, 0.5 if t else 3.4, ["kvmm0"] if t else [], [], [], functools.partial(emit_kv, t))

    def emit_q(t, c0, width):
        for c in range(c0 // 512, (c0 + width - 1) // 512 + 1):
            k.load("wq%d" % c)
        res = jnp.dot(k.tok[pl.ds(t * ROWS, ROWS)], k.wq[:, c0 : c0 + width], preferred_element_type=F32)
        k.pq[t, :, :, :, c0 : c0 + width] = res.reshape(NZ, 2, R, width)
        if k.last_loads:
            k.last_loads()
            k.last_loads = None

    for t in range(CHUNKS):
        for c0, width in ZFIRST[t] + XFIRST[t]:
            add(
                "q%d_%d" % (t, c0),
                1 + t * 40 + (0.1 if c0 < ZFIRST[t][0][0] else 0),
                width / 620.0,
                ["kvmm%d" % t],
                [],
                [],
                functools.partial(emit_q, t, c0, width),
            )

    def ring(tag, rank, stride, cost, size, counts, own, start_after, step_waits, down=narrow, up=widen):
        for sign, n in ((1, counts[0]), (-1, counts[1])):
            base = 0 if sign > 0 else counts[0]
            for s in range(n):
                name = (tag, sign, s)

                def emit(sign=sign, n=n, s=s, base=base, name=name):
                    d = k.zi(sign * (n - s))
                    value = own(sign, s, d)
                    if s > 0:
                        value = value + up(k.buf[tag, "r"][base + s - 1])
                    k.buf[tag, "s"][base + s] = down(value)
                    k.send(name, k.buf[tag, "s"].at[base + s], k.buf[tag, "r"].at[base + s], k.dev_z(sign), tag, k.buf[tag, "s"])

                waits = list(step_waits(sign, s))
                after = list(start_after)
                if s > 0:
                    waits.append((tag, sign, s - 1))
                    after.append((tag, sign, s - 1))
                add(name, rank + stride * s, cost, after, waits, [(name, zlink(sign), size)], emit)
        return [(tag, 1, counts[0] - 1), (tag, -1, counts[1] - 1)]

    def ring_sum(tag, counts, pick, up=widen):
        bufs = k.buf[tag, "r"]
        return up(pick(bufs, counts[0] - 1)) + up(pick(bufs, NZ - 2))

    for t in range(CHUNKS):
        tag, counts, base = "kv%d" % t, split(t), 20 * t
        last = ring(
            tag,
            base + 2,
            4,
            0.2,
            2 * R * 768,
            counts,
            lambda sign, s, d, t=t: k.pkv[t, d],
            ["kvmm%d" % t],
            lambda sign, s: [],
            narrow_pair,
            widen_pair,
        )

        def kv_pair(t, tag, counts):
            return k.pkv[t, k.z] + ring_sum(tag, counts, lambda b, i: b[i], widen_pair)

        def emit_kv_fin(t=t, tag=tag, counts=counts):
            k.buf[tag + "x", "s"][...] = narrow_pair(kv_pair(t, tag, counts))
            k.send(tag + "x", k.buf[tag + "x", "s"], k.buf[tag + "x", "r"], k.dev_x())

        add(tag + "fin", base + 2, 0.2, last, last, [(tag + "x", ["x"], 2 * R * 768)], emit_kv_fin)

        def emit_kv_own(t=t, tag=tag, counts=counts):
            k.load("tab")
            value = kv_pair(t, tag, counts) + widen_pair(k.buf[tag + "x", "r"][...])
            for i in range(2):
                k.kvf[t, k.z, i, :, 0:HEAD] = k.rotate(value[i, :, 0:HEAD], t, i).astype(BF)
            k.kvf[t, k.z, :, :, HEAD : 2 * HEAD] = value[:, :, HEAD : 2 * HEAD].astype(BF)

        add(tag + "own", base + 2, 0.3, [tag + "fin"], [tag + "x"], [], emit_kv_own)

    def gather(tag, rank, stride, size, counts, block, start_after, start_waits, seven):
        for sign, n in ((1, counts[0]), (-1, counts[1])):
            for s in range(n):
                name = (tag, sign, s)

                def emit(sign=sign, s=s, name=name):
                    here = block(k.zi(-sign * s))
                    k.send(name, here, here, k.dev_z(sign), tag, seven())

                after = list(start_after) if s == 0 else [(tag, sign, s - 1)]
                waits = list(start_waits) if s == 0 else [(tag, sign, s - 1)]
                add(name, rank + stride * s, 0.1, after, waits, [(name, zlink(sign), size)], emit)
        return [(tag, 1, counts[0] - 1), (tag, -1, counts[1] - 1)]

    kg_last = [
        gather(
            "kg%d" % t,
            20 * t + 2,
            1,
            2 * R * 512,
            split(1 - t),
            lambda d, t=t: k.kvf.at[t, d],
            ["kv%down" % t],
            [],
            lambda t=t: k.kvf.at[t, 0 : NZ - 1],
        )
        for t in range(CHUNKS)
    ]

    for t in range(CHUNKS):
        base = 40 * t
        own_nodes = {}
        for j, (c0, width) in enumerate(ZFIRST[t]):
            tag, counts = "zf%d_%d" % (t, c0), split(j)
            last = ring(
                tag,
                base + 3 + 0.2 * j,
                8,
                0.2,
                2 * R * width * 2,
                counts,
                lambda sign, s, d, c0=c0, width=width, t=t: k.pq[t, d, :, :, c0 : c0 + width],
                ["q%d_%d" % (t, c0)],
                lambda sign, s: [],
            )

            def emit_fin(t=t, tag=tag, c0=c0, width=width, counts=counts):
                o = 1 - k.xh
                value = k.pq[t, k.z, o, :, c0 : c0 + width] + ring_sum(tag, counts, lambda b, i: b[i, o])
                k.buf[tag + "x", "s"][...] = value.astype(BF)
                k.send(tag + "x", k.buf[tag + "x", "s"], k.buf[tag + "x", "r"], k.dev_x())

            add(tag + "fin", base + 36, 0.2, last, last, [(tag + "x", ["x"], R * width * 2)], emit_fin)

            def emit_own(t=t, tag=tag, c0=c0, width=width, counts=counts):
                k.load("tab")
                value = k.pq[t, k.z, k.xh, :, c0 : c0 + width] + ring_sum(tag, counts, lambda b, i: b[i, k.xh])
                k.store_query(t, c0, value + k.buf[tag + "x", "r"][...].astype(F32))

            add(tag + "own", base + 37, 0.25, [tag + "fin"], [tag + "x"], [], emit_own)
            own_nodes[c0] = tag + "own"

        for j, (c0, width) in enumerate(XFIRST[t]):
            tag, counts = "xf%d_%d" % (t, c0), split(j + t)
            slots = [(1, s) for s in range(counts[0])] + [(-1, s) for s in range(counts[1])] + [(0, 0)]
            queue = sorted(range(NZ), key=lambda i, slots=slots: (slots[i][1] if slots[i][0] else 9, i))

            def where(i, counts=counts, slots=slots):
                sign, s = slots[i]
                n = counts[0] if sign > 0 else counts[1]
                return k.zi(sign * (n - s)) if sign else k.z

            for place, i in enumerate(queue):

                def emit_x(t=t, tag=tag, i=i, c0=c0, width=width, where=where):
                    k.buf[tag + "x", "s"][i] = k.pq[t, where(i), 1 - k.xh, :, c0 : c0 + width].astype(BF)
                    k.send(
                        (tag, "x", i),
                        k.buf[tag + "x", "s"].at[i],
                        k.buf[tag + "x", "r"].at[i],
                        k.dev_x(),
                        tag + "x",
                        k.buf[tag + "x", "s"],
                    )

                add(
                    (tag, "x", i),
                    base + 4 + 0.1 * place - (8 if t else 0),
                    0.1,
                    ["q%d_%d" % (t, c0)],
                    [],
                    [((tag, "x", i), ["x"], R * width * 2)],
                    emit_x,
                )

            def own_xf(sign, s, d, t=t, tag=tag, c0=c0, width=width, counts=counts):
                i = s if sign > 0 else counts[0] + s
                return k.pq[t, d, k.xh, :, c0 : c0 + width] + k.buf[tag + "x", "r"][i].astype(F32)

            last = ring(
                tag,
                base + 9,
                8,
                0.2,
                R * width * 2,
                counts,
                own_xf,
                [(tag, "x", i) for i in range(NZ)],
                lambda sign, s, tag=tag, counts=counts: [(tag, "x", s if sign > 0 else counts[0] + s)],
            )

            def emit_xf_own(t=t, tag=tag, c0=c0, width=width, counts=counts):
                k.load("tab")
                value = k.pq[t, k.z, k.xh, :, c0 : c0 + width] + k.buf[tag + "x", "r"][NZ - 1].astype(F32)
                k.store_query(t, c0, value + ring_sum(tag, counts, lambda b, i: b[i]))

            add(tag + "own", base + 37.5, 0.25, last, last + [(tag, "x", NZ - 1)], [], emit_xf_own)
            own_nodes[c0] = tag + "own"

        add("mask%d" % t, base + 20, 0.3, ["kvmm0"], [], [], functools.partial(lambda t: k.mask(t), t))
        keys_in = [m for u in range(t + 1) for m in kg_last[u]]
        keys_after = [m for u in range(t + 1) for m in ["kv%down" % u] + kg_last[u]]
        for place, (c0, width) in enumerate(ZFIRST[t] + XFIRST[t]):
            gtag = "g%d_%d" % (t, c0)

            def emit_att(t=t, gtag=gtag, c0=c0, width=width):
                k.attend(t, c0 // HEAD, width // HEAD)
                here = k.att.at[t, k.z, k.xh, :, c0 : c0 + width]
                count = NZ if (c0, width) in XFIRST[t] else 1
                k.send(
                    (gtag, "x", 0), here, here, k.dev_x(), gtag + "x", k.att.at[t, 0:count, 0, :, c0 : c0 + width]
                )

            add(
                gtag + "att",
                base + 40 + place,
                width / 1700.0 + 0.15,
                [own_nodes[c0], "mask%d" % t] + keys_after,
                keys_in,
                [((gtag, "x", 0), ["x"], R * width * 2)],
                emit_att,
            )
        last_step = []
        for j, (c0, width) in enumerate(ZFIRST[t]):
            gtag = "g%d_%d" % (t, c0)
            gather(
                gtag,
                base + 44 + 0.1 * j,
                4,
                2 * R * width * 2,
                split(j),
                lambda d, t=t, c0=c0, width=width: k.att.at[t, d, :, :, c0 : c0 + width],
                [gtag + "att"],
                [(gtag, "x", 0)],
                lambda t=t, c0=c0, width=width: k.att.at[t, 0 : NZ - 1, :, :, c0 : c0 + width],
            )
            last_step.append((gtag, False, split(j)))
        for j, (c0, width) in enumerate(XFIRST[t]):
            gtag, counts = "g%d_%d" % (t, c0), split(j + t)
            gather(
                gtag,
                base + 43,
                4,
                R * width * 2,
                counts,
                lambda d, t=t, c0=c0, width=width: k.att.at[t, d, k.xh, :, c0 : c0 + width],
                [gtag + "att"],
                [],
                lambda t=t, c0=c0, width=width: k.att.at[t, 0 : NZ - 1, 0, :, c0 : c0 + width],
            )
            last_step.append((gtag, True, counts))
            for sign, n in ((1, counts[0]), (-1, counts[1])):
                for s in range(n):
                    name = (gtag, "x", sign, s)

                    def emit_pass(t=t, gtag=gtag, sign=sign, s=s, name=name, c0=c0, width=width):
                        here = k.att.at[t, k.zi(-sign * (s + 1)), k.xh, :, c0 : c0 + width]
                        blocks = 1 if s == 3 else 2
                        k.send(
                            name,
                            here,
                            here,
                            k.dev_x(),
                            gtag + "x",
                            k.att.at[t, 0:NZ, 0, :, c0 : c0 + width],
                            ("pass", t, s),
                            k.att.at[t, 0:blocks, 0, :, 0 : XWIDTH[t]],
                        )

                    after = [(gtag, sign, s + 1)] if s + 1 < n else [(gtag, sign, s)]
                    add(
                        name,
                        base + 43.5 + 4 * s,
                        0.1,
                        after,
                        [(gtag, sign, s)],
                        [(name, ["x"], R * width * 2)],
                        emit_pass,
                    )
        for rounds in OUTS[t]:
            r = rounds[-1]
            shifts, first = [], (2 * rounds[0] - 1 if rounds[0] else 0)
            waits, after = [], []
            for q in rounds:
                shifts += [0] if q == 0 else [4] if q == 4 else [-q, q]
                for gtag, passes, counts in last_step:
                    if q == 0:
                        waits.append((gtag, "x", 0))
                        after.append(gtag + "att")
                    for sign, n in ((1, counts[0]), (-1, counts[1])):
                        if 0 < q <= n:
                            waits.append((gtag, sign, q - 1))
                            after.append((gtag, sign, q - 1))
                            if passes:
                                waits.append((gtag, "x", sign, q - 1))
                                after.append((gtag, "x", sign, q - 1))

            def emit_out(t=t, r=r, shifts=shifts, first=first):
                k.load("wout")
                count = len(shifts)
                rows = [k.att[t, k.zi(s)].reshape(2 * R, QCOLS) for s in shifts]
                lhs = rows[0] if count == 1 else jnp.concatenate(rows, 0)
                for delta in (2, 1, 3, 0):
                    c0 = pl.multiple_of(lax.rem(k.y + delta, NY) * 256, 256)
                    res = jnp.dot(lhs, k.wout[:, pl.ds(c0, 256)], preferred_element_type=F32)
                    res = res.reshape(count, 2 * R, 256)
                    if delta == 0:
                        k.oown[t, first : first + count] = res
                    else:
                        k.ys[t, delta - 1, first : first + count] = res.astype(BF)
                        k.send(
                            ("y", t, r, delta),
                            k.ys.at[t, delta - 1, first : first + count],
                            k.yr.at[t, delta - 1, first : first + count],
                            k.dev_y(delta),
                            "y",
                            k.ys,
                            ("y", t, r),
                            k.yr.at[t, :, first : first + count],
                        )

            size = len(shifts) * 2 * R * 512
            add(
                ("out", t, r),
                base + 45 + 4 * r,
                0.55 + 0.15 + 0.0024 * 2 * R * len(shifts),
                after,
                waits,
                [(("y", t, r, 2), ["y+", "y-"], size), (("y", t, r, 1), ["y+"], size), (("y", t, r, 3), ["y-"], size)],
                emit_out,
            )

            def emit_fin(t=t, shifts=shifts, first=first):
                for i, shift in enumerate(shifts):
                    total = k.oown[t, first + i]
                    for delta in range(NY - 1):
                        total = total + k.yr[t, delta, first + i].astype(F32)
                    row = pl.multiple_of(t * ROWS + k.zi(shift) * 2 * R, 2 * R)
                    k.out[pl.ds(row, 2 * R), :] = total.astype(BF)

            add(
                ("fin", t, r),
                base + 50 + 4 * r,
                0.15 + 0.05 * len(shifts),
                [("out", t, r)],
                [("y", t, r, delta) for delta in (1, 2, 3)],
                [],
                emit_fin,
            )
    return nodes


def buffers():
    shapes = {}
    for t in range(CHUNKS):
        shapes["kv%d" % t] = (7, 2, R, 384)
        shapes["kv%dx" % t] = (2, R, 384)
        for c0, width in ZFIRST[t]:
            shapes["zf%d_%d" % (t, c0)] = (7, 2, R, width)
            shapes["zf%d_%dx" % (t, c0)] = (R, width)
        for c0, width in XFIRST[t]:
            shapes["xf%d_%d" % (t, c0)] = (7, R, width)
            shapes["xf%d_%dx" % (t, c0)] = (8, R, width)
    return shapes


class Kernel:
    pass


def kernel(order_names, messages, *refs):
    shapes = buffers()
    names = ["docs", "h_tok", "h_wq", "h_wk", "h_wv", "h_wout", "h_tab", "out"]
    names += ["tok", "wq", "wkv", "wout", "tab", "bias", "pq", "pkv", "kvf", "qs", "att", "oown", "ys", "yr"]
    k = Kernel()
    for name, ref in zip(names, refs):
        setattr(k, name, ref)
    rest = refs[len(names) :]
    k.buf = {}
    for i, name in enumerate(shapes):
        k.buf[name, "s"], k.buf[name, "r"] = rest[2 * i], rest[2 * i + 1]
    send_sem, recv_sem, load_sem = rest[2 * len(shapes) :]

    loop, k.y = lax.axis_index("loop"), lax.axis_index("column")
    k.xh, k.z = loop // NZ, lax.rem(loop, NZ)
    k.zi = lambda delta: lax.rem(k.z + (delta + NZ), NZ) if delta else k.z
    k.dev_z = lambda sign: {"loop": k.xh * NZ + k.zi(sign)}
    k.dev_x = lambda: {"loop": (1 - k.xh) * NZ + k.z}
    k.dev_y = lambda delta: {"column": lax.rem(k.y + delta, NY)}
    mesh_id = pl.DeviceIdType.MESH

    barrier = pltpu.get_barrier_semaphore()
    peers = [k.dev_z(1), k.dev_z(-1), k.dev_x()] + [k.dev_y(delta) for delta in (1, 2, 3)]
    for peer in peers:
        pl.semaphore_signal(barrier, inc=1, device_id=peer, device_id_type=mesh_id)

    loads, started = {}, []

    def start_load(name, src, dst):
        loads[name] = pltpu.make_async_copy(src, dst, load_sem.at[len(started)])
        started.append(name)
        loads[name].start()

    def first_loads():
        start_load("wk", k.h_wk, k.wkv.at[:, 0:HEAD])
        start_load("wv", k.h_wv, k.wkv.at[:, HEAD : 2 * HEAD])
        for t in range(CHUNKS):
            start_load("tok%d" % t, k.h_tok.at[pl.ds(t * ROWS, ROWS)], k.tok.at[pl.ds(t * ROWS, ROWS)])

    def query_loads():
        for c in QUERY_PARTS:
            cols = slice(c * 512, (c + 1) * 512)
            start_load("wq%d" % c, k.h_wq.at[:, cols], k.wq.at[:, cols])

    def last_loads():
        start_load("tab", k.h_tab.at[:, k.z], k.tab)
        start_load("wout", k.h_wout, k.wout)

    first_loads()
    k.query_loads, k.last_loads = query_loads, last_loads

    def load(name):
        if name in ("tab", "wout") and k.last_loads:
            k.last_loads()
            k.last_loads = None
        if name == "wkv":
            load("wk")
            load("wv")
        elif name in loads:
            loads.pop(name).wait()

    k.load = load
    k.ready = lambda: pl.semaphore_wait(barrier, len(peers))
    sent, waited, send_groups, recv_groups, recv_wholes = {}, set(), {}, {}, {}

    def send(name, src, dst, device, group=None, whole=None, recv=None, recv_whole=None):
        group, recv = group or name, recv or name
        i = list(send_groups).index(group) if group in send_groups else len(send_groups)
        j = recv_ids.setdefault(recv, len(recv_ids))
        sent[name] = pltpu.make_async_remote_copy(
            src_ref=src,
            dst_ref=dst,
            send_sem=send_sem.at[i],
            recv_sem=recv_sem.at[j],
            device_id=device,
            device_id_type=mesh_id,
        )
        sent[name].start()
        recv_groups[name] = recv
        if group not in send_groups:
            ref = src if whole is None else whole
            send_groups[group] = pltpu.make_async_remote_copy(ref, ref, send_sem.at[i], recv_sem.at[j], device, mesh_id)
        if recv not in recv_wholes:
            ref = dst if recv_whole is None else recv_whole
            recv_wholes[recv] = pltpu.make_async_remote_copy(ref, ref, send_sem.at[i], recv_sem.at[j], device, mesh_id)

    def receive(name):
        recv = recv_groups[name]
        if recv not in waited:
            waited.add(recv)
            recv_wholes[recv].wait_recv()

    recv_ids = {}
    k.send = send

    def rotate(value, t, half):
        table = k.tab[t, half]
        return value * table[:, 0:HEAD] + pltpu.roll(value, HEAD // 2, 1) * table[:, HEAD : 2 * HEAD]

    k.rotate = rotate

    def store_query(t, c0, value):
        for i in range(value.shape[1] // HEAD):
            k.qs[t, c0 // HEAD + i] = rotate(value[:, i * HEAD : (i + 1) * HEAD], t, k.xh).astype(BF)

    k.store_query = store_query

    def mask(t):
        keys = (t + 1) * ROWS
        row = t * ROWS + (k.z * 2 + k.xh) * R + lax.broadcasted_iota(jnp.int32, (R, keys), 0)
        col = lax.broadcasted_iota(jnp.int32, (R, keys), 1)
        docs = jnp.broadcast_to(k.docs[0:1, 0:keys].astype(F32), (R, keys))
        mine = jnp.sum(jnp.where(row == col, docs, 0.0), axis=1, keepdims=True)
        allowed = (docs == mine) & (col <= row)
        k.bias[t, :, 0:keys] = jnp.where(allowed, 0.0, -1e30)

    k.mask = mask

    def attend(t, first, count):
        keys = (t + 1) * ROWS
        query = k.qs[t, first : first + count].reshape(count * R, HEAD)
        key = k.kvf[0 : t + 1, :, :, :, 0:HEAD].reshape(keys, HEAD)
        value = k.kvf[0 : t + 1, :, :, :, HEAD : 2 * HEAD].reshape(keys, HEAD)
        scores = lax.dot_general(query, key, (((1,), (1,)), ((), ())), preferred_element_type=F32)
        scores = (scores * SCALE).reshape(count, R, keys) + k.bias[t, :, 0:keys][None]
        top = jnp.max(scores, axis=-1, keepdims=True)
        weights = jnp.exp2(scores - top)
        total = jnp.sum(weights, axis=-1, keepdims=True)
        mixed = jnp.dot(weights.reshape(count * R, keys).astype(BF), value, preferred_element_type=F32)
        mixed = (mixed.reshape(count, R, HEAD) / total).astype(BF)
        for i in range(count):
            c0 = (first + i) * HEAD
            k.att[t, k.z, k.xh, :, c0 : c0 + HEAD] = mixed[i]

    k.attend = attend

    nodes = {node.name: node for node in build(k)}
    for name in order_names:
        node = nodes[name]
        for message in node.waits:
            receive(message)
        node.emit()
    for name in messages:
        receive(name)
    for copy in send_groups.values():
        copy.wait_send()
    for name in list(loads):
        load(name)


def semaphores(messages):
    sends, receives = set(), set()
    for name in messages:
        group, receive = name, name
        if isinstance(name, tuple):
            tag = name[0]
            if tag == "y":
                group, receive = "y", name[:3]
            elif name[1] == "x":
                group = tag + "x"
                if len(name) == 4:
                    receive = ("pass", tag[:2], name[3])
            else:
                group = tag
        sends.add(group)
        receives.add(receive)
    return len(sends), len(receives)


def shards(tokens, doc_ids, w_query, key_weight, value_weight, w_out):
    nodes = build(None)
    order = [nodes[i] for i in ORDER]
    messages = [send[0] for node in order for send in node.sends]
    sends, receives = semaphores(messages)
    scratch = [
        pltpu.VMEM((SEQ, MODEL), BF),
        pltpu.VMEM((MODEL, QCOLS), BF),
        pltpu.VMEM((MODEL, 2 * HEAD), BF),
        pltpu.VMEM((QCOLS, OCOLS), BF),
        pltpu.VMEM((CHUNKS, 2, R, 2 * HEAD), F32),
        pltpu.VMEM((CHUNKS, R, SEQ), F32),
        pltpu.VMEM((CHUNKS, NZ, 2, R, QCOLS), F32),
        pltpu.VMEM((CHUNKS, NZ, 2, R, 2 * HEAD), F32),
        pltpu.VMEM((CHUNKS, NZ, 2, R, 2 * HEAD), BF),
        pltpu.VMEM((CHUNKS, QCOLS // HEAD, R, HEAD), BF),
        pltpu.VMEM((CHUNKS, NZ, 2, R, QCOLS), BF),
        pltpu.VMEM((CHUNKS, NZ, 2 * R, 256), F32),
        pltpu.VMEM((CHUNKS, NY - 1, NZ, 2 * R, 256), BF),
        pltpu.VMEM((CHUNKS, NY - 1, NZ, 2 * R, 256), BF),
    ]
    for shape in buffers().values():
        scratch += [pltpu.VMEM(shape, BF), pltpu.VMEM(shape, BF)]
    scratch += [
        pltpu.SemaphoreType.DMA((sends,)),
        pltpu.SemaphoreType.DMA((receives,)),
        pltpu.SemaphoreType.DMA((16,)),
    ]
    anywhere = pl.BlockSpec(memory_space=pl.ANY)
    vmem = pl.BlockSpec(memory_space=pltpu.VMEM)
    return pl.pallas_call(
        functools.partial(kernel, [node.name for node in order], messages),
        out_shape=jax.ShapeDtypeStruct((SEQ, 256), BF),
        in_specs=[vmem] + [anywhere] * 6,
        out_specs=vmem,
        scratch_shapes=scratch,
        compiler_params=pltpu.CompilerParams(
            collective_id=0, has_side_effects=True, vmem_limit_bytes=56 * 1024 * 1024
        ),
        name="sublayer",
    )(doc_ids.reshape(1, SEQ), tokens, w_query, key_weight, value_weight, w_out, jnp.asarray(rotary_table()))


def solution(mesh):
    placed = (
        P("dp", "loop"),
        P("dp"),
        P("loop", "column"),
        P("loop", "column"),
        P("loop", "column"),
        P("column", "loop"),
    )
    return jax.shard_map(
        shards, mesh=mesh, in_specs=placed, out_specs=P("dp", ("loop", "column")), check_vma=False
    )
```

```python
import functools
import math

import jax
import jax.numpy as jnp
import numpy as np
from jax import lax
from jax.experimental import pallas as pl
from jax.experimental.pallas import tpu as pltpu
from jax.sharding import PartitionSpec as P

HEAD = 128
SEQ = 1024
MODEL = 1024
QCOLS = 2048
OCOLS = 1024
NZ = 8
NY = 4
CHUNKS = 2
ROWS = SEQ // CHUNKS
R = ROWS // (2 * NZ)
XFIRST = (((0, 768), (768, 640)), ((0, 640), (640, 640)))
ZFIRST = (((1408, 640),), ((1280, 384), (1664, 384)))
QUERY_PARTS = (2, 3, 0, 1)
XWIDTH = tuple(sum(width for _, width in streams) for streams in XFIRST)
OUTS = (((0,), (1,), (2,), (3,), (4,)), ((0,), (1,), (2,), (3,), (4,)))
BF = jnp.bfloat16
F32 = jnp.float32
SCALE = math.log2(math.e) / math.sqrt(HEAD)
ORDER = (
    0, 9, 13, 1, 18, 5, 21, 135, 131, 3, 51, 6, 55, 10, 14, 56, 54, 140, 143, 19, 53, 22, 2, 132, 45, 4, 41, 52,
    11, 144, 15, 71, 50, 7, 8, 66, 23, 57, 168, 42, 152, 46, 20, 12, 133, 24, 136, 145, 58, 141, 62, 82, 16, 43,
    67, 25, 69, 72, 47, 166, 73, 165, 68, 59, 150, 154, 17, 149, 167, 30, 70, 27, 170, 74, 77, 63, 169, 26, 172,
    171, 34, 151, 38, 176, 142, 155, 28, 153, 31, 156, 44, 78, 137, 134, 146, 173, 75, 35, 160, 60, 39, 32, 29, 79,
    181, 161, 177, 48, 157, 174, 76, 40, 80, 36, 147, 64, 33, 61, 138, 81, 37, 178, 162, 158, 85, 175, 65, 49, 83,
    84, 179, 139, 97, 107, 159, 182, 93, 110, 148, 163, 183, 180, 185, 217, 214, 111, 108, 164, 94, 184, 200, 100,
    203, 98, 117, 121, 114, 86, 104, 90, 218, 215, 112, 186, 221, 224, 204, 95, 101, 109, 99, 201, 105, 210, 193,
    196, 190, 87, 207, 115, 91, 219, 187, 225, 205, 216, 113, 96, 118, 102, 123, 197, 106, 202, 116, 191, 119, 194,
    208, 211, 88, 92, 222, 230, 220, 122, 188, 223, 206, 226, 228, 198, 212, 209, 125, 195, 120, 192, 103, 89, 127,
    189, 227, 213, 232, 199, 234, 129, 236, 233, 229, 126, 124, 235, 128, 231, 130, 237,
)


def narrow(value):
    return value.astype(BF)


def widen(value):
    return value.astype(F32)


def narrow_pair(value):
    key = value[..., 0:HEAD]
    high = key.astype(BF)
    low = (key - high.astype(F32)).astype(BF)
    return jnp.concatenate([high, low, value[..., HEAD : 2 * HEAD].astype(BF)], -1)


def widen_pair(value):
    value = value.astype(F32)
    key = value[..., 0:HEAD] + value[..., HEAD : 2 * HEAD]
    return jnp.concatenate([key, value[..., 2 * HEAD : 3 * HEAD]], -1)


class Node:
    def __init__(self, name, rank, cost, after, waits, sends, emit):
        self.name, self.rank, self.cost = name, rank, cost
        self.after, self.waits, self.sends, self.emit = after, waits, sends, emit


def rotary_table():
    frequency = np.exp(-np.log(500000.0) * np.arange(HEAD // 2, dtype=np.float64) * 2.0 / HEAD)
    angles = np.arange(SEQ, dtype=np.float64)[:, None] * frequency
    cosine, sine = np.cos(angles), np.sin(angles)
    table = np.concatenate([cosine, cosine, -sine, sine], 1).astype(np.float32)
    return table.reshape(CHUNKS, NZ, 2, R, 2 * HEAD)


def split(parity):
    return (4, 3) if parity == 0 else (3, 4)


def build(k):
    nodes = []

    def add(name, rank, cost, after, waits, sends, emit):
        nodes.append(Node(name, rank, cost, after, waits, sends, emit))

    def zlink(sign):
        return ["z+"] if sign > 0 else ["z-"]

    def emit_kv(t):
        k.load("wkv")
        k.load("tok%d" % t)
        if t == 0:
            k.query_loads()
        res = jnp.dot(k.tok[pl.ds(t * ROWS, ROWS)], k.wkv[...], preferred_element_type=F32)
        k.pkv[t] = res.reshape(NZ, 2, R, 2 * HEAD)
        if t == 0:
            k.ready()

    for t in range(CHUNKS):
        add("kvmm%d" % t, t, 0.5 if t else 3.4, ["kvmm0"] if t else [], [], [], functools.partial(emit_kv, t))

    def emit_q(t, c0, width):
        for c in range(c0 // 512, (c0 + width - 1) // 512 + 1):
            k.load("wq%d" % c)
        res = jnp.dot(k.tok[pl.ds(t * ROWS, ROWS)], k.wq[:, c0 : c0 + width], preferred_element_type=F32)
        k.pq[t, :, :, :, c0 : c0 + width] = res.reshape(NZ, 2, R, width)
        if k.last_loads:
            k.last_loads()
            k.last_loads = None

    for t in range(CHUNKS):
        for c0, width in ZFIRST[t] + XFIRST[t]:
            add(
                "q%d_%d" % (t, c0),
                1 + t * 40 + (0.1 if c0 < ZFIRST[t][0][0] else 0),
                width / 620.0,
                ["kvmm%d" % t],
                [],
                [],
                functools.partial(emit_q, t, c0, width),
            )

    def ring(tag, rank, stride, cost, size, counts, own, start_after, step_waits, down=narrow, up=widen):
        for sign, n in ((1, counts[0]), (-1, counts[1])):
            base = 0 if sign > 0 else counts[0]
            for s in range(n):
                name = (tag, sign, s)

                def emit(sign=sign, n=n, s=s, base=base, name=name):
                    d = k.zi(sign * (n - s))
                    value = own(sign, s, d)
                    if s > 0:
                        value = value + up(k.buf[tag, "r"][base + s - 1])
                    k.buf[tag, "s"][base + s] = down(value)
                    k.send(name, k.buf[tag, "s"].at[base + s], k.buf[tag, "r"].at[base + s], k.dev_z(sign), tag, k.buf[tag, "s"])

                waits = list(step_waits(sign, s))
                after = list(start_after)
                if s > 0:
                    waits.append((tag, sign, s - 1))
                    after.append((tag, sign, s - 1))
                add(name, rank + stride * s, cost, after, waits, [(name, zlink(sign), size)], emit)
        return [(tag, 1, counts[0] - 1), (tag, -1, counts[1] - 1)]

    def ring_sum(tag, counts, pick, up=widen):
        bufs = k.buf[tag, "r"]
        return up(pick(bufs, counts[0] - 1)) + up(pick(bufs, NZ - 2))

    for t in range(CHUNKS):
        tag, counts, base = "kv%d" % t, split(t), 20 * t
        last = ring(
            tag,
            base + 2,
            4,
            0.2,
            2 * R * 768,
            counts,
            lambda sign, s, d, t=t: k.pkv[t, d],
            ["kvmm%d" % t],
            lambda sign, s: [],
            narrow_pair,
            widen_pair,
        )

        def kv_pair(t, tag, counts):
            return k.pkv[t, k.z] + ring_sum(tag, counts, lambda b, i: b[i], widen_pair)

        def emit_kv_fin(t=t, tag=tag, counts=counts):
            k.buf[tag + "x", "s"][...] = narrow_pair(kv_pair(t, tag, counts))
            k.send(tag + "x", k.buf[tag + "x", "s"], k.buf[tag + "x", "r"], k.dev_x())

        add(tag + "fin", base + 2, 0.2, last, last, [(tag + "x", ["x"], 2 * R * 768)], emit_kv_fin)

        def emit_kv_own(t=t, tag=tag, counts=counts):
            k.load("tab")
            value = kv_pair(t, tag, counts) + widen_pair(k.buf[tag + "x", "r"][...])
            for i in range(2):
                k.kvf[t, k.z, i, :, 0:HEAD] = k.rotate(value[i, :, 0:HEAD], t, i).astype(BF)
            k.kvf[t, k.z, :, :, HEAD : 2 * HEAD] = value[:, :, HEAD : 2 * HEAD].astype(BF)

        add(tag + "own", base + 2, 0.3, [tag + "fin"], [tag + "x"], [], emit_kv_own)

    def gather(tag, rank, stride, size, counts, block, start_after, start_waits, seven):
        for sign, n in ((1, counts[0]), (-1, counts[1])):
            for s in range(n):
                name = (tag, sign, s)

                def emit(sign=sign, s=s, name=name):
                    here = block(k.zi(-sign * s))
                    k.send(name, here, here, k.dev_z(sign), tag, seven())

                after = list(start_after) if s == 0 else [(tag, sign, s - 1)]
                waits = list(start_waits) if s == 0 else [(tag, sign, s - 1)]
                add(name, rank + stride * s, 0.1, after, waits, [(name, zlink(sign), size)], emit)
        return [(tag, 1, counts[0] - 1), (tag, -1, counts[1] - 1)]

    kg_last = [
        gather(
            "kg%d" % t,
            20 * t + 2,
            1,
            2 * R * 512,
            split(1 - t),
            lambda d, t=t: k.kvf.at[t, d],
            ["kv%down" % t],
            [],
            lambda t=t: k.kvf.at[t, 0 : NZ - 1],
        )
        for t in range(CHUNKS)
    ]

    for t in range(CHUNKS):
        base = 40 * t
        own_nodes = {}
        for j, (c0, width) in enumerate(ZFIRST[t]):
            tag, counts = "zf%d_%d" % (t, c0), split(j)
            last = ring(
                tag,
                base + 3 + 0.2 * j,
                8,
                0.2,
                2 * R * width * 2,
                counts,
                lambda sign, s, d, c0=c0, width=width, t=t: k.pq[t, d, :, :, c0 : c0 + width],
                ["q%d_%d" % (t, c0)],
                lambda sign, s: [],
            )

            def emit_fin(t=t, tag=tag, c0=c0, width=width, counts=counts):
                o = 1 - k.xh
                value = k.pq[t, k.z, o, :, c0 : c0 + width] + ring_sum(tag, counts, lambda b, i: b[i, o])
                k.buf[tag + "x", "s"][...] = value.astype(BF)
                k.send(tag + "x", k.buf[tag + "x", "s"], k.buf[tag + "x", "r"], k.dev_x())

            add(tag + "fin", base + 36, 0.2, last, last, [(tag + "x", ["x"], R * width * 2)], emit_fin)

            def emit_own(t=t, tag=tag, c0=c0, width=width, counts=counts):
                k.load("tab")
                value = k.pq[t, k.z, k.xh, :, c0 : c0 + width] + ring_sum(tag, counts, lambda b, i: b[i, k.xh])
                k.store_query(t, c0, value + k.buf[tag + "x", "r"][...].astype(F32))

            add(tag + "own", base + 37, 0.25, [tag + "fin"], [tag + "x"], [], emit_own)
            own_nodes[c0] = tag + "own"

        for j, (c0, width) in enumerate(XFIRST[t]):
            tag, counts = "xf%d_%d" % (t, c0), split(j + t)
            slots = [(1, s) for s in range(counts[0])] + [(-1, s) for s in range(counts[1])] + [(0, 0)]
            queue = sorted(range(NZ), key=lambda i, slots=slots: (slots[i][1] if slots[i][0] else 9, i))

            def where(i, counts=counts, slots=slots):
                sign, s = slots[i]
                n = counts[0] if sign > 0 else counts[1]
                return k.zi(sign * (n - s)) if sign else k.z

            for place, i in enumerate(queue):

                def emit_x(t=t, tag=tag, i=i, c0=c0, width=width, where=where):
                    k.buf[tag + "x", "s"][i] = k.pq[t, where(i), 1 - k.xh, :, c0 : c0 + width].astype(BF)
                    k.send(
                        (tag, "x", i),
                        k.buf[tag + "x", "s"].at[i],
                        k.buf[tag + "x", "r"].at[i],
                        k.dev_x(),
                        tag + "x",
                        k.buf[tag + "x", "s"],
                    )

                add(
                    (tag, "x", i),
                    base + 4 + 0.1 * place - (8 if t else 0),
                    0.1,
                    ["q%d_%d" % (t, c0)],
                    [],
                    [((tag, "x", i), ["x"], R * width * 2)],
                    emit_x,
                )

            def own_xf(sign, s, d, t=t, tag=tag, c0=c0, width=width, counts=counts):
                i = s if sign > 0 else counts[0] + s
                return k.pq[t, d, k.xh, :, c0 : c0 + width] + k.buf[tag + "x", "r"][i].astype(F32)

            last = ring(
                tag,
                base + 9,
                8,
                0.2,
                R * width * 2,
                counts,
                own_xf,
                [(tag, "x", i) for i in range(NZ)],
                lambda sign, s, tag=tag, counts=counts: [(tag, "x", s if sign > 0 else counts[0] + s)],
            )

            def emit_xf_own(t=t, tag=tag, c0=c0, width=width, counts=counts):
                k.load("tab")
                value = k.pq[t, k.z, k.xh, :, c0 : c0 + width] + k.buf[tag + "x", "r"][NZ - 1].astype(F32)
                k.store_query(t, c0, value + ring_sum(tag, counts, lambda b, i: b[i]))

            add(tag + "own", base + 37.5, 0.25, last, last + [(tag, "x", NZ - 1)], [], emit_xf_own)
            own_nodes[c0] = tag + "own"

        add("mask%d" % t, base + 20, 0.3, ["kvmm0"], [], [], functools.partial(lambda t: k.mask(t), t))
        keys_in = [m for u in range(t + 1) for m in kg_last[u]]
        keys_after = [m for u in range(t + 1) for m in ["kv%down" % u] + kg_last[u]]
        for place, (c0, width) in enumerate(ZFIRST[t] + XFIRST[t]):
            gtag = "g%d_%d" % (t, c0)

            def emit_att(t=t, gtag=gtag, c0=c0, width=width):
                k.attend(t, c0 // HEAD, width // HEAD)
                here = k.att.at[t, k.z, k.xh, :, c0 : c0 + width]
                count = NZ if (c0, width) in XFIRST[t] else 1
                k.send(
                    (gtag, "x", 0), here, here, k.dev_x(), gtag + "x", k.att.at[t, 0:count, 0, :, c0 : c0 + width]
                )

            add(
                gtag + "att",
                base + 40 + place,
                width / 1700.0 + 0.15,
                [own_nodes[c0], "mask%d" % t] + keys_after,
                keys_in,
                [((gtag, "x", 0), ["x"], R * width * 2)],
                emit_att,
            )
        last_step = []
        for j, (c0, width) in enumerate(ZFIRST[t]):
            gtag = "g%d_%d" % (t, c0)
            gather(
                gtag,
                base + 44 + 0.1 * j,
                4,
                2 * R * width * 2,
                split(j),
                lambda d, t=t, c0=c0, width=width: k.att.at[t, d, :, :, c0 : c0 + width],
                [gtag + "att"],
                [(gtag, "x", 0)],
                lambda t=t, c0=c0, width=width: k.att.at[t, 0 : NZ - 1, :, :, c0 : c0 + width],
            )
            last_step.append((gtag, False, split(j)))
        for j, (c0, width) in enumerate(XFIRST[t]):
            gtag, counts = "g%d_%d" % (t, c0), split(j + t)
            gather(
                gtag,
                base + 43,
                4,
                R * width * 2,
                counts,
                lambda d, t=t, c0=c0, width=width: k.att.at[t, d, k.xh, :, c0 : c0 + width],
                [gtag + "att"],
                [],
                lambda t=t, c0=c0, width=width: k.att.at[t, 0 : NZ - 1, 0, :, c0 : c0 + width],
            )
            last_step.append((gtag, True, counts))
            for sign, n in ((1, counts[0]), (-1, counts[1])):
                for s in range(n):
                    name = (gtag, "x", sign, s)

                    def emit_pass(t=t, gtag=gtag, sign=sign, s=s, name=name, c0=c0, width=width):
                        here = k.att.at[t, k.zi(-sign * (s + 1)), k.xh, :, c0 : c0 + width]
                        blocks = 1 if s == 3 else 2
                        k.send(
                            name,
                            here,
                            here,
                            k.dev_x(),
                            gtag + "x",
                            k.att.at[t, 0:NZ, 0, :, c0 : c0 + width],
                            ("pass", t, s),
                            k.att.at[t, 0:blocks, 0, :, 0 : XWIDTH[t]],
                        )

                    after = [(gtag, sign, s + 1)] if s + 1 < n else [(gtag, sign, s)]
                    add(
                        name,
                        base + 43.5 + 4 * s,
                        0.1,
                        after,
                        [(gtag, sign, s)],
                        [(name, ["x"], R * width * 2)],
                        emit_pass,
                    )
        for rounds in OUTS[t]:
            r = rounds[-1]
            shifts, first = [], (2 * rounds[0] - 1 if rounds[0] else 0)
            waits, after = [], []
            for q in rounds:
                shifts += [0] if q == 0 else [4] if q == 4 else [-q, q]
                for gtag, passes, counts in last_step:
                    if q == 0:
                        waits.append((gtag, "x", 0))
                        after.append(gtag + "att")
                    for sign, n in ((1, counts[0]), (-1, counts[1])):
                        if 0 < q <= n:
                            waits.append((gtag, sign, q - 1))
                            after.append((gtag, sign, q - 1))
                            if passes:
                                waits.append((gtag, "x", sign, q - 1))
                                after.append((gtag, "x", sign, q - 1))

            def emit_out(t=t, r=r, shifts=shifts, first=first):
                k.load("wout")
                count = len(shifts)
                rows = [k.att[t, k.zi(s)].reshape(2 * R, QCOLS) for s in shifts]
                lhs = rows[0] if count == 1 else jnp.concatenate(rows, 0)
                for delta in (2, 1, 3, 0):
                    c0 = pl.multiple_of(lax.rem(k.y + delta, NY) * 256, 256)
                    res = jnp.dot(lhs, k.wout[:, pl.ds(c0, 256)], preferred_element_type=F32)
                    res = res.reshape(count, 2 * R, 256)
                    if delta == 0:
                        k.oown[t, first : first + count] = res
                    else:
                        k.ys[t, delta - 1, first : first + count] = res.astype(BF)
                        k.send(
                            ("y", t, r, delta),
                            k.ys.at[t, delta - 1, first : first + count],
                            k.yr.at[t, delta - 1, first : first + count],
                            k.dev_y(delta),
                            "y",
                            k.ys,
                            ("y", t, r),
                            k.yr.at[t, :, first : first + count],
                        )

            size = len(shifts) * 2 * R * 512
            add(
                ("out", t, r),
                base + 45 + 4 * r,
                0.55 + 0.15 + 0.0024 * 2 * R * len(shifts),
                after,
                waits,
                [(("y", t, r, 2), ["y+", "y-"], size), (("y", t, r, 1), ["y+"], size), (("y", t, r, 3), ["y-"], size)],
                emit_out,
            )

            def emit_fin(t=t, shifts=shifts, first=first):
                for i, shift in enumerate(shifts):
                    total = k.oown[t, first + i]
                    for delta in range(NY - 1):
                        total = total + k.yr[t, delta, first + i].astype(F32)
                    row = pl.multiple_of(t * ROWS + k.zi(shift) * 2 * R, 2 * R)
                    k.out[pl.ds(row, 2 * R), :] = total.astype(BF)

            add(
                ("fin", t, r),
                base + 50 + 4 * r,
                0.15 + 0.05 * len(shifts),
                [("out", t, r)],
                [("y", t, r, delta) for delta in (1, 2, 3)],
                [],
                emit_fin,
            )
    return nodes


def buffers():
    shapes = {}
    for t in range(CHUNKS):
        shapes["kv%d" % t] = (7, 2, R, 384)
        shapes["kv%dx" % t] = (2, R, 384)
        for c0, width in ZFIRST[t]:
            shapes["zf%d_%d" % (t, c0)] = (7, 2, R, width)
            shapes["zf%d_%dx" % (t, c0)] = (R, width)
        for c0, width in XFIRST[t]:
            shapes["xf%d_%d" % (t, c0)] = (7, R, width)
            shapes["xf%d_%dx" % (t, c0)] = (8, R, width)
    return shapes


class Kernel:
    pass


def kernel(order_names, messages, *refs):
    shapes = buffers()
    names = ["docs", "h_tok", "h_wq", "h_wk", "h_wv", "h_wout", "h_tab", "out"]
    names += ["tok", "wq", "wkv", "wout", "tab", "bias", "pq", "pkv", "kvf", "qs", "att", "oown", "ys", "yr"]
    k = Kernel()
    for name, ref in zip(names, refs):
        setattr(k, name, ref)
    rest = refs[len(names) :]
    k.buf = {}
    for i, name in enumerate(shapes):
        k.buf[name, "s"], k.buf[name, "r"] = rest[2 * i], rest[2 * i + 1]
    send_sem, recv_sem, load_sem = rest[2 * len(shapes) :]

    loop, k.y = lax.axis_index("loop"), lax.axis_index("column")
    k.xh, k.z = loop // NZ, lax.rem(loop, NZ)
    k.zi = lambda delta: lax.rem(k.z + (delta + NZ), NZ) if delta else k.z
    k.dev_z = lambda sign: {"loop": k.xh * NZ + k.zi(sign)}
    k.dev_x = lambda: {"loop": (1 - k.xh) * NZ + k.z}
    k.dev_y = lambda delta: {"column": lax.rem(k.y + delta, NY)}
    mesh_id = pl.DeviceIdType.MESH

    barrier = pltpu.get_barrier_semaphore()
    peers = [k.dev_z(1), k.dev_z(-1), k.dev_x()] + [k.dev_y(delta) for delta in (1, 2, 3)]
    for peer in peers:
        pl.semaphore_signal(barrier, inc=1, device_id=peer, device_id_type=mesh_id)

    loads, started = {}, []

    def start_load(name, src, dst):
        loads[name] = pltpu.make_async_copy(src, dst, load_sem.at[len(started)])
        started.append(name)
        loads[name].start()

    def first_loads():
        start_load("wk", k.h_wk, k.wkv.at[:, 0:HEAD])
        start_load("wv", k.h_wv, k.wkv.at[:, HEAD : 2 * HEAD])
        for t in range(CHUNKS):
            start_load("tok%d" % t, k.h_tok.at[pl.ds(t * ROWS, ROWS)], k.tok.at[pl.ds(t * ROWS, ROWS)])

    def query_loads():
        for c in QUERY_PARTS:
            cols = slice(c * 512, (c + 1) * 512)
            start_load("wq%d" % c, k.h_wq.at[:, cols], k.wq.at[:, cols])

    def last_loads():
        start_load("tab", k.h_tab.at[:, k.z], k.tab)
        start_load("wout", k.h_wout, k.wout)

    first_loads()
    k.query_loads, k.last_loads = query_loads, last_loads

    def load(name):
        if name in ("tab", "wout") and k.last_loads:
            k.last_loads()
            k.last_loads = None
        if name == "wkv":
            load("wk")
            load("wv")
        elif name in loads:
            loads.pop(name).wait()

    k.load = load
    k.ready = lambda: pl.semaphore_wait(barrier, len(peers))
    sent, waited, send_groups, recv_groups, recv_wholes = {}, set(), {}, {}, {}

    def send(name, src, dst, device, group=None, whole=None, recv=None, recv_whole=None):
        group, recv = group or name, recv or name
        i = list(send_groups).index(group) if group in send_groups else len(send_groups)
        j = recv_ids.setdefault(recv, len(recv_ids))
        sent[name] = pltpu.make_async_remote_copy(
            src_ref=src,
            dst_ref=dst,
            send_sem=send_sem.at[i],
            recv_sem=recv_sem.at[j],
            device_id=device,
            device_id_type=mesh_id,
        )
        sent[name].start()
        recv_groups[name] = recv
        if group not in send_groups:
            ref = src if whole is None else whole
            send_groups[group] = pltpu.make_async_remote_copy(ref, ref, send_sem.at[i], recv_sem.at[j], device, mesh_id)
        if recv not in recv_wholes:
            ref = dst if recv_whole is None else recv_whole
            recv_wholes[recv] = pltpu.make_async_remote_copy(ref, ref, send_sem.at[i], recv_sem.at[j], device, mesh_id)

    def receive(name):
        recv = recv_groups[name]
        if recv not in waited:
            waited.add(recv)
            recv_wholes[recv].wait_recv()

    recv_ids = {}
    k.send = send

    def rotate(value, t, half):
        table = k.tab[t, half]
        return value * table[:, 0:HEAD] + pltpu.roll(value, HEAD // 2, 1) * table[:, HEAD : 2 * HEAD]

    k.rotate = rotate

    def store_query(t, c0, value):
        for i in range(value.shape[1] // HEAD):
            k.qs[t, c0 // HEAD + i] = rotate(value[:, i * HEAD : (i + 1) * HEAD], t, k.xh).astype(BF)

    k.store_query = store_query

    def mask(t):
        keys = (t + 1) * ROWS
        row = t * ROWS + (k.z * 2 + k.xh) * R + lax.broadcasted_iota(jnp.int32, (R, keys), 0)
        col = lax.broadcasted_iota(jnp.int32, (R, keys), 1)
        docs = jnp.broadcast_to(k.docs[0:1, 0:keys].astype(F32), (R, keys))
        mine = jnp.sum(jnp.where(row == col, docs, 0.0), axis=1, keepdims=True)
        allowed = (docs == mine) & (col <= row)
        k.bias[t, :, 0:keys] = jnp.where(allowed, 0.0, -1e30)

    k.mask = mask

    def attend(t, first, count):
        keys = (t + 1) * ROWS
        query = k.qs[t, first : first + count].reshape(count * R, HEAD)
        key = k.kvf[0 : t + 1, :, :, :, 0:HEAD].reshape(keys, HEAD)
        value = k.kvf[0 : t + 1, :, :, :, HEAD : 2 * HEAD].reshape(keys, HEAD)
        scores = lax.dot_general(query, key, (((1,), (1,)), ((), ())), preferred_element_type=F32)
        scores = (scores * SCALE).reshape(count, R, keys) + k.bias[t, :, 0:keys][None]
        top = jnp.max(scores, axis=-1, keepdims=True)
        weights = jnp.exp2(scores - top)
        total = jnp.sum(weights, axis=-1, keepdims=True)
        mixed = jnp.dot(weights.reshape(count * R, keys).astype(BF), value, preferred_element_type=F32)
        mixed = (mixed.reshape(count, R, HEAD) / total).astype(BF)
        for i in range(count):
            c0 = (first + i) * HEAD
            k.att[t, k.z, k.xh, :, c0 : c0 + HEAD] = mixed[i]

    k.attend = attend

    nodes = {node.name: node for node in build(k)}
    for name in order_names:
        node = nodes[name]
        for message in node.waits:
            receive(message)
        node.emit()
    for name in messages:
        receive(name)
    for copy in send_groups.values():
        copy.wait_send()
    for name in list(loads):
        load(name)


def semaphores(messages):
    sends, receives = set(), set()
    for name in messages:
        group, receive = name, name
        if isinstance(name, tuple):
            tag = name[0]
            if tag == "y":
                group, receive = "y", name[:3]
            elif name[1] == "x":
                group = tag + "x"
                if len(name) == 4:
                    receive = ("pass", tag[:2], name[3])
            else:
                group = tag
        sends.add(group)
        receives.add(receive)
    return len(sends), len(receives)


def shards(tokens, doc_ids, w_query, key_weight, value_weight, w_out):
    nodes = build(None)
    order = [nodes[i] for i in ORDER]
    messages = [send[0] for node in order for send in node.sends]
    sends, receives = semaphores(messages)
    scratch = [
        pltpu.VMEM((SEQ, MODEL), BF),
        pltpu.VMEM((MODEL, QCOLS), BF),
        pltpu.VMEM((MODEL, 2 * HEAD), BF),
        pltpu.VMEM((QCOLS, OCOLS), BF),
        pltpu.VMEM((CHUNKS, 2, R, 2 * HEAD), F32),
        pltpu.VMEM((CHUNKS, R, SEQ), F32),
        pltpu.VMEM((CHUNKS, NZ, 2, R, QCOLS), F32),
        pltpu.VMEM((CHUNKS, NZ, 2, R, 2 * HEAD), F32),
        pltpu.VMEM((CHUNKS, NZ, 2, R, 2 * HEAD), BF),
        pltpu.VMEM((CHUNKS, QCOLS // HEAD, R, HEAD), BF),
        pltpu.VMEM((CHUNKS, NZ, 2, R, QCOLS), BF),
        pltpu.VMEM((CHUNKS, NZ, 2 * R, 256), F32),
        pltpu.VMEM((CHUNKS, NY - 1, NZ, 2 * R, 256), BF),
        pltpu.VMEM((CHUNKS, NY - 1, NZ, 2 * R, 256), BF),
    ]
    for shape in buffers().values():
        scratch += [pltpu.VMEM(shape, BF), pltpu.VMEM(shape, BF)]
    scratch += [
        pltpu.SemaphoreType.DMA((sends,)),
        pltpu.SemaphoreType.DMA((receives,)),
        pltpu.SemaphoreType.DMA((16,)),
    ]
    anywhere = pl.BlockSpec(memory_space=pl.ANY)
    vmem = pl.BlockSpec(memory_space=pltpu.VMEM)
    return pl.pallas_call(
        functools.partial(kernel, [node.name for node in order], messages),
        out_shape=pltpu.VMEM((SEQ, 256), BF),
        in_specs=[vmem] + [anywhere] * 6,
        out_specs=vmem,
        scratch_shapes=scratch,
        compiler_params=pltpu.CompilerParams(
            collective_id=0, has_side_effects=True, vmem_limit_bytes=56 * 1024 * 1024
        ),
        name="sublayer",
    )(doc_ids.reshape(1, SEQ), tokens, w_query, key_weight, value_weight, w_out, jnp.asarray(rotary_table()))


def solution(mesh):
    placed = (
        P("dp", "loop"),
        P("dp"),
        P("loop", "column"),
        P("loop", "column"),
        P("loop", "column"),
        P("column", "loop"),
    )
    return jax.shard_map(
        shards, mesh=mesh, in_specs=placed, out_specs=P("dp", ("loop", "column")), check_vma=False
    )
```

```python
import functools
import math

import jax
import jax.numpy as jnp
import numpy as np
from jax import lax
from jax.experimental import pallas as pl
from jax.experimental.pallas import tpu as pltpu
from jax.sharding import PartitionSpec as P

HEAD = 128
SEQ = 1024
MODEL = 1024
QCOLS = 2048
OCOLS = 1024
NZ = 8
NY = 4
CHUNKS = 2
ROWS = SEQ // CHUNKS
R = ROWS // (2 * NZ)
XFIRST = (((0, 768), (768, 640)), ((0, 640), (640, 640)))
ZFIRST = (((1408, 640),), ((1280, 384), (1664, 384)))
QUERY_PARTS = (2, 3, 0, 1)
XWIDTH = tuple(sum(width for _, width in streams) for streams in XFIRST)
OUTS = (((0,), (1,), (2,), (3,), (4,)), ((0,), (1,), (2,), (3,), (4,)))
BF = jnp.bfloat16
F32 = jnp.float32
SCALE = math.log2(math.e) / math.sqrt(HEAD)
ORDER = (
    0, 9, 13, 1, 18, 5, 21, 135, 131, 3, 51, 6, 55, 10, 14, 56, 54, 140, 143, 19, 53, 22, 2, 132, 45, 4, 41, 52,
    11, 144, 15, 71, 50, 7, 8, 66, 23, 57, 168, 42, 152, 46, 20, 12, 133, 24, 136, 145, 58, 141, 62, 82, 16, 43,
    67, 25, 69, 72, 47, 166, 73, 165, 68, 59, 150, 154, 17, 149, 167, 30, 70, 27, 170, 74, 77, 63, 169, 26, 172,
    171, 34, 151, 38, 176, 142, 155, 28, 153, 31, 156, 44, 78, 137, 134, 146, 173, 75, 35, 160, 60, 39, 32, 29, 79,
    181, 161, 177, 48, 157, 174, 76, 40, 80, 36, 147, 64, 33, 61, 138, 81, 37, 178, 162, 158, 85, 175, 65, 49, 83,
    84, 179, 139, 97, 107, 159, 182, 93, 110, 148, 163, 183, 180, 185, 217, 214, 111, 108, 164, 94, 184, 200, 100,
    203, 98, 117, 121, 114, 86, 104, 90, 218, 215, 112, 186, 221, 224, 204, 95, 101, 109, 99, 201, 105, 210, 193,
    196, 190, 87, 207, 115, 91, 219, 187, 225, 205, 216, 113, 96, 118, 102, 123, 197, 106, 202, 116, 191, 119, 194,
    208, 211, 88, 92, 222, 230, 220, 122, 188, 223, 206, 226, 228, 198, 212, 209, 125, 195, 120, 192, 103, 89, 127,
    189, 227, 213, 232, 199, 234, 129, 236, 233, 229, 126, 124, 235, 128, 231, 130, 237,
)


def narrow(value):
    return value.astype(BF)


def widen(value):
    return value.astype(F32)


def narrow_pair(value):
    key = value[..., 0:HEAD]
    high = key.astype(BF)
    low = (key - high.astype(F32)).astype(BF)
    return jnp.concatenate([high, low, value[..., HEAD : 2 * HEAD].astype(BF)], -1)


def widen_pair(value):
    value = value.astype(F32)
    key = value[..., 0:HEAD] + value[..., HEAD : 2 * HEAD]
    return jnp.concatenate([key, value[..., 2 * HEAD : 3 * HEAD]], -1)


class Node:
    def __init__(self, name, rank, cost, after, waits, sends, emit):
        self.name, self.rank, self.cost = name, rank, cost
        self.after, self.waits, self.sends, self.emit = after, waits, sends, emit


def rotary_table():
    frequency = np.exp(-np.log(500000.0) * np.arange(HEAD // 2, dtype=np.float64) * 2.0 / HEAD)
    angles = np.arange(SEQ, dtype=np.float64)[:, None] * frequency
    cosine, sine = np.cos(angles), np.sin(angles)
    table = np.concatenate([cosine, cosine, -sine, sine], 1).astype(np.float32)
    return table.reshape(CHUNKS, NZ, 2, R, 2 * HEAD)


def split(parity):
    return (4, 3) if parity == 0 else (3, 4)


def build(k):
    nodes = []

    def add(name, rank, cost, after, waits, sends, emit):
        nodes.append(Node(name, rank, cost, after, waits, sends, emit))

    def zlink(sign):
        return ["z+"] if sign > 0 else ["z-"]

    def emit_kv(t):
        if t == 0:
            k.query_loads()
        k.load("wkv")
        k.load("tok%d" % t)
        res = jnp.dot(k.tok[pl.ds(t * ROWS, ROWS)], k.wkv[...], preferred_element_type=F32)
        k.pkv[t] = res.reshape(NZ, 2, R, 2 * HEAD)
        if t == 0:
            k.ready()

    for t in range(CHUNKS):
        add("kvmm%d" % t, t, 0.5 if t else 3.4, ["kvmm0"] if t else [], [], [], functools.partial(emit_kv, t))

    def emit_q(t, c0, width):
        for c in range(c0 // 512, (c0 + width - 1) // 512 + 1):
            k.load("wq%d" % c)
        res = jnp.dot(k.tok[pl.ds(t * ROWS, ROWS)], k.wq[:, c0 : c0 + width], preferred_element_type=F32)
        k.pq[t, :, :, :, c0 : c0 + width] = res.reshape(NZ, 2, R, width)

    for t in range(CHUNKS):
        for c0, width in ZFIRST[t] + XFIRST[t]:
            add(
                "q%d_%d" % (t, c0),
                1 + t * 40 + (0.1 if c0 < ZFIRST[t][0][0] else 0),
                width / 620.0,
                ["kvmm%d" % t],
                [],
                [],
                functools.partial(emit_q, t, c0, width),
            )

    def ring(tag, rank, stride, cost, size, counts, own, start_after, step_waits, down=narrow, up=widen):
        for sign, n in ((1, counts[0]), (-1, counts[1])):
            base = 0 if sign > 0 else counts[0]
            for s in range(n):
                name = (tag, sign, s)

                def emit(sign=sign, n=n, s=s, base=base, name=name):
                    d = k.zi(sign * (n - s))
                    value = own(sign, s, d)
                    if s > 0:
                        value = value + up(k.buf[tag, "r"][base + s - 1])
                    k.buf[tag, "s"][base + s] = down(value)
                    k.send(name, k.buf[tag, "s"].at[base + s], k.buf[tag, "r"].at[base + s], k.dev_z(sign), tag, k.buf[tag, "s"])

                waits = list(step_waits(sign, s))
                after = list(start_after)
                if s > 0:
                    waits.append((tag, sign, s - 1))
                    after.append((tag, sign, s - 1))
                add(name, rank + stride * s, cost, after, waits, [(name, zlink(sign), size)], emit)
        return [(tag, 1, counts[0] - 1), (tag, -1, counts[1] - 1)]

    def ring_sum(tag, counts, pick, up=widen):
        bufs = k.buf[tag, "r"]
        return up(pick(bufs, counts[0] - 1)) + up(pick(bufs, NZ - 2))

    for t in range(CHUNKS):
        tag, counts, base = "kv%d" % t, split(t), 20 * t
        last = ring(
            tag,
            base + 2,
            4,
            0.2,
            2 * R * 768,
            counts,
            lambda sign, s, d, t=t: k.pkv[t, d],
            ["kvmm%d" % t],
            lambda sign, s: [],
            narrow_pair,
            widen_pair,
        )

        def kv_pair(t, tag, counts):
            return k.pkv[t, k.z] + ring_sum(tag, counts, lambda b, i: b[i], widen_pair)

        def emit_kv_fin(t=t, tag=tag, counts=counts):
            if k.last_loads:
                k.last_loads()
                k.last_loads = None
            k.buf[tag + "x", "s"][...] = narrow_pair(kv_pair(t, tag, counts))
            k.send(tag + "x", k.buf[tag + "x", "s"], k.buf[tag + "x", "r"], k.dev_x())

        add(tag + "fin", base + 2, 0.2, last, last, [(tag + "x", ["x"], 2 * R * 768)], emit_kv_fin)

        def emit_kv_own(t=t, tag=tag, counts=counts):
            k.load("tab")
            value = kv_pair(t, tag, counts) + widen_pair(k.buf[tag + "x", "r"][...])
            for i in range(2):
                k.kvf[t, k.z, i, :, 0:HEAD] = k.rotate(value[i, :, 0:HEAD], t, i).astype(BF)
            k.kvf[t, k.z, :, :, HEAD : 2 * HEAD] = value[:, :, HEAD : 2 * HEAD].astype(BF)

        add(tag + "own", base + 2, 0.3, [tag + "fin"], [tag + "x"], [], emit_kv_own)

    def gather(tag, rank, stride, size, counts, block, start_after, start_waits, seven):
        for sign, n in ((1, counts[0]), (-1, counts[1])):
            for s in range(n):
                name = (tag, sign, s)

                def emit(sign=sign, s=s, name=name):
                    here = block(k.zi(-sign * s))
                    k.send(name, here, here, k.dev_z(sign), tag, seven())

                after = list(start_after) if s == 0 else [(tag, sign, s - 1)]
                waits = list(start_waits) if s == 0 else [(tag, sign, s - 1)]
                add(name, rank + stride * s, 0.1, after, waits, [(name, zlink(sign), size)], emit)
        return [(tag, 1, counts[0] - 1), (tag, -1, counts[1] - 1)]

    kg_last = [
        gather(
            "kg%d" % t,
            20 * t + 2,
            1,
            2 * R * 512,
            split(1 - t),
            lambda d, t=t: k.kvf.at[t, d],
            ["kv%down" % t],
            [],
            lambda t=t: k.kvf.at[t, 0 : NZ - 1],
        )
        for t in range(CHUNKS)
    ]

    for t in range(CHUNKS):
        base = 40 * t
        own_nodes = {}
        for j, (c0, width) in enumerate(ZFIRST[t]):
            tag, counts = "zf%d_%d" % (t, c0), split(j)
            last = ring(
                tag,
                base + 3 + 0.2 * j,
                8,
                0.2,
                2 * R * width * 2,
                counts,
                lambda sign, s, d, c0=c0, width=width, t=t: k.pq[t, d, :, :, c0 : c0 + width],
                ["q%d_%d" % (t, c0)],
                lambda sign, s: [],
            )

            def emit_fin(t=t, tag=tag, c0=c0, width=width, counts=counts):
                o = 1 - k.xh
                value = k.pq[t, k.z, o, :, c0 : c0 + width] + ring_sum(tag, counts, lambda b, i: b[i, o])
                k.buf[tag + "x", "s"][...] = value.astype(BF)
                k.send(tag + "x", k.buf[tag + "x", "s"], k.buf[tag + "x", "r"], k.dev_x())

            add(tag + "fin", base + 36, 0.2, last, last, [(tag + "x", ["x"], R * width * 2)], emit_fin)

            def emit_own(t=t, tag=tag, c0=c0, width=width, counts=counts):
                k.load("tab")
                value = k.pq[t, k.z, k.xh, :, c0 : c0 + width] + ring_sum(tag, counts, lambda b, i: b[i, k.xh])
                k.store_query(t, c0, value + k.buf[tag + "x", "r"][...].astype(F32))

            add(tag + "own", base + 37, 0.25, [tag + "fin"], [tag + "x"], [], emit_own)
            own_nodes[c0] = tag + "own"

        for j, (c0, width) in enumerate(XFIRST[t]):
            tag, counts = "xf%d_%d" % (t, c0), split(j + t)
            slots = [(1, s) for s in range(counts[0])] + [(-1, s) for s in range(counts[1])] + [(0, 0)]
            queue = sorted(range(NZ), key=lambda i, slots=slots: (slots[i][1] if slots[i][0] else 9, i))

            def where(i, counts=counts, slots=slots):
                sign, s = slots[i]
                n = counts[0] if sign > 0 else counts[1]
                return k.zi(sign * (n - s)) if sign else k.z

            for place, i in enumerate(queue):

                def emit_x(t=t, tag=tag, i=i, c0=c0, width=width, where=where):
                    k.buf[tag + "x", "s"][i] = k.pq[t, where(i), 1 - k.xh, :, c0 : c0 + width].astype(BF)
                    k.send(
                        (tag, "x", i),
                        k.buf[tag + "x", "s"].at[i],
                        k.buf[tag + "x", "r"].at[i],
                        k.dev_x(),
                        tag + "x",
                        k.buf[tag + "x", "s"],
                    )

                add(
                    (tag, "x", i),
                    base + 4 + 0.1 * place - (8 if t else 0),
                    0.1,
                    ["q%d_%d" % (t, c0)],
                    [],
                    [((tag, "x", i), ["x"], R * width * 2)],
                    emit_x,
                )

            def own_xf(sign, s, d, t=t, tag=tag, c0=c0, width=width, counts=counts):
                i = s if sign > 0 else counts[0] + s
                return k.pq[t, d, k.xh, :, c0 : c0 + width] + k.buf[tag + "x", "r"][i].astype(F32)

            last = ring(
                tag,
                base + 9,
                8,
                0.2,
                R * width * 2,
                counts,
                own_xf,
                [(tag, "x", i) for i in range(NZ)],
                lambda sign, s, tag=tag, counts=counts: [(tag, "x", s if sign > 0 else counts[0] + s)],
            )

            def emit_xf_own(t=t, tag=tag, c0=c0, width=width, counts=counts):
                k.load("tab")
                value = k.pq[t, k.z, k.xh, :, c0 : c0 + width] + k.buf[tag + "x", "r"][NZ - 1].astype(F32)
                k.store_query(t, c0, value + ring_sum(tag, counts, lambda b, i: b[i]))

            add(tag + "own", base + 37.5, 0.25, last, last + [(tag, "x", NZ - 1)], [], emit_xf_own)
            own_nodes[c0] = tag + "own"

        add("mask%d" % t, base + 20, 0.3, ["kvmm0"], [], [], functools.partial(lambda t: k.mask(t), t))
        keys_in = [m for u in range(t + 1) for m in kg_last[u]]
        keys_after = [m for u in range(t + 1) for m in ["kv%down" % u] + kg_last[u]]
        for place, (c0, width) in enumerate(ZFIRST[t] + XFIRST[t]):
            gtag = "g%d_%d" % (t, c0)

            def emit_att(t=t, gtag=gtag, c0=c0, width=width):
                k.attend(t, c0 // HEAD, width // HEAD)
                here = k.att.at[t, k.z, k.xh, :, c0 : c0 + width]
                count = NZ if (c0, width) in XFIRST[t] else 1
                k.send(
                    (gtag, "x", 0), here, here, k.dev_x(), gtag + "x", k.att.at[t, 0:count, 0, :, c0 : c0 + width]
                )

            add(
                gtag + "att",
                base + 40 + place,
                width / 1700.0 + 0.15,
                [own_nodes[c0], "mask%d" % t] + keys_after,
                keys_in,
                [((gtag, "x", 0), ["x"], R * width * 2)],
                emit_att,
            )
        last_step = []
        for j, (c0, width) in enumerate(ZFIRST[t]):
            gtag = "g%d_%d" % (t, c0)
            gather(
                gtag,
                base + 44 + 0.1 * j,
                4,
                2 * R * width * 2,
                split(j),
                lambda d, t=t, c0=c0, width=width: k.att.at[t, d, :, :, c0 : c0 + width],
                [gtag + "att"],
                [(gtag, "x", 0)],
                lambda t=t, c0=c0, width=width: k.att.at[t, 0 : NZ - 1, :, :, c0 : c0 + width],
            )
            last_step.append((gtag, False, split(j)))
        for j, (c0, width) in enumerate(XFIRST[t]):
            gtag, counts = "g%d_%d" % (t, c0), split(j + t)
            gather(
                gtag,
                base + 43,
                4,
                R * width * 2,
                counts,
                lambda d, t=t, c0=c0, width=width: k.att.at[t, d, k.xh, :, c0 : c0 + width],
                [gtag + "att"],
                [],
                lambda t=t, c0=c0, width=width: k.att.at[t, 0 : NZ - 1, 0, :, c0 : c0 + width],
            )
            last_step.append((gtag, True, counts))
            for sign, n in ((1, counts[0]), (-1, counts[1])):
                for s in range(n):
                    name = (gtag, "x", sign, s)

                    def emit_pass(t=t, gtag=gtag, sign=sign, s=s, name=name, c0=c0, width=width):
                        here = k.att.at[t, k.zi(-sign * (s + 1)), k.xh, :, c0 : c0 + width]
                        blocks = 1 if s == 3 else 2
                        k.send(
                            name,
                            here,
                            here,
                            k.dev_x(),
                            gtag + "x",
                            k.att.at[t, 0:NZ, 0, :, c0 : c0 + width],
                            ("pass", t, s),
                            k.att.at[t, 0:blocks, 0, :, 0 : XWIDTH[t]],
                        )

                    after = [(gtag, sign, s + 1)] if s + 1 < n else [(gtag, sign, s)]
                    add(
                        name,
                        base + 43.5 + 4 * s,
                        0.1,
                        after,
                        [(gtag, sign, s)],
                        [(name, ["x"], R * width * 2)],
                        emit_pass,
                    )
        for rounds in OUTS[t]:
            r = rounds[-1]
            shifts, first = [], (2 * rounds[0] - 1 if rounds[0] else 0)
            waits, after = [], []
            for q in rounds:
                shifts += [0] if q == 0 else [4] if q == 4 else [-q, q]
                for gtag, passes, counts in last_step:
                    if q == 0:
                        waits.append((gtag, "x", 0))
                        after.append(gtag + "att")
                    for sign, n in ((1, counts[0]), (-1, counts[1])):
                        if 0 < q <= n:
                            waits.append((gtag, sign, q - 1))
                            after.append((gtag, sign, q - 1))
                            if passes:
                                waits.append((gtag, "x", sign, q - 1))
                                after.append((gtag, "x", sign, q - 1))

            def emit_out(t=t, r=r, shifts=shifts, first=first):
                k.load("wout")
                count = len(shifts)
                rows = [k.att[t, k.zi(s)].reshape(2 * R, QCOLS) for s in shifts]
                lhs = rows[0] if count == 1 else jnp.concatenate(rows, 0)
                for delta in (2, 1, 3, 0):
                    c0 = pl.multiple_of(lax.rem(k.y + delta, NY) * 256, 256)
                    res = jnp.dot(lhs, k.wout[:, pl.ds(c0, 256)], preferred_element_type=F32)
                    res = res.reshape(count, 2 * R, 256)
                    if delta == 0:
                        k.oown[t, first : first + count] = res
                    else:
                        k.ys[t, delta - 1, first : first + count] = res.astype(BF)
                        k.send(
                            ("y", t, r, delta),
                            k.ys.at[t, delta - 1, first : first + count],
                            k.yr.at[t, delta - 1, first : first + count],
                            k.dev_y(delta),
                            "y",
                            k.ys,
                            ("y", t, r),
                            k.yr.at[t, :, first : first + count],
                        )

            size = len(shifts) * 2 * R * 512
            add(
                ("out", t, r),
                base + 45 + 4 * r,
                0.55 + 0.15 + 0.0024 * 2 * R * len(shifts),
                after,
                waits,
                [(("y", t, r, 2), ["y+", "y-"], size), (("y", t, r, 1), ["y+"], size), (("y", t, r, 3), ["y-"], size)],
                emit_out,
            )

            def emit_fin(t=t, shifts=shifts, first=first):
                for i, shift in enumerate(shifts):
                    total = k.oown[t, first + i]
                    for delta in range(NY - 1):
                        total = total + k.yr[t, delta, first + i].astype(F32)
                    row = pl.multiple_of(t * ROWS + k.zi(shift) * 2 * R, 2 * R)
                    k.out[pl.ds(row, 2 * R), :] = total.astype(BF)

            add(
                ("fin", t, r),
                base + 50 + 4 * r,
                0.15 + 0.05 * len(shifts),
                [("out", t, r)],
                [("y", t, r, delta) for delta in (1, 2, 3)],
                [],
                emit_fin,
            )
    return nodes


def buffers():
    shapes = {}
    for t in range(CHUNKS):
        shapes["kv%d" % t] = (7, 2, R, 384)
        shapes["kv%dx" % t] = (2, R, 384)
        for c0, width in ZFIRST[t]:
            shapes["zf%d_%d" % (t, c0)] = (7, 2, R, width)
            shapes["zf%d_%dx" % (t, c0)] = (R, width)
        for c0, width in XFIRST[t]:
            shapes["xf%d_%d" % (t, c0)] = (7, R, width)
            shapes["xf%d_%dx" % (t, c0)] = (8, R, width)
    return shapes


class Kernel:
    pass


def kernel(order_names, messages, *refs):
    shapes = buffers()
    names = ["docs", "h_tok", "h_wq", "h_wk", "h_wv", "h_wout", "h_tab", "out"]
    names += ["tok", "wq", "wkv", "wout", "tab", "bias", "pq", "pkv", "kvf", "qs", "att", "oown", "ys", "yr"]
    k = Kernel()
    for name, ref in zip(names, refs):
        setattr(k, name, ref)
    rest = refs[len(names) :]
    k.buf = {}
    for i, name in enumerate(shapes):
        k.buf[name, "s"], k.buf[name, "r"] = rest[2 * i], rest[2 * i + 1]
    send_sem, recv_sem, load_sem = rest[2 * len(shapes) :]

    loop, k.y = lax.axis_index("loop"), lax.axis_index("column")
    k.xh, k.z = loop // NZ, lax.rem(loop, NZ)
    k.zi = lambda delta: lax.rem(k.z + (delta + NZ), NZ) if delta else k.z
    k.dev_z = lambda sign: {"loop": k.xh * NZ + k.zi(sign)}
    k.dev_x = lambda: {"loop": (1 - k.xh) * NZ + k.z}
    k.dev_y = lambda delta: {"column": lax.rem(k.y + delta, NY)}
    mesh_id = pl.DeviceIdType.MESH

    barrier = pltpu.get_barrier_semaphore()
    peers = [k.dev_z(1), k.dev_z(-1), k.dev_x()] + [k.dev_y(delta) for delta in (1, 2, 3)]
    for peer in peers:
        pl.semaphore_signal(barrier, inc=1, device_id=peer, device_id_type=mesh_id)

    loads, started = {}, []

    def start_load(name, src, dst):
        loads[name] = pltpu.make_async_copy(src, dst, load_sem.at[len(started)])
        started.append(name)
        loads[name].start()

    def first_loads():
        start_load("wk", k.h_wk, k.wkv.at[:, 0:HEAD])
        start_load("wv", k.h_wv, k.wkv.at[:, HEAD : 2 * HEAD])
        for t in range(CHUNKS):
            start_load("tok%d" % t, k.h_tok.at[pl.ds(t * ROWS, ROWS)], k.tok.at[pl.ds(t * ROWS, ROWS)])

    def query_loads():
        for c in QUERY_PARTS:
            cols = slice(c * 512, (c + 1) * 512)
            start_load("wq%d" % c, k.h_wq.at[:, cols], k.wq.at[:, cols])

    def last_loads():
        start_load("tab", k.h_tab.at[:, k.z], k.tab)
        start_load("wout", k.h_wout, k.wout)

    first_loads()
    k.query_loads, k.last_loads = query_loads, last_loads

    def load(name):
        if name in ("tab", "wout") and k.last_loads:
            k.last_loads()
            k.last_loads = None
        if name == "wkv":
            load("wk")
            load("wv")
        elif name in loads:
            loads.pop(name).wait()

    k.load = load
    k.ready = lambda: pl.semaphore_wait(barrier, len(peers))
    sent, waited, send_groups, recv_groups, recv_wholes = {}, set(), {}, {}, {}

    def send(name, src, dst, device, group=None, whole=None, recv=None, recv_whole=None):
        group, recv = group or name, recv or name
        i = list(send_groups).index(group) if group in send_groups else len(send_groups)
        j = recv_ids.setdefault(recv, len(recv_ids))
        sent[name] = pltpu.make_async_remote_copy(
            src_ref=src,
            dst_ref=dst,
            send_sem=send_sem.at[i],
            recv_sem=recv_sem.at[j],
            device_id=device,
            device_id_type=mesh_id,
        )
        sent[name].start()
        recv_groups[name] = recv
        if group not in send_groups:
            ref = src if whole is None else whole
            send_groups[group] = pltpu.make_async_remote_copy(ref, ref, send_sem.at[i], recv_sem.at[j], device, mesh_id)
        if recv not in recv_wholes:
            ref = dst if recv_whole is None else recv_whole
            recv_wholes[recv] = pltpu.make_async_remote_copy(ref, ref, send_sem.at[i], recv_sem.at[j], device, mesh_id)

    def receive(name):
        recv = recv_groups[name]
        if recv not in waited:
            waited.add(recv)
            recv_wholes[recv].wait_recv()

    recv_ids = {}
    k.send = send

    def rotate(value, t, half):
        table = k.tab[t, half]
        return value * table[:, 0:HEAD] + pltpu.roll(value, HEAD // 2, 1) * table[:, HEAD : 2 * HEAD]

    k.rotate = rotate

    def store_query(t, c0, value):
        for i in range(value.shape[1] // HEAD):
            k.qs[t, c0 // HEAD + i] = rotate(value[:, i * HEAD : (i + 1) * HEAD], t, k.xh).astype(BF)

    k.store_query = store_query

    def mask(t):
        keys = (t + 1) * ROWS
        row = t * ROWS + (k.z * 2 + k.xh) * R + lax.broadcasted_iota(jnp.int32, (R, keys), 0)
        col = lax.broadcasted_iota(jnp.int32, (R, keys), 1)
        docs = jnp.broadcast_to(k.docs[0:1, 0:keys].astype(F32), (R, keys))
        mine = jnp.sum(jnp.where(row == col, docs, 0.0), axis=1, keepdims=True)
        allowed = (docs == mine) & (col <= row)
        k.bias[t, :, 0:keys] = jnp.where(allowed, 0.0, -1e30)

    k.mask = mask

    def attend(t, first, count):
        keys = (t + 1) * ROWS
        query = k.qs[t, first : first + count].reshape(count * R, HEAD)
        key = k.kvf[0 : t + 1, :, :, :, 0:HEAD].reshape(keys, HEAD)
        value = k.kvf[0 : t + 1, :, :, :, HEAD : 2 * HEAD].reshape(keys, HEAD)
        scores = lax.dot_general(query, key, (((1,), (1,)), ((), ())), preferred_element_type=F32)
        scores = (scores * SCALE).reshape(count, R, keys) + k.bias[t, :, 0:keys][None]
        top = jnp.max(scores, axis=-1, keepdims=True)
        weights = jnp.exp2(scores - top)
        total = jnp.sum(weights, axis=-1, keepdims=True)
        mixed = jnp.dot(weights.reshape(count * R, keys).astype(BF), value, preferred_element_type=F32)
        mixed = (mixed.reshape(count, R, HEAD) / total).astype(BF)
        for i in range(count):
            c0 = (first + i) * HEAD
            k.att[t, k.z, k.xh, :, c0 : c0 + HEAD] = mixed[i]

    k.attend = attend

    nodes = {node.name: node for node in build(k)}
    for name in order_names:
        node = nodes[name]
        for message in node.waits:
            receive(message)
        node.emit()
    for name in messages:
        receive(name)
    for copy in send_groups.values():
        copy.wait_send()
    for name in list(loads):
        load(name)


def semaphores(messages):
    sends, receives = set(), set()
    for name in messages:
        group, receive = name, name
        if isinstance(name, tuple):
            tag = name[0]
            if tag == "y":
                group, receive = "y", name[:3]
            elif name[1] == "x":
                group = tag + "x"
                if len(name) == 4:
                    receive = ("pass", tag[:2], name[3])
            else:
                group = tag
        sends.add(group)
        receives.add(receive)
    return len(sends), len(receives)


def shards(tokens, doc_ids, w_query, key_weight, value_weight, w_out):
    nodes = build(None)
    order = [nodes[i] for i in ORDER]
    messages = [send[0] for node in order for send in node.sends]
    sends, receives = semaphores(messages)
    scratch = [
        pltpu.VMEM((SEQ, MODEL), BF),
        pltpu.VMEM((MODEL, QCOLS), BF),
        pltpu.VMEM((MODEL, 2 * HEAD), BF),
        pltpu.VMEM((QCOLS, OCOLS), BF),
        pltpu.VMEM((CHUNKS, 2, R, 2 * HEAD), F32),
        pltpu.VMEM((CHUNKS, R, SEQ), F32),
        pltpu.VMEM((CHUNKS, NZ, 2, R, QCOLS), F32),
        pltpu.VMEM((CHUNKS, NZ, 2, R, 2 * HEAD), F32),
        pltpu.VMEM((CHUNKS, NZ, 2, R, 2 * HEAD), BF),
        pltpu.VMEM((CHUNKS, QCOLS // HEAD, R, HEAD), BF),
        pltpu.VMEM((CHUNKS, NZ, 2, R, QCOLS), BF),
        pltpu.VMEM((CHUNKS, NZ, 2 * R, 256), F32),
        pltpu.VMEM((CHUNKS, NY - 1, NZ, 2 * R, 256), BF),
        pltpu.VMEM((CHUNKS, NY - 1, NZ, 2 * R, 256), BF),
    ]
    for shape in buffers().values():
        scratch += [pltpu.VMEM(shape, BF), pltpu.VMEM(shape, BF)]
    scratch += [
        pltpu.SemaphoreType.DMA((sends,)),
        pltpu.SemaphoreType.DMA((receives,)),
        pltpu.SemaphoreType.DMA((16,)),
    ]
    anywhere = pl.BlockSpec(memory_space=pl.ANY)
    vmem = pl.BlockSpec(memory_space=pltpu.VMEM)
    return pl.pallas_call(
        functools.partial(kernel, [node.name for node in order], messages),
        out_shape=pltpu.VMEM((SEQ, 256), BF),
        in_specs=[vmem] + [anywhere] * 6,
        out_specs=vmem,
        scratch_shapes=scratch,
        compiler_params=pltpu.CompilerParams(
            collective_id=0, has_side_effects=True, vmem_limit_bytes=56 * 1024 * 1024
        ),
        name="sublayer",
    )(doc_ids.reshape(1, SEQ), tokens, w_query, key_weight, value_weight, w_out, jnp.asarray(rotary_table()))


def solution(mesh):
    placed = (
        P("dp", "loop"),
        P("dp"),
        P("loop", "column"),
        P("loop", "column"),
        P("loop", "column"),
        P("column", "loop"),
    )
    return jax.shard_map(
        shards, mesh=mesh, in_specs=placed, out_specs=P("dp", ("loop", "column")), check_vma=False
    )
```

```python
import functools
import math

import jax
import jax.numpy as jnp
import numpy as np
from jax import lax
from jax.experimental import pallas as pl
from jax.experimental.pallas import tpu as pltpu
from jax.sharding import PartitionSpec as P

HEAD = 128
SEQ = 1024
MODEL = 1024
QCOLS = 2048
OCOLS = 1024
NZ = 8
NY = 4
CHUNKS = 2
ROWS = SEQ // CHUNKS
R = ROWS // (2 * NZ)
XFIRST = (((0, 768), (768, 640)), ((0, 640), (640, 640)))
ZFIRST = (((1408, 640),), ((1280, 384), (1664, 384)))
QUERY_PARTS = (2, 3, 1, 0)
XWIDTH = tuple(sum(width for _, width in streams) for streams in XFIRST)
OUTS = (((0,), (1,), (2,), (3,), (4,)), ((0,), (1,), (2,), (3,), (4,)))
BF = jnp.bfloat16
F32 = jnp.float32
SCALE = math.log2(math.e) / math.sqrt(HEAD)
ORDER = (
    0, 13, 9, 1, 21, 18, 2, 41, 45, 4, 72, 66, 10, 6, 14, 22, 69, 70, 67, 5, 135, 143, 140, 68, 19, 3, 131, 52, 53,
    73, 11, 23, 7, 150, 46, 50, 71, 15, 42, 82, 136, 20, 12, 24, 77, 141, 144, 47, 132, 43, 16, 8, 165, 152, 25,
    156, 142, 51, 55, 78, 54, 166, 56, 168, 74, 154, 17, 57, 30, 58, 145, 26, 34, 27, 133, 169, 38, 137, 149, 62,
    181, 59, 167, 153, 31, 155, 79, 35, 151, 160, 170, 39, 44, 146, 171, 75, 63, 134, 172, 176, 32, 60, 80, 28,
    173, 161, 36, 61, 76, 64, 48, 157, 177, 29, 174, 33, 138, 40, 162, 81, 37, 147, 158, 65, 178, 84, 85, 49, 83,
    139, 175, 179, 163, 110, 107, 148, 97, 93, 183, 159, 182, 180, 185, 217, 94, 100, 214, 164, 184, 203, 98, 111,
    117, 104, 200, 108, 186, 196, 114, 218, 224, 121, 86, 204, 90, 190, 193, 228, 112, 215, 201, 95, 210, 118, 207,
    99, 109, 221, 219, 115, 187, 205, 87, 101, 197, 211, 105, 91, 194, 225, 216, 202, 122, 113, 208, 96, 222, 106,
    191, 123, 188, 220, 206, 119, 102, 116, 198, 88, 230, 92, 226, 212, 125, 223, 195, 192, 209, 232, 227, 213,
    189, 103, 229, 199, 120, 89, 127, 124, 234, 231, 236, 129, 233, 126, 235, 237, 128, 130,
)


def narrow(value):
    return value.astype(BF)


def widen(value):
    return value.astype(F32)


def narrow_pair(value):
    key = value[..., 0:HEAD]
    high = key.astype(BF)
    low = (key - high.astype(F32)).astype(BF)
    return jnp.concatenate([high, low, value[..., HEAD : 2 * HEAD].astype(BF)], -1)


def widen_pair(value):
    value = value.astype(F32)
    key = value[..., 0:HEAD] + value[..., HEAD : 2 * HEAD]
    return jnp.concatenate([key, value[..., 2 * HEAD : 3 * HEAD]], -1)


class Node:
    def __init__(self, name, rank, cost, after, waits, sends, emit):
        self.name, self.rank, self.cost = name, rank, cost
        self.after, self.waits, self.sends, self.emit = after, waits, sends, emit


def rotary_table():
    frequency = np.exp(-np.log(500000.0) * np.arange(HEAD // 2, dtype=np.float64) * 2.0 / HEAD)
    angles = np.arange(SEQ, dtype=np.float64)[:, None] * frequency
    cosine, sine = np.cos(angles), np.sin(angles)
    table = np.concatenate([cosine, cosine, -sine, sine], 1).astype(np.float32)
    return table.reshape(CHUNKS, NZ, 2, R, 2 * HEAD)


def split(parity):
    return (4, 3) if parity == 0 else (3, 4)


def build(k):
    nodes = []

    def add(name, rank, cost, after, waits, sends, emit):
        nodes.append(Node(name, rank, cost, after, waits, sends, emit))

    def zlink(sign):
        return ["z+"] if sign > 0 else ["z-"]

    def emit_kv(t):
        k.load("wkv")
        k.load("tok%d" % t)
        if t == 0:
            k.query_loads()
        res = jnp.dot(k.tok[pl.ds(t * ROWS, ROWS)], k.wkv[...], preferred_element_type=F32)
        k.pkv[t] = res.reshape(NZ, 2, R, 2 * HEAD)
        if t == 0:
            k.ready()

    for t in range(CHUNKS):
        add("kvmm%d" % t, t, 0.5 if t else 3.4, ["kvmm0"] if t else [], [], [], functools.partial(emit_kv, t))

    def emit_q(t, c0, width):
        for c in range(c0 // 512, (c0 + width - 1) // 512 + 1):
            k.load("wq%d" % c)
        res = jnp.dot(k.tok[pl.ds(t * ROWS, ROWS)], k.wq[:, c0 : c0 + width], preferred_element_type=F32)
        k.pq[t, :, :, :, c0 : c0 + width] = res.reshape(NZ, 2, R, width)
        if k.last_loads:
            k.last_loads()
            k.last_loads = None

    for t in range(CHUNKS):
        for c0, width in ZFIRST[t] + XFIRST[t]:
            add(
                "q%d_%d" % (t, c0),
                1 + t * 40 + (0.1 if c0 < ZFIRST[t][0][0] else 0),
                width / 620.0,
                ["kvmm%d" % t],
                [],
                [],
                functools.partial(emit_q, t, c0, width),
            )

    def ring(tag, rank, stride, cost, size, counts, own, start_after, step_waits, down=narrow, up=widen):
        for sign, n in ((1, counts[0]), (-1, counts[1])):
            base = 0 if sign > 0 else counts[0]
            for s in range(n):
                name = (tag, sign, s)

                def emit(sign=sign, n=n, s=s, base=base, name=name):
                    d = k.zi(sign * (n - s))
                    value = own(sign, s, d)
                    if s > 0:
                        value = value + up(k.buf[tag, "r"][base + s - 1])
                    k.buf[tag, "s"][base + s] = down(value)
                    k.send(name, k.buf[tag, "s"].at[base + s], k.buf[tag, "r"].at[base + s], k.dev_z(sign), tag, k.buf[tag, "s"])

                waits = list(step_waits(sign, s))
                after = list(start_after)
                if s > 0:
                    waits.append((tag, sign, s - 1))
                    after.append((tag, sign, s - 1))
                add(name, rank + stride * s, cost, after, waits, [(name, zlink(sign), size)], emit)
        return [(tag, 1, counts[0] - 1), (tag, -1, counts[1] - 1)]

    def ring_sum(tag, counts, pick, up=widen):
        bufs = k.buf[tag, "r"]
        return up(pick(bufs, counts[0] - 1)) + up(pick(bufs, NZ - 2))

    for t in range(CHUNKS):
        tag, counts, base = "kv%d" % t, split(t), 20 * t
        last = ring(
            tag,
            base + 2,
            4,
            0.2,
            2 * R * 768,
            counts,
            lambda sign, s, d, t=t: k.pkv[t, d],
            ["kvmm%d" % t],
            lambda sign, s: [],
            narrow_pair,
            widen_pair,
        )

        def kv_pair(t, tag, counts):
            return k.pkv[t, k.z] + ring_sum(tag, counts, lambda b, i: b[i], widen_pair)

        def emit_kv_fin(t=t, tag=tag, counts=counts):
            k.buf[tag + "x", "s"][...] = narrow_pair(kv_pair(t, tag, counts))
            k.send(tag + "x", k.buf[tag + "x", "s"], k.buf[tag + "x", "r"], k.dev_x())

        add(tag + "fin", base + 2, 0.2, last, last, [(tag + "x", ["x"], 2 * R * 768)], emit_kv_fin)

        def emit_kv_own(t=t, tag=tag, counts=counts):
            k.load("tab")
            value = kv_pair(t, tag, counts) + widen_pair(k.buf[tag + "x", "r"][...])
            for i in range(2):
                k.kvf[t, k.z, i, :, 0:HEAD] = k.rotate(value[i, :, 0:HEAD], t, i).astype(BF)
            k.kvf[t, k.z, :, :, HEAD : 2 * HEAD] = value[:, :, HEAD : 2 * HEAD].astype(BF)

        add(tag + "own", base + 2, 0.3, [tag + "fin"], [tag + "x"], [], emit_kv_own)

    def gather(tag, rank, stride, size, counts, block, start_after, start_waits, seven):
        for sign, n in ((1, counts[0]), (-1, counts[1])):
            for s in range(n):
                name = (tag, sign, s)

                def emit(sign=sign, s=s, name=name):
                    here = block(k.zi(-sign * s))
                    k.send(name, here, here, k.dev_z(sign), tag, seven())

                after = list(start_after) if s == 0 else [(tag, sign, s - 1)]
                waits = list(start_waits) if s == 0 else [(tag, sign, s - 1)]
                add(name, rank + stride * s, 0.1, after, waits, [(name, zlink(sign), size)], emit)
        return [(tag, 1, counts[0] - 1), (tag, -1, counts[1] - 1)]

    kg_last = [
        gather(
            "kg%d" % t,
            20 * t + 2,
            1,
            2 * R * 512,
            split(1 - t),
            lambda d, t=t: k.kvf.at[t, d],
            ["kv%down" % t],
            [],
            lambda t=t: k.kvf.at[t, 0 : NZ - 1],
        )
        for t in range(CHUNKS)
    ]

    for t in range(CHUNKS):
        base = 40 * t
        own_nodes = {}
        for j, (c0, width) in enumerate(ZFIRST[t]):
            tag, counts = "zf%d_%d" % (t, c0), split(j)
            last = ring(
                tag,
                base + 3 + 0.2 * j,
                8,
                0.2,
                2 * R * width * 2,
                counts,
                lambda sign, s, d, c0=c0, width=width, t=t: k.pq[t, d, :, :, c0 : c0 + width],
                ["q%d_%d" % (t, c0)],
                lambda sign, s: [],
            )

            def emit_fin(t=t, tag=tag, c0=c0, width=width, counts=counts):
                o = 1 - k.xh
                value = k.pq[t, k.z, o, :, c0 : c0 + width] + ring_sum(tag, counts, lambda b, i: b[i, o])
                k.buf[tag + "x", "s"][...] = value.astype(BF)
                k.send(tag + "x", k.buf[tag + "x", "s"], k.buf[tag + "x", "r"], k.dev_x())

            add(tag + "fin", base + 36, 0.2, last, last, [(tag + "x", ["x"], R * width * 2)], emit_fin)

            def emit_own(t=t, tag=tag, c0=c0, width=width, counts=counts):
                k.load("tab")
                value = k.pq[t, k.z, k.xh, :, c0 : c0 + width] + ring_sum(tag, counts, lambda b, i: b[i, k.xh])
                k.store_query(t, c0, value + k.buf[tag + "x", "r"][...].astype(F32))

            add(tag + "own", base + 37, 0.25, [tag + "fin"], [tag + "x"], [], emit_own)
            own_nodes[c0] = tag + "own"

        for j, (c0, width) in enumerate(XFIRST[t]):
            tag, counts = "xf%d_%d" % (t, c0), split(j + t)
            slots = [(1, s) for s in range(counts[0])] + [(-1, s) for s in range(counts[1])] + [(0, 0)]
            queue = sorted(range(NZ), key=lambda i, slots=slots: (slots[i][1] if slots[i][0] else 9, i))

            def where(i, counts=counts, slots=slots):
                sign, s = slots[i]
                n = counts[0] if sign > 0 else counts[1]
                return k.zi(sign * (n - s)) if sign else k.z

            for place, i in enumerate(queue):

                def emit_x(t=t, tag=tag, i=i, c0=c0, width=width, where=where):
                    k.buf[tag + "x", "s"][i] = k.pq[t, where(i), 1 - k.xh, :, c0 : c0 + width].astype(BF)
                    k.send(
                        (tag, "x", i),
                        k.buf[tag + "x", "s"].at[i],
                        k.buf[tag + "x", "r"].at[i],
                        k.dev_x(),
                        tag + "x",
                        k.buf[tag + "x", "s"],
                    )

                add(
                    (tag, "x", i),
                    base + 4 + 0.1 * place - (8 if t else 0),
                    0.1,
                    ["q%d_%d" % (t, c0)],
                    [],
                    [((tag, "x", i), ["x"], R * width * 2)],
                    emit_x,
                )

            def own_xf(sign, s, d, t=t, tag=tag, c0=c0, width=width, counts=counts):
                i = s if sign > 0 else counts[0] + s
                return k.pq[t, d, k.xh, :, c0 : c0 + width] + k.buf[tag + "x", "r"][i].astype(F32)

            last = ring(
                tag,
                base + 9,
                8,
                0.2,
                R * width * 2,
                counts,
                own_xf,
                [(tag, "x", i) for i in range(NZ)],
                lambda sign, s, tag=tag, counts=counts: [(tag, "x", s if sign > 0 else counts[0] + s)],
            )

            def emit_xf_own(t=t, tag=tag, c0=c0, width=width, counts=counts):
                k.load("tab")
                value = k.pq[t, k.z, k.xh, :, c0 : c0 + width] + k.buf[tag + "x", "r"][NZ - 1].astype(F32)
                k.store_query(t, c0, value + ring_sum(tag, counts, lambda b, i: b[i]))

            add(tag + "own", base + 37.5, 0.25, last, last + [(tag, "x", NZ - 1)], [], emit_xf_own)
            own_nodes[c0] = tag + "own"

        add("mask%d" % t, base + 20, 0.3, ["kvmm0"], [], [], functools.partial(lambda t: k.mask(t), t))
        keys_in = [m for u in range(t + 1) for m in kg_last[u]]
        keys_after = [m for u in range(t + 1) for m in ["kv%down" % u] + kg_last[u]]
        for place, (c0, width) in enumerate(ZFIRST[t] + XFIRST[t]):
            gtag = "g%d_%d" % (t, c0)

            def emit_att(t=t, gtag=gtag, c0=c0, width=width):
                k.attend(t, c0 // HEAD, width // HEAD)
                here = k.att.at[t, k.z, k.xh, :, c0 : c0 + width]
                count = NZ if (c0, width) in XFIRST[t] else 1
                k.send(
                    (gtag, "x", 0), here, here, k.dev_x(), gtag + "x", k.att.at[t, 0:count, 0, :, c0 : c0 + width]
                )

            add(
                gtag + "att",
                base + 40 + place,
                width / 1700.0 + 0.15,
                [own_nodes[c0], "mask%d" % t] + keys_after,
                keys_in,
                [((gtag, "x", 0), ["x"], R * width * 2)],
                emit_att,
            )
        last_step = []
        for j, (c0, width) in enumerate(ZFIRST[t]):
            gtag = "g%d_%d" % (t, c0)
            gather(
                gtag,
                base + 44 + 0.1 * j,
                4,
                2 * R * width * 2,
                split(j),
                lambda d, t=t, c0=c0, width=width: k.att.at[t, d, :, :, c0 : c0 + width],
                [gtag + "att"],
                [(gtag, "x", 0)],
                lambda t=t, c0=c0, width=width: k.att.at[t, 0 : NZ - 1, :, :, c0 : c0 + width],
            )
            last_step.append((gtag, False, split(j)))
        for j, (c0, width) in enumerate(XFIRST[t]):
            gtag, counts = "g%d_%d" % (t, c0), split(j + t)
            gather(
                gtag,
                base + 43,
                4,
                R * width * 2,
                counts,
                lambda d, t=t, c0=c0, width=width: k.att.at[t, d, k.xh, :, c0 : c0 + width],
                [gtag + "att"],
                [],
                lambda t=t, c0=c0, width=width: k.att.at[t, 0 : NZ - 1, 0, :, c0 : c0 + width],
            )
            last_step.append((gtag, True, counts))
            for sign, n in ((1, counts[0]), (-1, counts[1])):
                for s in range(n):
                    name = (gtag, "x", sign, s)

                    def emit_pass(t=t, gtag=gtag, sign=sign, s=s, name=name, c0=c0, width=width):
                        here = k.att.at[t, k.zi(-sign * (s + 1)), k.xh, :, c0 : c0 + width]
                        blocks = 1 if s == 3 else 2
                        k.send(
                            name,
                            here,
                            here,
                            k.dev_x(),
                            gtag + "x",
                            k.att.at[t, 0:NZ, 0, :, c0 : c0 + width],
                            ("pass", t, s),
                            k.att.at[t, 0:blocks, 0, :, 0 : XWIDTH[t]],
                        )

                    after = [(gtag, sign, s + 1)] if s + 1 < n else [(gtag, sign, s)]
                    add(
                        name,
                        base + 43.5 + 4 * s,
                        0.1,
                        after,
                        [(gtag, sign, s)],
                        [(name, ["x"], R * width * 2)],
                        emit_pass,
                    )
        for rounds in OUTS[t]:
            r = rounds[-1]
            shifts, first = [], (2 * rounds[0] - 1 if rounds[0] else 0)
            waits, after = [], []
            for q in rounds:
                shifts += [0] if q == 0 else [4] if q == 4 else [-q, q]
                for gtag, passes, counts in last_step:
                    if q == 0:
                        waits.append((gtag, "x", 0))
                        after.append(gtag + "att")
                    for sign, n in ((1, counts[0]), (-1, counts[1])):
                        if 0 < q <= n:
                            waits.append((gtag, sign, q - 1))
                            after.append((gtag, sign, q - 1))
                            if passes:
                                waits.append((gtag, "x", sign, q - 1))
                                after.append((gtag, "x", sign, q - 1))

            def emit_out(t=t, r=r, shifts=shifts, first=first):
                k.load("wout")
                count = len(shifts)
                rows = [k.att[t, k.zi(s)].reshape(2 * R, QCOLS) for s in shifts]
                lhs = rows[0] if count == 1 else jnp.concatenate(rows, 0)
                for delta in (2, 1, 3, 0):
                    c0 = pl.multiple_of(lax.rem(k.y + delta, NY) * 256, 256)
                    res = jnp.dot(lhs, k.wout[:, pl.ds(c0, 256)], preferred_element_type=F32)
                    res = res.reshape(count, 2 * R, 256)
                    if delta == 0:
                        k.oown[t, first : first + count] = res
                    else:
                        k.ys[t, delta - 1, first : first + count] = res.astype(BF)
                        k.send(
                            ("y", t, r, delta),
                            k.ys.at[t, delta - 1, first : first + count],
                            k.yr.at[t, delta - 1, first : first + count],
                            k.dev_y(delta),
                            "y",
                            k.ys,
                            ("y", t, r),
                            k.yr.at[t, :, first : first + count],
                        )

            size = len(shifts) * 2 * R * 512
            add(
                ("out", t, r),
                base + 45 + 4 * r,
                0.55 + 0.15 + 0.0024 * 2 * R * len(shifts),
                after,
                waits,
                [(("y", t, r, 2), ["y+", "y-"], size), (("y", t, r, 1), ["y+"], size), (("y", t, r, 3), ["y-"], size)],
                emit_out,
            )

            def emit_fin(t=t, shifts=shifts, first=first):
                for i, shift in enumerate(shifts):
                    total = k.oown[t, first + i]
                    for delta in range(NY - 1):
                        total = total + k.yr[t, delta, first + i].astype(F32)
                    row = pl.multiple_of(t * ROWS + k.zi(shift) * 2 * R, 2 * R)
                    k.out[pl.ds(row, 2 * R), :] = total.astype(BF)

            add(
                ("fin", t, r),
                base + 50 + 4 * r,
                0.15 + 0.05 * len(shifts),
                [("out", t, r)],
                [("y", t, r, delta) for delta in (1, 2, 3)],
                [],
                emit_fin,
            )
    return nodes


def buffers():
    shapes = {}
    for t in range(CHUNKS):
        shapes["kv%d" % t] = (7, 2, R, 384)
        shapes["kv%dx" % t] = (2, R, 384)
        for c0, width in ZFIRST[t]:
            shapes["zf%d_%d" % (t, c0)] = (7, 2, R, width)
            shapes["zf%d_%dx" % (t, c0)] = (R, width)
        for c0, width in XFIRST[t]:
            shapes["xf%d_%d" % (t, c0)] = (7, R, width)
            shapes["xf%d_%dx" % (t, c0)] = (8, R, width)
    return shapes


class Kernel:
    pass


def kernel(order_names, messages, *refs):
    shapes = buffers()
    names = ["docs", "h_tok", "h_wq", "h_wk", "h_wv", "h_wout", "h_tab", "out"]
    names += ["tok", "wq", "wkv", "wout", "tab", "bias", "pq", "pkv", "kvf", "qs", "att", "oown", "ys", "yr"]
    k = Kernel()
    for name, ref in zip(names, refs):
        setattr(k, name, ref)
    rest = refs[len(names) :]
    k.buf = {}
    for i, name in enumerate(shapes):
        k.buf[name, "s"], k.buf[name, "r"] = rest[2 * i], rest[2 * i + 1]
    send_sem, recv_sem, load_sem = rest[2 * len(shapes) :]

    loop, k.y = lax.axis_index("loop"), lax.axis_index("column")
    k.xh, k.z = loop // NZ, lax.rem(loop, NZ)
    k.zi = lambda delta: lax.rem(k.z + (delta + NZ), NZ) if delta else k.z
    k.dev_z = lambda sign: {"loop": k.xh * NZ + k.zi(sign)}
    k.dev_x = lambda: {"loop": (1 - k.xh) * NZ + k.z}
    k.dev_y = lambda delta: {"column": lax.rem(k.y + delta, NY)}
    mesh_id = pl.DeviceIdType.MESH

    barrier = pltpu.get_barrier_semaphore()
    peers = [k.dev_z(1), k.dev_z(-1), k.dev_x()] + [k.dev_y(delta) for delta in (1, 2, 3)]
    for peer in peers:
        pl.semaphore_signal(barrier, inc=1, device_id=peer, device_id_type=mesh_id)

    loads, started = {}, []

    def start_load(name, src, dst):
        loads[name] = pltpu.make_async_copy(src, dst, load_sem.at[len(started)])
        started.append(name)
        loads[name].start()

    def first_loads():
        start_load("wk", k.h_wk, k.wkv.at[:, 0:HEAD])
        start_load("wv", k.h_wv, k.wkv.at[:, HEAD : 2 * HEAD])
        for t in range(CHUNKS):
            start_load("tok%d" % t, k.h_tok.at[pl.ds(t * ROWS, ROWS)], k.tok.at[pl.ds(t * ROWS, ROWS)])

    def query_loads():
        for c in QUERY_PARTS:
            cols = slice(c * 512, (c + 1) * 512)
            start_load("wq%d" % c, k.h_wq.at[:, cols], k.wq.at[:, cols])

    def last_loads():
        start_load("tab", k.h_tab.at[:, k.z], k.tab)
        start_load("wout", k.h_wout, k.wout)

    first_loads()
    k.query_loads, k.last_loads = query_loads, last_loads

    def load(name):
        if name in ("tab", "wout") and k.last_loads:
            k.last_loads()
            k.last_loads = None
        if name == "wkv":
            load("wk")
            load("wv")
        elif name in loads:
            loads.pop(name).wait()

    k.load = load
    k.ready = lambda: pl.semaphore_wait(barrier, len(peers))
    sent, waited, send_groups, recv_groups, recv_wholes = {}, set(), {}, {}, {}

    def send(name, src, dst, device, group=None, whole=None, recv=None, recv_whole=None):
        group, recv = group or name, recv or name
        i = list(send_groups).index(group) if group in send_groups else len(send_groups)
        j = recv_ids.setdefault(recv, len(recv_ids))
        sent[name] = pltpu.make_async_remote_copy(
            src_ref=src,
            dst_ref=dst,
            send_sem=send_sem.at[i],
            recv_sem=recv_sem.at[j],
            device_id=device,
            device_id_type=mesh_id,
        )
        sent[name].start()
        recv_groups[name] = recv
        if group not in send_groups:
            ref = src if whole is None else whole
            send_groups[group] = pltpu.make_async_remote_copy(ref, ref, send_sem.at[i], recv_sem.at[j], device, mesh_id)
        if recv not in recv_wholes:
            ref = dst if recv_whole is None else recv_whole
            recv_wholes[recv] = pltpu.make_async_remote_copy(ref, ref, send_sem.at[i], recv_sem.at[j], device, mesh_id)

    def receive(name):
        recv = recv_groups[name]
        if recv not in waited:
            waited.add(recv)
            recv_wholes[recv].wait_recv()

    recv_ids = {}
    k.send = send

    def rotate(value, t, half):
        table = k.tab[t, half]
        return value * table[:, 0:HEAD] + pltpu.roll(value, HEAD // 2, 1) * table[:, HEAD : 2 * HEAD]

    k.rotate = rotate

    def store_query(t, c0, value):
        for i in range(value.shape[1] // HEAD):
            k.qs[t, c0 // HEAD + i] = rotate(value[:, i * HEAD : (i + 1) * HEAD], t, k.xh).astype(BF)

    k.store_query = store_query

    def mask(t):
        keys = (t + 1) * ROWS
        row = t * ROWS + (k.z * 2 + k.xh) * R + lax.broadcasted_iota(jnp.int32, (R, keys), 0)
        col = lax.broadcasted_iota(jnp.int32, (R, keys), 1)
        docs = jnp.broadcast_to(k.docs[0:1, 0:keys].astype(F32), (R, keys))
        mine = jnp.sum(jnp.where(row == col, docs, 0.0), axis=1, keepdims=True)
        allowed = (docs == mine) & (col <= row)
        k.bias[t, :, 0:keys] = jnp.where(allowed, 0.0, -1e30)

    k.mask = mask

    def attend(t, first, count):
        keys = (t + 1) * ROWS
        query = k.qs[t, first : first + count].reshape(count * R, HEAD)
        key = k.kvf[0 : t + 1, :, :, :, 0:HEAD].reshape(keys, HEAD)
        value = k.kvf[0 : t + 1, :, :, :, HEAD : 2 * HEAD].reshape(keys, HEAD)
        scores = lax.dot_general(query, key, (((1,), (1,)), ((), ())), preferred_element_type=F32)
        scores = (scores * SCALE).reshape(count, R, keys) + k.bias[t, :, 0:keys][None]
        top = jnp.max(scores, axis=-1, keepdims=True)
        weights = jnp.exp2(scores - top)
        total = jnp.sum(weights, axis=-1, keepdims=True)
        mixed = jnp.dot(weights.reshape(count * R, keys).astype(BF), value, preferred_element_type=F32)
        mixed = (mixed.reshape(count, R, HEAD) / total).astype(BF)
        for i in range(count):
            c0 = (first + i) * HEAD
            k.att[t, k.z, k.xh, :, c0 : c0 + HEAD] = mixed[i]

    k.attend = attend

    nodes = {node.name: node for node in build(k)}
    for name in order_names:
        node = nodes[name]
        for message in node.waits:
            receive(message)
        node.emit()
    for name in messages:
        receive(name)
    for copy in send_groups.values():
        copy.wait_send()
    for name in list(loads):
        load(name)


def semaphores(messages):
    sends, receives = set(), set()
    for name in messages:
        group, receive = name, name
        if isinstance(name, tuple):
            tag = name[0]
            if tag == "y":
                group, receive = "y", name[:3]
            elif name[1] == "x":
                group = tag + "x"
                if len(name) == 4:
                    receive = ("pass", tag[:2], name[3])
            else:
                group = tag
        sends.add(group)
        receives.add(receive)
    return len(sends), len(receives)


def shards(tokens, doc_ids, w_query, key_weight, value_weight, w_out):
    nodes = build(None)
    order = [nodes[i] for i in ORDER]
    messages = [send[0] for node in order for send in node.sends]
    sends, receives = semaphores(messages)
    scratch = [
        pltpu.VMEM((SEQ, MODEL), BF),
        pltpu.VMEM((MODEL, QCOLS), BF),
        pltpu.VMEM((MODEL, 2 * HEAD), BF),
        pltpu.VMEM((QCOLS, OCOLS), BF),
        pltpu.VMEM((CHUNKS, 2, R, 2 * HEAD), F32),
        pltpu.VMEM((CHUNKS, R, SEQ), F32),
        pltpu.VMEM((CHUNKS, NZ, 2, R, QCOLS), F32),
        pltpu.VMEM((CHUNKS, NZ, 2, R, 2 * HEAD), F32),
        pltpu.VMEM((CHUNKS, NZ, 2, R, 2 * HEAD), BF),
        pltpu.VMEM((CHUNKS, QCOLS // HEAD, R, HEAD), BF),
        pltpu.VMEM((CHUNKS, NZ, 2, R, QCOLS), BF),
        pltpu.VMEM((CHUNKS, NZ, 2 * R, 256), F32),
        pltpu.VMEM((CHUNKS, NY - 1, NZ, 2 * R, 256), BF),
        pltpu.VMEM((CHUNKS, NY - 1, NZ, 2 * R, 256), BF),
    ]
    for shape in buffers().values():
        scratch += [pltpu.VMEM(shape, BF), pltpu.VMEM(shape, BF)]
    scratch += [
        pltpu.SemaphoreType.DMA((sends,)),
        pltpu.SemaphoreType.DMA((receives,)),
        pltpu.SemaphoreType.DMA((16,)),
    ]
    anywhere = pl.BlockSpec(memory_space=pl.ANY)
    vmem = pl.BlockSpec(memory_space=pltpu.VMEM)
    return pl.pallas_call(
        functools.partial(kernel, [node.name for node in order], messages),
        out_shape=pltpu.VMEM((SEQ, 256), BF),
        in_specs=[vmem] + [anywhere] * 6,
        out_specs=vmem,
        scratch_shapes=scratch,
        compiler_params=pltpu.CompilerParams(
            collective_id=0, has_side_effects=True, vmem_limit_bytes=56 * 1024 * 1024
        ),
        name="sublayer",
    )(doc_ids.reshape(1, SEQ), tokens, w_query, key_weight, value_weight, w_out, jnp.asarray(rotary_table()))


def solution(mesh):
    placed = (
        P("dp", "loop"),
        P("dp"),
        P("loop", "column"),
        P("loop", "column"),
        P("loop", "column"),
        P("column", "loop"),
    )
    return jax.shard_map(
        shards, mesh=mesh, in_specs=placed, out_specs=P("dp", ("loop", "column")), check_vma=False
    )
```
